32 devices in a mesh: freq: 2 (over y), row: 4 (over z), col: 4 (over x, core).
Axes of the slice: x: 2, y: 2, z: 4, core: 2. Of those that a mesh axis runs over, the one named last changes fastest.
Arguments:
- traces: bfloat16 [4, 6144, 6144], P('freq', 'row', 'col'), parts along dimension 0, may hold values from -6 to 6
- recv_live: int32 [12288], P('freq'), parts along dimension 0, may hold values 0 or 1
- missing: int32 [8, 96], P('freq'), parts along dimension 0, may hold values from 0 to 1535, as said below
- wavelet: float32 [4], P('freq'), parts along dimension 0, may hold values from 0.5 to 1.5
Outputs:
- primaries: float32 [4, 6144, 512], P('freq', 'row', 'col'), parts along dimension 0
The draws below stay inside these ranges and needn't reach their ends.
There are 2 independent parts, one for each index of `freq`. The reference program is written for one: setup_inputs(seed, part) draws one part's arguments, and reference() takes and returns one part's arrays. A program takes and returns all parts, laid end to end along the dimension named above; each array names one. Nothing has to cross between parts.
Inputs may be any that keep to these rules, and one draw needn't show every extreme that they name: `missing`: each row lists 96 distinct positions within one block of 1536 shots, the shots of that block that were not recorded; the block's first and last shots are always among them.
All inputs are finite; a program needn't handle non-finite values.
Results may differ from the reference program's by a relative error of at most 0.0003.
Values may be sent and summed in bfloat16 or wider, within the bound.
No kernel may reach another device: no remote copies, remote signals or barrier semaphores. Data moves between devices by JAX's collectives and lax.ppermute only.
A program may use at most 128 MiB of HBM per device.

```python
import math
import jax
import jax.numpy as jnp
from jax import lax

ORDER = 6144
WIN = 128
MISS = 96
TILE = 1536
BLOCKS = 4
N_ROW = 4


def draw_missing(key, part):
    sub_keys = jax.random.split(key, BLOCKS)

    def one_block(sub_key):
        shuffled = jax.random.permutation(sub_key, TILE - 2)[:MISS - 2] + 1
        ends = jnp.array([0, TILE - 1], jnp.int32)
        return jnp.concatenate([ends, shuffled.astype(jnp.int32)])
    return jax.vmap(one_block)(sub_keys)


def set_ends(drawn, key, least, top_value):
    shape = drawn.shape
    index_at = [jax.random.randint(jax.random.fold_in(key, axis), (), 0, shape[axis]) for axis in range(len(shape))]
    drawn = drawn.at[tuple(index_at)].set(least)
    longest = shape.index(max(shape))
    index_at[longest] = (index_at[longest] + 1) % shape[longest]
    return drawn.at[tuple(index_at)].set(top_value)


def block_scale(key, shape, pieces, smallest, high):
    def one(position, blocks):
        heights = jax.random.uniform(jax.random.fold_in(jax.random.fold_in(key, 6), position), (blocks,), jnp.float32, smallest / len(pieces), high / len(pieces))
        return jnp.repeat(jnp.exp(heights), shape[position] // blocks).reshape((-1,) + (1,) * (len(shape) - position - 1))

    loudness = one(*pieces[0])
    for cut in pieces[1:]:
        loudness = loudness * one(*cut)
    return loudness


def centred(rng, shape, spread, limit, shards=(), held_as=jnp.bfloat16):
    gain = block_scale(rng, shape, shards, -0.22, 0.18) if shards else 1.0
    values = jax.random.normal(rng, shape, jnp.float32) * spread * gain
    return jnp.minimum(jnp.maximum(values, -limit), limit).astype(held_as)


def setup_inputs(seed: int = 0, part: int = 0) -> dict:
    arg_keys = jax.random.split(jax.random.key(seed), 5)
    part_keys = jax.random.split(jax.random.fold_in(arg_keys[4], part), 5)
    return {
        "traces": centred(part_keys[0], (2, ORDER, ORDER), 1.0, 6.0, ((1, 4), (2, 4))),
        "recv_live": set_ends((jax.random.randint(part_keys[1], (ORDER,), 0, 8) < 7).astype(jnp.int32), jax.random.fold_in(part_keys[1], 1), 0, 1),
        "missing": draw_missing(jax.random.fold_in(jax.random.fold_in(arg_keys[4], part), 71), part),
        "wavelet": jnp.clip(jax.random.uniform(part_keys[3], (2,), jnp.float32, 0.5, 1.5), 0.5, 1.5),
    }


def reference(traces, recv_live, missing, wavelet):
    tile_size = ORDER // N_ROW
    positions = jnp.arange(tile_size, dtype=jnp.int32)
    dead_rows = jnp.any(positions[None, :, None] == missing[:, None, :], axis=2).reshape(ORDER)
    shot_live = jnp.logical_not(dead_rows)
    recv_mask = recv_live == 1
    zero_bf = jnp.zeros((), jnp.bfloat16)
    direct = jnp.where(recv_mask[None, None, :], traces, zero_bf)
    flipped = jnp.swapaxes(traces, 1, 2)
    mirrored = jnp.where(recv_mask[None, :, None] & shot_live[None, None, :], flipped, zero_bf)
    filled = jnp.where(shot_live[None, :, None], direct, mirrored).astype(jnp.bfloat16)
    window = filled.reshape(2, ORDER, N_ROW, tile_size)[:, :, :, :WIN].reshape(2, ORDER, N_ROW * WIN)
    left_tile = filled.astype(jnp.float32)
    right_tile = window.astype(jnp.float32)

    def matmul(first, second):
        return jnp.dot(first, second, precision=lax.Precision.HIGHEST, preferred_element_type=jnp.float32)
    real_part = matmul(left_tile[0], right_tile[0]) - matmul(left_tile[1], right_tile[1])
    imag_part = matmul(left_tile[0], right_tile[1]) + matmul(left_tile[1], right_tile[0])
    norm_scale = 1.0 / math.sqrt(ORDER)
    pred_real = (wavelet[0] * real_part - wavelet[1] * imag_part) * norm_scale
    pred_imag = (wavelet[0] * imag_part + wavelet[1] * real_part) * norm_scale
    return jnp.stack([right_tile[0] - pred_real, right_tile[1] - pred_imag])
```

```python
import functools
import math

import jax
import jax.numpy as jnp
from jax import lax
from jax.experimental import pallas as pl
from jax.experimental.pallas import tpu as pltpu
from jax.sharding import PartitionSpec as P

WIN = 128
LANES = 128
VMEM_LIMIT = 56 * 2**20


def row_block(rows):
    for size in (512, 384, 256, 128):
        if rows % size == 0:
            return size
    return rows


def one_hot(positions_row, rows, dtype):
    lanes = positions_row.shape[1]
    row_ids = lax.broadcasted_iota(jnp.int32, (rows, lanes), 0)
    return jnp.where(row_ids == positions_row, 1.0, 0.0).astype(dtype)


def pick_kernel(traces_ref, miss_ref, recv_ref, live_ref, out_ref, hot_ref):
    @pl.when(pl.program_id(0) == 0)
    def _():
        hot = one_hot(miss_ref[...], hot_ref.shape[0], jnp.bfloat16)
        alive = jnp.dot(recv_ref[...], hot, preferred_element_type=jnp.float32)
        hot_ref[...] = hot * alive[0:1].astype(jnp.bfloat16)

    misses = out_ref.shape[1]
    for part in range(2):
        picked = jnp.dot(traces_ref[part], hot_ref[...], preferred_element_type=jnp.float32)
        turned = picked.T * live_ref[0:1, :]
        out_ref[part] = turned[:misses].astype(jnp.bfloat16)


def pick_columns(traces, miss_lanes, recv8, live8, misses):
    _, rows, cols = traces.shape
    block = row_block(rows)
    return pl.pallas_call(
        pick_kernel,
        grid=(rows // block,),
        in_specs=[
            pl.BlockSpec((2, block, cols), lambda i: (0, i, 0)),
            pl.BlockSpec((1, LANES), lambda i: (0, 0)),
            pl.BlockSpec((8, cols), lambda i: (0, 0)),
            pl.BlockSpec((8, block), lambda i: (0, i)),
        ],
        out_specs=pl.BlockSpec((2, misses, block), lambda i: (0, 0, i)),
        out_shape=jax.ShapeDtypeStruct((2, misses, rows), jnp.bfloat16),
        scratch_shapes=[pltpu.VMEM((cols, LANES), jnp.bfloat16)],
        compiler_params=pltpu.CompilerParams(vmem_limit_bytes=VMEM_LIMIT),
        cost_estimate=pl.CostEstimate(
            flops=4 * rows * cols * LANES, bytes_accessed=4 * rows * cols, transcendentals=0
        ),
        name="pick_columns",
    )(traces, miss_lanes, recv8, live8)


def window_kernel(raw_ref, patch_ref, miss_ref, recv_ref, out_ref):
    rows = raw_ref.shape[1]
    misses = patch_ref.shape[1]
    hot = one_hot(miss_ref[...], rows, jnp.float32)
    dead = jnp.max(hot, axis=1, keepdims=True)
    hot = hot[:, :misses].astype(jnp.bfloat16)
    keep = (1.0 - dead) * recv_ref[0:1, :].astype(jnp.float32)
    for part in range(2):
        patch = jnp.dot(hot, patch_ref[part], preferred_element_type=jnp.float32)
        filled = raw_ref[part].astype(jnp.float32) * keep + patch
        out_ref[:, part * WIN:(part + 1) * WIN] = filled.astype(jnp.bfloat16)


def fill_window(raw, patch, miss_lanes, recv8):
    rows = raw.shape[1]
    return pl.pallas_call(
        window_kernel,
        out_shape=jax.ShapeDtypeStruct((rows, 2 * WIN), jnp.bfloat16),
        compiler_params=pltpu.CompilerParams(vmem_limit_bytes=VMEM_LIMIT),
        cost_estimate=pl.CostEstimate(
            flops=4 * rows * LANES * WIN, bytes_accessed=8 * rows * WIN, transcendentals=0
        ),
        name="fill_window",
    )(raw, patch, miss_lanes, recv8)


def complex_rows(real_rows, imag_rows, right):
    first = jnp.dot(real_rows, right, preferred_element_type=jnp.float32)
    second = jnp.dot(imag_rows, right, preferred_element_type=jnp.float32)
    real_part = first[:, :WIN] - second[:, WIN:]
    imag_part = first[:, WIN:] + second[:, :WIN]
    return real_part, imag_part


def product_kernel(grid_size, col_ref, traces_ref, recv_ref, right_ref, extra_ref, *outs):
    send_ref, keep_ref, send_extra_ref, keep_extra_ref = outs
    recv = recv_ref[0:1, :]
    real_rows = traces_ref[0] * recv
    imag_rows = traces_ref[1] * recv
    for offset in range(grid_size):
        right = right_ref[col_ref[0] ^ offset]
        out_ref = send_ref if offset % 2 else keep_ref
        real_part, imag_part = complex_rows(real_rows, imag_rows, right)
        out_ref[offset // 2, :, :WIN] = real_part
        out_ref[offset // 2, :, WIN:] = imag_part

    @pl.when(pl.program_id(0) == 0)
    def _():
        for offset in range(grid_size):
            right = right_ref[col_ref[0] ^ offset]
            out_ref = send_extra_ref if offset % 2 else keep_extra_ref
            real_part, imag_part = complex_rows(extra_ref[0], extra_ref[1], right)
            out_ref[offset // 2, :, :WIN] = real_part
            out_ref[offset // 2, :, WIN:] = imag_part


def products(col_index, traces, recv8, right, extra):
    _, rows, cols = traces.shape
    grid_size = right.shape[0]
    misses = extra.shape[1]
    block = row_block(rows)
    half = grid_size // 2
    main = pl.BlockSpec((half, block, 2 * WIN), lambda i, c: (0, i, 0))
    tail = pl.BlockSpec((half, misses, 2 * WIN), lambda i, c: (0, 0, 0))
    main_shape = jax.ShapeDtypeStruct((half, rows, 2 * WIN), jnp.float32)
    tail_shape = jax.ShapeDtypeStruct((half, misses, 2 * WIN), jnp.float32)
    return pl.pallas_call(
        functools.partial(product_kernel, grid_size),
        grid_spec=pltpu.PrefetchScalarGridSpec(
            num_scalar_prefetch=1,
            grid=(rows // block,),
            in_specs=[
                pl.BlockSpec((2, block, cols), lambda i, c: (0, i, 0)),
                pl.BlockSpec((8, cols), lambda i, c: (0, 0)),
                pl.BlockSpec((grid_size, cols, 2 * WIN), lambda i, c: (0, 0, 0)),
                pl.BlockSpec((2, misses, cols), lambda i, c: (0, 0, 0)),
            ],
            out_specs=[main, main, tail, tail],
        ),
        out_shape=[main_shape, main_shape, tail_shape, tail_shape],
        compiler_params=pltpu.CompilerParams(vmem_limit_bytes=VMEM_LIMIT),
        cost_estimate=pl.CostEstimate(
            flops=8 * (rows + misses) * cols * WIN * grid_size,
            bytes_accessed=4 * rows * cols + 8 * grid_size * rows * WIN,
            transcendentals=0,
        ),
        name="products",
    )(col_index, traces, recv8, right, extra)


def finish_kernel(miss_ref, wave_ref, raw_ref, recv_ref, extra_ref, *refs):
    sums, extra_sums = refs[:3], refs[3:6]
    out_ref, row_ref = refs[6], refs[7]

    def subtract(window, terms):
        total = terms[0][...] + terms[1][...] + terms[2][...]
        real_part, imag_part = total[:, :WIN], total[:, WIN:]
        pred_real = real_part * wave_ref[0] - imag_part * wave_ref[1]
        pred_imag = imag_part * wave_ref[0] + real_part * wave_ref[1]
        return window[0] - pred_real, window[1] - pred_imag

    recv = recv_ref[0:1, :].astype(jnp.float32)
    window = [raw_ref[part].astype(jnp.float32) * recv for part in range(2)]
    out_ref[0], out_ref[1] = subtract(window, sums)
    window = [extra_ref[part].astype(jnp.float32) for part in range(2)]
    row_ref[0], row_ref[1] = subtract(window, extra_sums)

    def place(m, carry):
        for part in range(2):
            out_ref[part, pl.ds(miss_ref[m], 1), :] = row_ref[part, pl.ds(m, 1), :]
        return carry

    lax.fori_loop(0, row_ref.shape[1], place, 0, unroll=8)


def finish(miss, wave, raw, recv8, extra, sums, extra_sums):
    _, rows, _ = raw.shape
    misses = extra.shape[1]
    vmem = pl.BlockSpec(memory_space=pltpu.VMEM)
    smem = pl.BlockSpec(memory_space=pltpu.SMEM)
    return pl.pallas_call(
        finish_kernel,
        in_specs=[smem, smem] + [vmem] * 9,
        out_specs=vmem,
        out_shape=jax.ShapeDtypeStruct((2, rows, WIN), jnp.float32),
        scratch_shapes=[pltpu.VMEM((2, misses, WIN), jnp.float32)],
        compiler_params=pltpu.CompilerParams(vmem_limit_bytes=VMEM_LIMIT),
        cost_estimate=pl.CostEstimate(
            flops=20 * rows * WIN, bytes_accessed=36 * rows * WIN, transcendentals=0
        ),
        name="finish",
    )(miss, wave, raw, recv8, extra, *sums, *extra_sums)


def local(traces, recv_live, missing, wavelet):
    tile = traces.shape[1]
    grid_size = lax.axis_size("row")
    misses = missing.shape[1]
    order = recv_live.shape[0]
    row_index = lax.axis_index("row")
    col_index = lax.axis_index("col")
    mirror = [
        (a * grid_size + b, b * grid_size + a) for a in range(grid_size) for b in range(grid_size)
    ]

    def transpose(block):
        return lax.ppermute(block, ("row", "col"), mirror)

    raw = traces[:, :, :WIN]
    raw_turned = transpose(raw)

    miss_row = lax.dynamic_index_in_dim(missing, row_index, 0, keepdims=False)
    miss_col = lax.dynamic_index_in_dim(missing, col_index, 0, keepdims=False)
    miss_col_lanes = jnp.pad(miss_col, (0, LANES - misses), constant_values=-1)[None]
    positions = jnp.arange(tile, dtype=jnp.int32)
    live_row = jnp.all(positions[:, None] != miss_row[None, :], axis=1)
    live8 = jnp.broadcast_to(live_row.astype(jnp.float32)[None], (8, tile))
    recv_mask = (recv_live == 1).astype(jnp.bfloat16)
    recv_row = lax.dynamic_slice_in_dim(recv_mask, row_index * tile, WIN)
    recv_row8 = jnp.broadcast_to(recv_row[None], (8, WIN))
    recv_col = lax.dynamic_slice_in_dim(recv_mask, col_index * tile, tile)
    recv_col8 = jnp.broadcast_to(recv_col[None], (8, tile))

    picked = pick_columns(traces, miss_col_lanes, recv_col8, live8, misses)
    extra = transpose(picked)
    window = fill_window(raw_turned, picked[:, :, :WIN], miss_col_lanes, recv_row8)
    right = lax.all_gather(window, "row", axis=0, tiled=False)

    send, keep, send_extra, keep_extra = products(
        col_index[None].astype(jnp.int32), traces, recv_col8, right, extra
    )

    def swap(block, stride):
        pairs = [(i, i ^ stride) for i in range(grid_size)]
        return lax.ppermute(block, "col", pairs)

    def halve_from(kept, got):
        stride = 2
        while kept.shape[0] > 2:
            total = kept + got
            got = swap(total[1::2], stride)
            kept = total[0::2]
            stride *= 2
        last = swap(kept[1] + got[1], stride)
        return (kept[0], got[0], last)

    def scatter_sum(sent, kept):
        return halve_from(kept, swap(sent, 1))

    sums = scatter_sum(send, keep)
    extra_sums = scatter_sum(send_extra, keep_extra)
    wave = wavelet * (1.0 / math.sqrt(order))
    return finish(
        miss_row, wave, raw, recv_col8[:, :WIN], extra[:, :, :WIN], sums, extra_sums
    )


def solution(mesh):
    in_specs = (P("freq", "row", "col"), P("freq"), P("freq", None), P("freq"))
    out_specs = P("freq", "row", "col")
    return jax.shard_map(local, mesh=mesh, in_specs=in_specs, out_specs=out_specs, check_vma=False)
```

```python
import functools
import math

import jax
import jax.numpy as jnp
from jax import lax
from jax.experimental import pallas as pl
from jax.experimental.pallas import tpu as pltpu
from jax.sharding import PartitionSpec as P

WIN = 128
LANES = 128
CHUNKS = 1
WIDTH = WIN // CHUNKS
VMEM_LIMIT = 48 * 2**20
VMEM = pl.BlockSpec(memory_space=pltpu.VMEM)
SMEM = pl.BlockSpec(memory_space=pltpu.SMEM)


def params():
    return pltpu.CompilerParams(vmem_limit_bytes=VMEM_LIMIT)


def cost(flops, accessed):
    return pl.CostEstimate(flops=int(flops), bytes_accessed=int(accessed), transcendentals=0)


def row_block(rows):
    for size in (512, 384, 256, 128):
        if rows % size == 0:
            return size
    return rows


def one_hot(positions_row, rows, dtype):
    lanes = positions_row.shape[1]
    row_ids = lax.broadcasted_iota(jnp.int32, (rows, lanes), 0)
    return jnp.where(row_ids == positions_row, 1.0, 0.0).astype(dtype)


def pack(real_part, imag_part):
    if CHUNKS == 1:
        return [jnp.concatenate([real_part, imag_part], axis=1)]
    first = lax.broadcasted_iota(jnp.int32, real_part.shape, 1) < WIDTH
    low = jnp.where(first, real_part, pltpu.roll(imag_part, WIDTH, 1))
    high = jnp.where(first, pltpu.roll(real_part, WIDTH, 1), imag_part)
    return [low, high]


def unpack(chunks):
    if CHUNKS == 1:
        return chunks[0][:, :WIN], chunks[0][:, WIN:]
    low, high = chunks
    first = lax.broadcasted_iota(jnp.int32, low.shape, 1) < WIDTH
    real_part = jnp.where(first, low, pltpu.roll(high, WIDTH, 1))
    imag_part = jnp.where(first, pltpu.roll(low, WIDTH, 1), high)
    return real_part, imag_part


def cut_kernel(traces_ref, *out_refs):
    chunks = pack(traces_ref[0].astype(jnp.float32), traces_ref[1].astype(jnp.float32))
    for out_ref, chunk in zip(out_refs, chunks):
        out_ref[...] = chunk.astype(jnp.bfloat16)


def cut_window(traces):
    rows = traces.shape[1]
    return pl.pallas_call(
        cut_kernel,
        grid=(1,),
        in_specs=[pl.BlockSpec((2, rows, WIN), lambda i: (0, 0, 0))],
        out_specs=[pl.BlockSpec((rows, 2 * WIDTH), lambda i: (0, 0))] * CHUNKS,
        out_shape=[jax.ShapeDtypeStruct((rows, 2 * WIDTH), jnp.bfloat16)] * CHUNKS,
        compiler_params=params(),
        cost_estimate=cost(rows * WIN, 8 * rows * WIN),
        name="cut_window",
    )(traces)


def pick_kernel(traces_ref, miss_ref, recv_ref, live_ref, out_ref, hot_ref):
    @pl.when(pl.program_id(0) == 0)
    def _():
        hot = one_hot(miss_ref[...], hot_ref.shape[0], jnp.bfloat16)
        alive = jnp.dot(recv_ref[...], hot, preferred_element_type=jnp.float32)
        hot_ref[...] = hot * alive[0:1].astype(jnp.bfloat16)

    misses = out_ref.shape[1]
    for part in range(2):
        picked = jnp.dot(traces_ref[part], hot_ref[...], preferred_element_type=jnp.float32)
        turned = picked.T * live_ref[0:1, :]
        out_ref[part] = turned[:misses].astype(jnp.bfloat16)


def pick_columns(traces, miss_lanes, recv8, live8, misses):
    _, rows, cols = traces.shape
    block = row_block(rows)
    return pl.pallas_call(
        pick_kernel,
        grid=(rows // block,),
        in_specs=[
            pl.BlockSpec((2, block, cols), lambda i: (0, i, 0)),
            pl.BlockSpec((1, LANES), lambda i: (0, 0)),
            pl.BlockSpec((8, cols), lambda i: (0, 0)),
            pl.BlockSpec((8, block), lambda i: (0, i)),
        ],
        out_specs=pl.BlockSpec((2, misses, block), lambda i: (0, 0, i)),
        out_shape=jax.ShapeDtypeStruct((2, misses, rows), jnp.bfloat16),
        scratch_shapes=[pltpu.VMEM((cols, LANES), jnp.bfloat16)],
        compiler_params=params(),
        cost_estimate=cost(4 * rows * cols * 2 * LANES, 4 * rows * cols),
        name="pick_columns",
    )(traces, miss_lanes, recv8, live8)


def fill_kernel(chunk, raw_ref, patch_ref, miss_ref, recv_ref, out_ref):
    rows = raw_ref.shape[0]
    misses = patch_ref.shape[1]
    hot = one_hot(miss_ref[...], rows, jnp.float32)
    dead = jnp.max(hot, axis=1, keepdims=True)
    hot = hot[:, :misses].astype(jnp.bfloat16)
    patch = pack(patch_ref[0].astype(jnp.float32), patch_ref[1].astype(jnp.float32))[chunk]
    mask = recv_ref[...].astype(jnp.float32)
    mask = pack(mask, mask)[chunk][0:1, :]
    moved = jnp.dot(hot, patch.astype(jnp.bfloat16), preferred_element_type=jnp.float32)
    filled = raw_ref[...].astype(jnp.float32) * ((1.0 - dead) * mask) + moved
    out_ref[...] = filled.astype(jnp.bfloat16)


def fill_window(chunk, raw, picked, miss_lanes, recv8):
    rows, lanes = raw.shape
    misses = picked.shape[1]
    return pl.pallas_call(
        functools.partial(fill_kernel, chunk),
        grid=(1,),
        in_specs=[
            pl.BlockSpec((rows, lanes), lambda i: (0, 0)),
            pl.BlockSpec((2, misses, WIN), lambda i: (0, 0, 0)),
            pl.BlockSpec((1, LANES), lambda i: (0, 0)),
            pl.BlockSpec((8, WIN), lambda i: (0, 0)),
        ],
        out_specs=pl.BlockSpec((rows, lanes), lambda i: (0, 0)),
        out_shape=jax.ShapeDtypeStruct((rows, lanes), jnp.bfloat16),
        compiler_params=params(),
        cost_estimate=cost(4 * rows * LANES * lanes, 8 * rows * lanes),
        name="fill_window",
    )(raw, picked, miss_lanes, recv8)


def complex_rows(real_rows, imag_rows, right):
    first = jnp.dot(real_rows, right, preferred_element_type=jnp.float32)
    second = jnp.dot(imag_rows, right, preferred_element_type=jnp.float32)
    if CHUNKS == 1:
        real_part = first[:, :WIN] - second[:, WIN:]
        imag_part = first[:, WIN:] + second[:, :WIN]
        return jnp.concatenate([real_part, imag_part], axis=1)
    turned = pltpu.roll(second, WIDTH, 1)
    low = lax.broadcasted_iota(jnp.int32, first.shape, 1) < WIDTH
    return first + jnp.where(low, -turned, turned)


def product_kernel(block, miss_ref, traces_ref, recv_ref, right_ref, extra_ref, out_ref, extra_out):
    step = pl.program_id(0)
    recv = recv_ref[0:1, :]
    right = right_ref[...]
    start = pl.multiple_of(step * block, block)
    out_ref[pl.ds(start, block), :] = complex_rows(
        traces_ref[0] * recv, traces_ref[1] * recv, right
    )

    @pl.when(step == pl.num_programs(0) - 1)
    def _():
        extra_out[...] = complex_rows(extra_ref[0], extra_ref[1], right)

        def place(m, carry):
            out_ref[pl.ds(miss_ref[m], 1), :] = extra_out[pl.ds(m, 1), :]
            return carry

        lax.fori_loop(0, extra_out.shape[0], place, 0, unroll=8)


def product(miss, traces, recv8, right, extra):
    _, rows, cols = traces.shape
    lanes = right.shape[1]
    misses = extra.shape[1]
    block = row_block(rows)
    return pl.pallas_call(
        functools.partial(product_kernel, block),
        grid_spec=pltpu.PrefetchScalarGridSpec(
            num_scalar_prefetch=1,
            grid=(rows // block,),
            in_specs=[
                pl.BlockSpec((2, block, cols), lambda i, m: (0, i, 0)),
                pl.BlockSpec((8, cols), lambda i, m: (0, 0)),
                pl.BlockSpec((cols, lanes), lambda i, m: (0, 0)),
                pl.BlockSpec((2, misses, cols), lambda i, m: (0, 0, 0)),
            ],
            out_specs=pl.BlockSpec((rows, lanes), lambda i, m: (0, 0)),
            scratch_shapes=[pltpu.VMEM((misses, lanes), jnp.float32)],
        ),
        out_shape=jax.ShapeDtypeStruct((rows, lanes), jnp.float32),
        compiler_params=params(),
        cost_estimate=cost(8 * rows * cols * WIN, 4 * rows * cols + 4 * rows * lanes),
        name="product",
    )(miss, traces, recv8, right, extra)


def own_kernel(miss_ref, traces_ref, recv_ref, extra_ref, out_ref, row_ref):
    recv = recv_ref[0:1, :].astype(jnp.float32)
    for part in range(2):
        out_ref[part] = traces_ref[part].astype(jnp.float32) * recv
        row_ref[part] = extra_ref[part].astype(jnp.float32)

    def place(m, carry):
        for part in range(2):
            out_ref[part, pl.ds(miss_ref[m], 1), :] = row_ref[part, pl.ds(m, 1), :]
        return carry

    lax.fori_loop(0, row_ref.shape[1], place, 0, unroll=8)


def own_window(miss, traces, recv8, extra):
    rows = traces.shape[1]
    misses = extra.shape[1]
    return pl.pallas_call(
        own_kernel,
        grid_spec=pltpu.PrefetchScalarGridSpec(
            num_scalar_prefetch=1,
            grid=(1,),
            in_specs=[
                pl.BlockSpec((2, rows, WIN), lambda i, m: (0, 0, 0)),
                pl.BlockSpec((8, WIN), lambda i, m: (0, 0)),
                pl.BlockSpec((2, misses, WIN), lambda i, m: (0, 0, 0)),
            ],
            out_specs=pl.BlockSpec((2, rows, WIN), lambda i, m: (0, 0, 0)),
            scratch_shapes=[pltpu.VMEM((2, misses, WIN), jnp.float32)],
        ),
        out_shape=jax.ShapeDtypeStruct((2, rows, WIN), jnp.float32),
        compiler_params=params(),
        cost_estimate=cost(4 * rows * WIN, 12 * rows * WIN),
        name="own_window",
    )(miss, traces, recv8, extra)


def finish_kernel(wave_ref, flag_ref, window_ref, *refs):
    out_ref = refs[-1]
    totals = []
    for chunk in range(CHUNKS):
        early_ref, last_ref, got_ref = refs[3 * chunk:3 * chunk + 3]
        totals.append(early_ref[...] + last_ref[...] * flag_ref[0] + got_ref[...])
    real_part, imag_part = unpack(totals)
    out_ref[0] = window_ref[0] - (real_part * wave_ref[0] - imag_part * wave_ref[1])
    out_ref[1] = window_ref[1] - (imag_part * wave_ref[0] + real_part * wave_ref[1])


def finish(wave, flag, window, terms):
    _, rows, _ = window.shape
    flat = [term for chunk in terms for term in chunk]
    return pl.pallas_call(
        finish_kernel,
        in_specs=[SMEM, SMEM] + [VMEM] * (1 + len(flat)),
        out_specs=VMEM,
        out_shape=jax.ShapeDtypeStruct(window.shape, jnp.float32),
        compiler_params=params(),
        cost_estimate=cost(20 * rows * WIN, 40 * rows * WIN),
        name="finish",
    )(wave, flag, window, *flat)


def spread(block, grid_size, row_index):
    up, down = [block], [block]
    for hop in range(1, grid_size):
        up.append(lax.ppermute(up[-1], "row", [(i, i + 1) for i in range(hop - 1, grid_size - 1)]))
        down.append(lax.ppermute(down[-1], "row", [(i + 1, i) for i in range(grid_size - hop)]))
    slots = [block]
    for offset in range(1, grid_size):
        chosen = None
        for row in range(grid_size):
            other = row ^ offset
            source = up[row - other] if other < row else down[other - row]
            chosen = source if chosen is None else jnp.where(row_index == row, source, chosen)
        slots.append(chosen)
    return slots


def sum_to_column(partial_sum, offset, grid_size):
    stride = 1
    while True:
        pairs = []
        for row in range(grid_size):
            for col in range(grid_size):
                apart = col ^ row ^ offset
                if apart % (2 * stride) == stride:
                    pairs.append((row * grid_size + col, row * grid_size + (col ^ stride)))
        got = lax.ppermute(partial_sum, ("row", "col"), pairs)
        stride *= 2
        if stride >= grid_size:
            return partial_sum, got
        partial_sum = partial_sum + got


def local(traces, recv_live, missing, wavelet):
    tile = traces.shape[1]
    grid_size = lax.axis_size("row")
    misses = missing.shape[1]
    order = recv_live.shape[0]
    row_index = lax.axis_index("row")
    col_index = lax.axis_index("col")
    mirror = [
        (a * grid_size + b, b * grid_size + a) for a in range(grid_size) for b in range(grid_size)
    ]

    def transpose(block):
        return lax.ppermute(block, ("row", "col"), mirror)

    turned = [transpose(chunk) for chunk in cut_window(traces)]

    miss_row = lax.dynamic_index_in_dim(missing, row_index, 0, keepdims=False)
    miss_col = lax.dynamic_index_in_dim(missing, col_index, 0, keepdims=False)
    miss_col_lanes = jnp.pad(miss_col, (0, LANES - misses), constant_values=-1)[None]
    positions = jnp.arange(tile, dtype=jnp.int32)
    live_row = jnp.all(positions[:, None] != miss_row[None, :], axis=1)
    live8 = jnp.broadcast_to(live_row.astype(jnp.float32)[None], (8, tile))
    recv_mask = (recv_live == 1).astype(jnp.bfloat16)
    recv_row = lax.dynamic_slice_in_dim(recv_mask, row_index * tile, WIN)
    recv_row8 = jnp.broadcast_to(recv_row[None], (8, WIN))
    recv_col = lax.dynamic_slice_in_dim(recv_mask, col_index * tile, tile)
    recv_col8 = jnp.broadcast_to(recv_col[None], (8, tile))

    picked = pick_columns(traces, miss_col_lanes, recv_col8, live8, misses)
    extra = transpose(picked)
    mine = row_index ^ col_index
    terms = []
    for chunk in range(CHUNKS):
        window = fill_window(chunk, turned[chunk], picked, miss_col_lanes, recv_row8)
        slots = spread(window, grid_size, row_index)
        early = None
        for offset in range(grid_size):
            partial_sum = product(miss_row, traces, recv_col8, slots[offset], extra)
            there, got = sum_to_column(partial_sum, offset, grid_size)
            if offset == grid_size - 1:
                terms.append((early, there, got))
                continue
            total = jnp.where(mine == offset, there, 0.0) + got
            early = total if early is None else early + total
    window = own_window(miss_row, traces, recv_col8, extra)
    wave = wavelet * (1.0 / math.sqrt(order))
    flag = (mine == grid_size - 1).astype(jnp.float32)[None]
    return finish(wave, flag, window, terms)


def solution(mesh):
    in_specs = (P("freq", "row", "col"), P("freq"), P("freq", None), P("freq"))
    out_specs = P("freq", "row", "col")
    return jax.shard_map(local, mesh=mesh, in_specs=in_specs, out_specs=out_specs, check_vma=False)
```

```python
import functools
import math

import jax
import jax.numpy as jnp
from jax import lax
from jax.experimental import pallas as pl
from jax.experimental.pallas import tpu as pltpu
from jax.sharding import PartitionSpec as P

WIN = 128
LANES = 128
CHUNKS = 1
WIDTH = WIN // CHUNKS
VMEM_LIMIT = 32 * 2**20
VMEM = pl.BlockSpec(memory_space=pltpu.VMEM)
SMEM = pl.BlockSpec(memory_space=pltpu.SMEM)


def params():
    return pltpu.CompilerParams(vmem_limit_bytes=VMEM_LIMIT)


def cost(flops, accessed):
    return pl.CostEstimate(
        flops=int(flops) // 64, bytes_accessed=int(accessed) // 64, transcendentals=0
    )


def row_block(rows):
    for size in (512, 384, 256, 128):
        if rows % size == 0:
            return size
    return rows


def one_hot(positions_row, rows, dtype):
    lanes = positions_row.shape[1]
    row_ids = lax.broadcasted_iota(jnp.int32, (rows, lanes), 0)
    return jnp.where(row_ids == positions_row, 1.0, 0.0).astype(dtype)


def pack(real_part, imag_part):
    if CHUNKS == 1:
        return [jnp.concatenate([real_part, imag_part], axis=1)]
    first = lax.broadcasted_iota(jnp.int32, real_part.shape, 1) < WIDTH
    low = jnp.where(first, real_part, pltpu.roll(imag_part, WIDTH, 1))
    high = jnp.where(first, pltpu.roll(real_part, WIDTH, 1), imag_part)
    return [low, high]


def unpack(chunks):
    if CHUNKS == 1:
        return chunks[0][:, :WIN], chunks[0][:, WIN:]
    low, high = chunks
    first = lax.broadcasted_iota(jnp.int32, low.shape, 1) < WIDTH
    real_part = jnp.where(first, low, pltpu.roll(high, WIDTH, 1))
    imag_part = jnp.where(first, pltpu.roll(low, WIDTH, 1), high)
    return real_part, imag_part


def halves(real_part, imag_part):
    return [real_part, imag_part] if CHUNKS == 1 else pack(real_part, imag_part)


def cut_kernel(traces_ref, *out_refs):
    parts = halves(traces_ref[0].astype(jnp.float32), traces_ref[1].astype(jnp.float32))
    for out_ref, part in zip(out_refs, parts):
        out_ref[...] = part.astype(jnp.bfloat16)


def cut_window(traces):
    rows = traces.shape[1]
    return pl.pallas_call(
        cut_kernel,
        grid=(1,),
        in_specs=[pl.BlockSpec((2, rows, WIN), lambda i: (0, 0, 0))],
        out_specs=[pl.BlockSpec((rows, WIN), lambda i: (0, 0))] * 2,
        out_shape=[jax.ShapeDtypeStruct((rows, WIN), jnp.bfloat16)] * 2,
        compiler_params=params(),
        cost_estimate=cost(rows * WIN, 8 * rows * WIN),
        name="cut_window",
    )(traces)


def pick_kernel(traces_ref, miss_ref, recv_ref, live_ref, out_ref, tile_ref, hot_ref):
    @pl.when(pl.program_id(0) == 0)
    def _():
        hot = one_hot(miss_ref[...], hot_ref.shape[0], jnp.bfloat16)
        alive = jnp.dot(recv_ref[...], hot, preferred_element_type=jnp.float32)
        hot_ref[...] = hot * alive[0:1].astype(jnp.bfloat16)

    misses = out_ref.shape[1]
    for part in range(2):
        picked = jnp.dot(traces_ref[part], hot_ref[...], preferred_element_type=jnp.float32)
        turned = picked.T * live_ref[0:1, :]
        out_ref[part] = turned[:misses].astype(jnp.bfloat16)
        tile_ref[part] = traces_ref[part] * recv_ref[0:1, :]


def pick_columns(traces, miss_lanes, recv8, live8, misses):
    _, rows, cols = traces.shape
    block = row_block(rows)
    return pl.pallas_call(
        pick_kernel,
        grid=(rows // block,),
        in_specs=[
            pl.BlockSpec((2, block, cols), lambda i: (0, i, 0)),
            pl.BlockSpec((1, LANES), lambda i: (0, 0)),
            pl.BlockSpec((8, cols), lambda i: (0, 0)),
            pl.BlockSpec((8, block), lambda i: (0, i)),
        ],
        out_specs=[
            pl.BlockSpec((2, misses, block), lambda i: (0, 0, i)),
            pl.BlockSpec((2, block, cols), lambda i: (0, i, 0)),
        ],
        out_shape=[
            jax.ShapeDtypeStruct((2, misses, rows), jnp.bfloat16),
            jax.ShapeDtypeStruct(traces.shape, jnp.bfloat16),
        ],
        scratch_shapes=[pltpu.VMEM((cols, LANES), jnp.bfloat16)],
        compiler_params=params(),
        cost_estimate=cost(4 * rows * cols * 2 * LANES, 4 * rows * cols),
        name="pick_columns",
    )(traces, miss_lanes, recv8, live8)


def fill_kernel(counts, first_half, patch_ref, miss_ref, recv_ref, *refs):
    out_ref = refs[-1]
    rows = out_ref.shape[0]
    misses = patch_ref.shape[1]
    hot = one_hot(miss_ref[...], rows, jnp.float32)
    dead = jnp.max(hot, axis=1, keepdims=True)
    hot = hot[:, :misses].astype(jnp.bfloat16)
    patches = halves(patch_ref[0].astype(jnp.float32), patch_ref[1].astype(jnp.float32))
    mask = recv_ref[...].astype(jnp.float32)
    mask = halves(mask, mask)[0][0:1, :]
    used = 0
    for index, count in enumerate(counts):
        arrived = refs[used][...].astype(jnp.float32)
        for more in refs[used + 1:used + count]:
            arrived = arrived + more[...].astype(jnp.float32)
        used += count
        patch = patches[first_half + index].astype(jnp.bfloat16)
        moved = jnp.dot(hot, patch, preferred_element_type=jnp.float32)
        filled = arrived * ((1.0 - dead) * mask) + moved
        out_ref[:, index * WIN:(index + 1) * WIN] = filled.astype(jnp.bfloat16)


def fill_window(first_half, arrived, picked, miss_lanes, recv8):
    rows = arrived[0][0].shape[0]
    misses = picked.shape[1]
    counts = tuple(len(group) for group in arrived)
    flat = [part for group in arrived for part in group]
    lanes = len(counts) * WIN
    whole = pl.BlockSpec((rows, WIN), lambda i: (0, 0))
    return pl.pallas_call(
        functools.partial(fill_kernel, counts, first_half),
        grid=(1,),
        in_specs=[
            pl.BlockSpec((2, misses, WIN), lambda i: (0, 0, 0)),
            pl.BlockSpec((1, LANES), lambda i: (0, 0)),
            pl.BlockSpec((8, WIN), lambda i: (0, 0)),
        ]
        + [whole] * len(flat),
        out_specs=pl.BlockSpec((rows, lanes), lambda i: (0, 0)),
        out_shape=jax.ShapeDtypeStruct((rows, lanes), jnp.bfloat16),
        compiler_params=params(),
        cost_estimate=cost(4 * rows * LANES * lanes, 8 * rows * lanes),
        name="fill_window",
    )(picked, miss_lanes, recv8, *flat)


def complex_rows(real_rows, imag_rows, right):
    first = jnp.dot(real_rows, right, preferred_element_type=jnp.float32)
    second = jnp.dot(imag_rows, right, preferred_element_type=jnp.float32)
    if CHUNKS == 1:
        real_part = first[:, :WIN] - second[:, WIN:]
        imag_part = first[:, WIN:] + second[:, :WIN]
        return jnp.concatenate([real_part, imag_part], axis=1)
    turned = pltpu.roll(second, WIDTH, 1)
    low = lax.broadcasted_iota(jnp.int32, first.shape, 1) < WIDTH
    return first + jnp.where(low, -turned, turned)


def choose(out_ref, pick, refs):
    for index, ref in enumerate(refs):

        @pl.when(pick == index)
        def _():
            out_ref[...] = ref[...]


def product_kernel(block, counts, pick_ref, tile_ref, *refs):
    total = sum(counts)
    out_refs, right_ref = refs[total:-1], refs[-1]
    used = 0
    for place, (count, out_ref) in enumerate(zip(counts, out_refs)):
        choose(right_ref, pick_ref[place], refs[used:used + count])
        used += count
        for start in range(0, out_ref.shape[0], block):
            rows = pl.ds(start, block)
            out_ref[rows, :] = complex_rows(
                tile_ref[0, rows, :], tile_ref[1, rows, :], right_ref[...]
            )


def products(tile, groups):
    _, rows, cols = tile.shape
    lanes = groups[0][1][0].shape[1]
    counts = tuple(len(sources) for _, sources in groups)
    flat = [source for _, sources in groups for source in sources]
    picks = jnp.stack([pick for pick, _ in groups]).astype(jnp.int32)
    return pl.pallas_call(
        functools.partial(product_kernel, row_block(rows), counts),
        in_specs=[SMEM] + [VMEM] * (1 + len(flat)),
        out_specs=[VMEM] * len(groups),
        out_shape=[jax.ShapeDtypeStruct((rows, lanes), jnp.float32)] * len(groups),
        scratch_shapes=[pltpu.VMEM((cols, lanes), jnp.bfloat16)],
        compiler_params=params(),
        cost_estimate=cost(8 * rows * cols * lanes * len(groups), 4 * rows * lanes),
        name="products",
    )(picks, tile, *flat)


def extra_kernel(counts, pick_ref, rows_ref, *refs):
    out_ref, right_ref = refs[-2:]
    used = 0
    for place, count in enumerate(counts):
        choose(right_ref, pick_ref[2 * place], refs[used:used + count])
        used += count
        out_ref[pick_ref[2 * place + 1]] = complex_rows(rows_ref[0], rows_ref[1], right_ref[...])


def extra_products(rows, groups):
    _, misses, cols = rows.shape
    lanes = groups[0][2][0].shape[1]
    counts = tuple(len(sources) for _, _, sources in groups)
    flat = [source for _, _, sources in groups for source in sources]
    picks = jnp.stack([x for pick, place, _ in groups for x in (pick, place)]).astype(jnp.int32)
    return pl.pallas_call(
        functools.partial(extra_kernel, counts),
        in_specs=[SMEM] + [VMEM] * (1 + len(flat)),
        out_specs=VMEM,
        out_shape=jax.ShapeDtypeStruct((len(groups), misses, lanes), jnp.float32),
        scratch_shapes=[pltpu.VMEM((cols, lanes), jnp.bfloat16)],
        compiler_params=params(),
        cost_estimate=cost(8 * misses * cols * lanes * len(groups), 4 * cols * lanes),
        name="extra_products",
    )(picks, rows, *flat)


def finish_kernel(counts, wave_ref, flag_ref, miss_ref, tile_ref, extra_ref, *refs):
    out_ref, row_ref = refs[-2:]
    totals = []
    used = 0
    for count in counts:
        total = refs[used][...]
        if count > 1:
            total = total * flag_ref[0]
        for ref in refs[used + 1:used + count]:
            total = total + ref[...]
        used += count
        totals.append(total)

    def write(target, window_ref, chunks):
        real_part, imag_part = unpack(chunks)
        real_pred = real_part * wave_ref[0] - imag_part * wave_ref[1]
        imag_pred = imag_part * wave_ref[0] + real_part * wave_ref[1]
        target[0] = window_ref[0].astype(jnp.float32) - real_pred
        target[1] = window_ref[1].astype(jnp.float32) - imag_pred

    write(out_ref, tile_ref, totals[:CHUNKS])
    write(row_ref, extra_ref, totals[CHUNKS:])

    def place(m, carry):
        for part in range(2):
            out_ref[part, pl.ds(miss_ref[m], 1), :] = row_ref[part, pl.ds(m, 1), :]
        return carry

    lax.fori_loop(0, row_ref.shape[1], place, 0, unroll=8)


def finish(wave, flag, miss, tile, extra, terms):
    _, rows, _ = tile.shape
    misses = extra.shape[1]
    counts = tuple(len(group) for group in terms)
    flat = [term for group in terms for term in group]
    window = lambda size: pl.BlockSpec((2, size, WIN), lambda i: (0, 0, 0))
    return pl.pallas_call(
        functools.partial(finish_kernel, counts),
        grid=(1,),
        in_specs=[SMEM, SMEM, SMEM, window(rows), window(misses)] + [VMEM] * len(flat),
        out_specs=window(rows),
        out_shape=jax.ShapeDtypeStruct((2, rows, WIN), jnp.float32),
        scratch_shapes=[pltpu.VMEM((2, misses, WIN), jnp.float32)],
        compiler_params=params(),
        cost_estimate=cost(20 * rows * WIN, 40 * rows * WIN),
        name="finish",
    )(wave, flag, miss, tile, extra, *flat)


def mirror_routes(grid_size):
    cells = [(a, b) for a in range(grid_size) for b in range(grid_size)]
    index = lambda row, col: row * grid_size + col
    whole = [(index(a, b), index(b, a)) for a, b in cells]
    near = [(index(a, b), index(b, a)) for a, b in cells if a // 2 == b // 2]
    far = [(a, b) for a, b in cells if a // 2 != b // 2]
    hop = lambda a, b: index(b, b // 2 * 2 + a % 2)
    first = [(index(a, b), hop(a, b)) for a, b in far]
    second = [(hop(a, b), index(b, a)) for a, b in far]
    if len({target for _, target in first}) < len(first):
        return whole, None
    return whole, (near, first, second)


def sources_of(up, down, offset, grid_size, row_index):
    places, sources = [], []
    for row in range(grid_size):
        other = row ^ offset
        source = up[row - other] if other < row else down[other - row]
        known = [index for index, seen in enumerate(sources) if seen is source]
        places.append(known[0] if known else len(sources))
        if not known:
            sources.append(source)
    pick = jnp.zeros((), jnp.int32)
    for row, place in enumerate(places):
        pick = jnp.where(row_index == row, place, pick)
    return pick, sources


def sum_route(offset, grid_size, stride, skip):
    route = []
    for row in range(grid_size):
        for col in range(grid_size):
            if ((col ^ row ^ offset) & ~skip) % (2 * stride) == stride:
                route.append((row * grid_size + col, row * grid_size + (col ^ stride)))
    return route


def local(traces, recv_live, missing, wavelet):
    tile = traces.shape[1]
    grid_size = lax.axis_size("row")
    misses = missing.shape[1]
    order = recv_live.shape[0]
    row_index = lax.axis_index("row")
    col_index = lax.axis_index("col")
    whole, hops = mirror_routes(grid_size)

    def move(block, route):
        return lax.ppermute(block, ("row", "col"), route)

    def transpose(block):
        return move(block, whole)

    def transpose_round(block):
        if hops is None:
            return [move(block, whole)]
        near, first, second = hops
        return [move(move(block, first), second), move(block, near)]

    direct, round_about = cut_window(traces)
    arrived = [[transpose(direct)], transpose_round(round_about)]
    if CHUNKS == 1:
        arrived = [arrived]
    else:
        arrived = [arrived[:1], arrived[1:]]

    miss_row = lax.dynamic_index_in_dim(missing, row_index, 0, keepdims=False)
    miss_col = lax.dynamic_index_in_dim(missing, col_index, 0, keepdims=False)
    as_lanes = lambda m: jnp.pad(m, (0, LANES - misses), constant_values=-1)[None]
    miss_col_lanes = as_lanes(miss_col)
    positions = jnp.arange(tile, dtype=jnp.int32)
    live_row = jnp.all(positions[:, None] != miss_row[None, :], axis=1)
    live8 = jnp.broadcast_to(live_row.astype(jnp.float32)[None], (8, tile))
    recv_mask = (recv_live == 1).astype(jnp.bfloat16)
    recv_row = lax.dynamic_slice_in_dim(recv_mask, row_index * tile, WIN)
    recv_row8 = jnp.broadcast_to(recv_row[None], (8, WIN))
    recv_col = lax.dynamic_slice_in_dim(recv_mask, col_index * tile, tile)
    recv_col8 = jnp.broadcast_to(recv_col[None], (8, tile))

    picked, tile_masked = pick_columns(traces, miss_col_lanes, recv_col8, live8, misses)
    extra = transpose(picked)
    apart = row_index ^ col_index
    strides = [2**bit for bit in range(grid_size.bit_length() - 1)]
    terms, extra_terms = [], []
    for chunk in range(CHUNKS):
        window = fill_window(chunk, arrived[chunk], picked, miss_col_lanes, recv_row8)
        up, down = [window], [window]
        sums = []

        def hop(distance):
            ends = [(i, i + 1) for i in range(distance - 1, grid_size - 1)]
            back = [(i + 1, i) for i in range(grid_size - distance)]
            up.append(lax.ppermute(up[-1], "row", ends))
            down.append(lax.ppermute(down[-1], "row", back))

        def add_up(total, offset, strides, skip):
            for stride in strides:
                total = total + move(total, sum_route(offset, grid_size, stride, skip))
            return total

        def last(total, offset, skip):
            return move(total, sum_route(offset, grid_size, strides[-1], skip))

        def options(offset):
            return sources_of(up, down, offset, grid_size, row_index)

        hop(1)
        hop(2)
        _, (block0,) = options(0)
        pick1, sources1 = options(1)
        odd = apart & 1
        everything = [block0] + sources1
        keep, sent = products(
            tile_masked,
            [
                (jnp.where(odd == 1, 1 + pick1, 0), everything),
                (jnp.where(odd == 1, 0, 1 + pick1), everything),
            ],
        )
        other_core = [(i, i ^ 1) for i in range(grid_size)]
        total = add_up(keep + lax.ppermute(sent, "col", other_core), 0, strides[1:-1], 1)
        up[-1], down[-1], total = lax.optimization_barrier((up[-1], down[-1], total))
        for distance in range(3, grid_size):
            hop(distance)
        got = last(total, 0, 1)
        tile, extra = lax.optimization_barrier((tile_masked, extra))
        early = None
        for offset in range(2, grid_size):
            mine = apart // 2 == 0 if offset == 2 else apart == offset - 1
            (new,) = products(tile, [options(offset)])
            new = add_up(new, offset, strides[:-1], 0)
            if offset < grid_size - 1:
                tile, got, new = lax.optimization_barrier((tile, got, new))
            term = jnp.where(mine, total, 0.0) + got
            early = term if early is None else early + term
            total, got = new, last(new, offset, 0)
        terms.append((total, early, got))
        group = [(pick, apart ^ offset, sources) for offset in range(grid_size)
                 for pick, sources in [options(offset)]]
        rest = extra_products(extra, group)
        for stride in strides:
            pairs = [(i, i ^ stride) for i in range(grid_size)]
            arrive = lax.ppermute(rest[1::2], "col", pairs)
            rest = rest[0::2] + arrive
        extra_terms.append((rest[0],))
    wave = wavelet * (1.0 / math.sqrt(order))
    flag = (apart == grid_size - 1).astype(jnp.float32)[None]
    return finish(wave, flag, miss_row, tile_masked, extra, terms + extra_terms)


def solution(mesh):
    in_specs = (P("freq", "row", "col"), P("freq"), P("freq", None), P("freq"))
    out_specs = P("freq", "row", "col")
    return jax.shard_map(local, mesh=mesh, in_specs=in_specs, out_specs=out_specs, check_vma=False)
```

```python
import functools
import math

import jax
import jax.numpy as jnp
from jax import lax
from jax.experimental import pallas as pl
from jax.experimental.pallas import tpu as pltpu
from jax.sharding import PartitionSpec as P

WIN = 128
LANES = 128
CHUNKS = 1
WIDTH = WIN // CHUNKS
VMEM_LIMIT = 48 * 2**20
VMEM = pl.BlockSpec(memory_space=pltpu.VMEM)
SMEM = pl.BlockSpec(memory_space=pltpu.SMEM)


def params():
    return pltpu.CompilerParams(vmem_limit_bytes=VMEM_LIMIT)


def cost(flops, accessed):
    return pl.CostEstimate(
        flops=int(flops) // 64, bytes_accessed=int(accessed) // 64, transcendentals=0
    )


def row_block(rows):
    for size in (512, 384, 256, 128):
        if rows % size == 0:
            return size
    return rows


def one_hot(positions_row, rows, dtype):
    lanes = positions_row.shape[1]
    row_ids = lax.broadcasted_iota(jnp.int32, (rows, lanes), 0)
    return jnp.where(row_ids == positions_row, 1.0, 0.0).astype(dtype)


def pack(real_part, imag_part):
    if CHUNKS == 1:
        return [jnp.concatenate([real_part, imag_part], axis=1)]
    first = lax.broadcasted_iota(jnp.int32, real_part.shape, 1) < WIDTH
    low = jnp.where(first, real_part, pltpu.roll(imag_part, WIDTH, 1))
    high = jnp.where(first, pltpu.roll(real_part, WIDTH, 1), imag_part)
    return [low, high]


def unpack(chunks):
    if CHUNKS == 1:
        return chunks[0][:, :WIN], chunks[0][:, WIN:]
    low, high = chunks
    first = lax.broadcasted_iota(jnp.int32, low.shape, 1) < WIDTH
    real_part = jnp.where(first, low, pltpu.roll(high, WIDTH, 1))
    imag_part = jnp.where(first, pltpu.roll(low, WIDTH, 1), high)
    return real_part, imag_part


def halves(real_part, imag_part):
    return [real_part, imag_part] if CHUNKS == 1 else pack(real_part, imag_part)


def cut_kernel(traces_ref, *out_refs):
    parts = halves(traces_ref[0].astype(jnp.float32), traces_ref[1].astype(jnp.float32))
    for out_ref, part in zip(out_refs, parts):
        out_ref[...] = part.astype(jnp.bfloat16)


def cut_window(traces):
    rows = traces.shape[1]
    return pl.pallas_call(
        cut_kernel,
        grid=(1,),
        in_specs=[pl.BlockSpec((2, rows, WIN), lambda i: (0, 0, 0))],
        out_specs=[pl.BlockSpec((rows, WIN), lambda i: (0, 0))] * 2,
        out_shape=[jax.ShapeDtypeStruct((rows, WIN), jnp.bfloat16)] * 2,
        compiler_params=params(),
        cost_estimate=cost(rows * WIN, 8 * rows * WIN),
        name="cut_window",
    )(traces)


def pick_kernel(traces_ref, miss_ref, recv_ref, live_ref, real_ref, imag_ref, hot_ref):
    @pl.when(pl.program_id(0) == 0)
    def _():
        hot = one_hot(miss_ref[...], hot_ref.shape[0], jnp.bfloat16)
        alive = jnp.dot(recv_ref[...], hot, preferred_element_type=jnp.float32)
        hot_ref[...] = hot * alive[0:1].astype(jnp.bfloat16)

    misses = real_ref.shape[0]
    for part, out_ref in enumerate((real_ref, imag_ref)):
        picked = jnp.dot(traces_ref[part], hot_ref[...], preferred_element_type=jnp.float32)
        turned = picked.T * live_ref[0:1, :]
        out_ref[...] = turned[:misses].astype(jnp.bfloat16)


def pick_columns(traces, miss_lanes, recv8, live8, misses):
    _, rows, cols = traces.shape
    block = row_block(rows)
    return pl.pallas_call(
        pick_kernel,
        grid=(rows // block,),
        in_specs=[
            pl.BlockSpec((2, block, cols), lambda i: (0, i, 0)),
            pl.BlockSpec((1, LANES), lambda i: (0, 0)),
            pl.BlockSpec((8, cols), lambda i: (0, 0)),
            pl.BlockSpec((8, block), lambda i: (0, i)),
        ],
        out_specs=[pl.BlockSpec((misses, block), lambda i: (0, i))] * 2,
        out_shape=[jax.ShapeDtypeStruct((misses, rows), jnp.bfloat16)] * 2,
        scratch_shapes=[pltpu.VMEM((cols, LANES), jnp.bfloat16)],
        compiler_params=params(),
        cost_estimate=cost(4 * rows * cols * 2 * LANES, 4 * rows * cols),
        name="pick_columns",
    )(traces, miss_lanes, recv8, live8)


def fill_kernel(counts, first_half, real_ref, imag_ref, miss_ref, recv_ref, *refs):
    out_ref = refs[-1]
    rows = out_ref.shape[0]
    misses = real_ref.shape[0]
    hot = one_hot(miss_ref[...], rows, jnp.float32)
    dead = jnp.max(hot, axis=1, keepdims=True)
    hot = hot[:, :misses].astype(jnp.bfloat16)
    patches = halves(real_ref[...].astype(jnp.float32), imag_ref[...].astype(jnp.float32))
    mask = recv_ref[...].astype(jnp.float32)
    mask = halves(mask, mask)[0][0:1, :]
    used = 0
    for index, count in enumerate(counts):
        arrived = refs[used][...].astype(jnp.float32)
        for more in refs[used + 1:used + count]:
            arrived = arrived + more[...].astype(jnp.float32)
        used += count
        patch = patches[first_half + index].astype(jnp.bfloat16)
        moved = jnp.dot(hot, patch, preferred_element_type=jnp.float32)
        filled = arrived * ((1.0 - dead) * mask) + moved
        out_ref[:, index * WIN:(index + 1) * WIN] = filled.astype(jnp.bfloat16)


def fill_window(first_half, arrived, picked, miss_lanes, recv8):
    rows = arrived[0][0].shape[0]
    misses = picked[0].shape[0]
    counts = tuple(len(group) for group in arrived)
    flat = [part for group in arrived for part in group]
    lanes = len(counts) * WIN
    whole = pl.BlockSpec((rows, WIN), lambda i: (0, 0))
    return pl.pallas_call(
        functools.partial(fill_kernel, counts, first_half),
        grid=(1,),
        in_specs=[
            pl.BlockSpec((misses, WIN), lambda i: (0, 0)),
            pl.BlockSpec((misses, WIN), lambda i: (0, 0)),
            pl.BlockSpec((1, LANES), lambda i: (0, 0)),
            pl.BlockSpec((8, WIN), lambda i: (0, 0)),
        ]
        + [whole] * len(flat),
        out_specs=pl.BlockSpec((rows, lanes), lambda i: (0, 0)),
        out_shape=jax.ShapeDtypeStruct((rows, lanes), jnp.bfloat16),
        compiler_params=params(),
        cost_estimate=cost(4 * rows * LANES * lanes, 8 * rows * lanes),
        name="fill_window",
    )(*picked, miss_lanes, recv8, *flat)


def complex_rows(real_rows, imag_rows, right):
    first = jnp.dot(real_rows, right, preferred_element_type=jnp.float32)
    second = jnp.dot(imag_rows, right, preferred_element_type=jnp.float32)
    if CHUNKS == 1:
        real_part = first[:, :WIN] - second[:, WIN:]
        imag_part = first[:, WIN:] + second[:, :WIN]
        return jnp.concatenate([real_part, imag_part], axis=1)
    turned = pltpu.roll(second, WIDTH, 1)
    low = lax.broadcasted_iota(jnp.int32, first.shape, 1) < WIDTH
    return first + jnp.where(low, -turned, turned)


def choose(out_ref, pick, refs):
    for index, ref in enumerate(refs):

        @pl.when(pick == index)
        def _():
            out_ref[...] = ref[...]


def product_kernel(counts, pick_ref, traces_ref, recv_ref, *refs):
    total, places = sum(counts), len(counts)
    out_refs, right_refs = refs[total:total + places], refs[total + places:]

    @pl.when(pl.program_id(0) == 0)
    def _():
        used = 0
        for place, count in enumerate(counts):
            choose(right_refs[place], pick_ref[place], refs[used:used + count])
            used += count

    recv = recv_ref[0:1, :]
    real_rows, imag_rows = traces_ref[0] * recv, traces_ref[1] * recv
    for out_ref, right_ref in zip(out_refs, right_refs):
        out_ref[...] = complex_rows(real_rows, imag_rows, right_ref[...])


def products(traces, recv8, groups):
    _, rows, cols = traces.shape
    lanes = groups[0][1][0].shape[1]
    counts = tuple(len(sources) for _, sources in groups)
    flat = [source for _, sources in groups for source in sources]
    picks = jnp.stack([pick for pick, _ in groups]).astype(jnp.int32)
    block = row_block(rows) // 2
    return pl.pallas_call(
        functools.partial(product_kernel, counts),
        grid=(rows // block,),
        in_specs=[
            SMEM,
            pl.BlockSpec((2, block, cols), lambda i: (0, i, 0)),
            pl.BlockSpec((8, cols), lambda i: (0, 0)),
        ]
        + [pl.BlockSpec((cols, lanes), lambda i: (0, 0))] * len(flat),
        out_specs=[pl.BlockSpec((block, lanes), lambda i: (i, 0))] * len(groups),
        out_shape=[jax.ShapeDtypeStruct((rows, lanes), jnp.float32)] * len(groups),
        scratch_shapes=[pltpu.VMEM((cols, lanes), jnp.bfloat16)] * len(groups),
        compiler_params=params(),
        cost_estimate=cost(8 * rows * cols * lanes * len(groups), 4 * rows * lanes),
        name="products",
    )(picks, traces, recv8, *flat)


def extra_kernel(counts, pick_ref, real_ref, imag_ref, *refs):
    out_ref, right_ref = refs[-2:]
    used = 0
    for place, count in enumerate(counts):
        choose(right_ref, pick_ref[2 * place], refs[used:used + count])
        used += count
        out_ref[pick_ref[2 * place + 1]] = complex_rows(real_ref[...], imag_ref[...], right_ref[...])


def extra_products(rows, groups):
    misses, cols = rows[0].shape
    lanes = groups[0][2][0].shape[1]
    counts = tuple(len(sources) for _, _, sources in groups)
    flat = [source for _, _, sources in groups for source in sources]
    picks = jnp.stack([x for pick, place, _ in groups for x in (pick, place)]).astype(jnp.int32)
    return pl.pallas_call(
        functools.partial(extra_kernel, counts),
        in_specs=[SMEM] + [VMEM] * (2 + len(flat)),
        out_specs=VMEM,
        out_shape=jax.ShapeDtypeStruct((len(groups), misses, lanes), jnp.float32),
        scratch_shapes=[pltpu.VMEM((cols, lanes), jnp.bfloat16)],
        compiler_params=params(),
        cost_estimate=cost(8 * misses * cols * lanes * len(groups), 4 * cols * lanes),
        name="extra_products",
    )(picks, *rows, *flat)


def finish_kernel(counts, wave_ref, flag_ref, miss_ref, recv_ref, tile_ref, real_ref, imag_ref, *refs):
    out_ref, row_ref = refs[-2:]
    totals = []
    used = 0
    for count in counts:
        total = refs[used][...]
        if count > 1:
            total = total * flag_ref[0]
        for ref in refs[used + 1:used + count]:
            total = total + ref[...]
        used += count
        totals.append(total)

    def write(target, window, chunks):
        real_part, imag_part = unpack(chunks)
        real_pred = real_part * wave_ref[0] - imag_part * wave_ref[1]
        imag_pred = imag_part * wave_ref[0] + real_part * wave_ref[1]
        target[0] = window[0] - real_pred
        target[1] = window[1] - imag_pred

    recv = recv_ref[0:1, :].astype(jnp.float32)
    write(out_ref, [tile_ref[part].astype(jnp.float32) * recv for part in range(2)], totals[:CHUNKS])
    write(row_ref, [ref[...].astype(jnp.float32) for ref in (real_ref, imag_ref)], totals[CHUNKS:])

    def place(m, carry):
        for part in range(2):
            out_ref[part, pl.ds(miss_ref[m], 1), :] = row_ref[part, pl.ds(m, 1), :]
        return carry

    lax.fori_loop(0, row_ref.shape[1], place, 0, unroll=8)


def finish(wave, flag, miss, recv8, traces, extra, terms):
    _, rows, _ = traces.shape
    misses = extra[0].shape[0]
    counts = tuple(len(group) for group in terms)
    flat = [term for group in terms for term in group]
    window = lambda size: pl.BlockSpec((2, size, WIN), lambda i: (0, 0, 0))
    return pl.pallas_call(
        functools.partial(finish_kernel, counts),
        grid=(1,),
        in_specs=[SMEM, SMEM, SMEM, pl.BlockSpec((8, WIN), lambda i: (0, 0)), window(rows)]
        + [pl.BlockSpec((misses, WIN), lambda i: (0, 0))] * 2
        + [VMEM] * len(flat),
        out_specs=window(rows),
        out_shape=jax.ShapeDtypeStruct((2, rows, WIN), jnp.float32),
        scratch_shapes=[pltpu.VMEM((2, misses, WIN), jnp.float32)],
        compiler_params=params(),
        cost_estimate=cost(20 * rows * WIN, 40 * rows * WIN),
        name="finish",
    )(wave, flag, miss, recv8, traces, *extra, *flat)


def mirror_routes(grid_size):
    cells = [(a, b) for a in range(grid_size) for b in range(grid_size)]
    index = lambda row, col: row * grid_size + col
    whole = [(index(a, b), index(b, a)) for a, b in cells]
    near = [(index(a, b), index(b, a)) for a, b in cells if a // 2 == b // 2]
    far = [(a, b) for a, b in cells if a // 2 != b // 2]
    hop = lambda a, b: index(a, a // 2 * 2 + b % 2)
    first = [(index(a, b), hop(a, b)) for a, b in far]
    second = [(hop(a, b), index(b, a)) for a, b in far]
    if len({target for _, target in first}) < len(first):
        return whole, None
    return whole, (near, first, second)


def sources_of(up, down, offset, grid_size, row_index):
    places, sources = [], []
    for row in range(grid_size):
        other = row ^ offset
        source = up[row - other] if other < row else down[other - row]
        known = [index for index, seen in enumerate(sources) if seen is source]
        places.append(known[0] if known else len(sources))
        if not known:
            sources.append(source)
    pick = jnp.zeros((), jnp.int32)
    for row, place in enumerate(places):
        pick = jnp.where(row_index == row, place, pick)
    return pick, sources


def sum_route(offset, grid_size, stride, skip):
    route = []
    for row in range(grid_size):
        for col in range(grid_size):
            if ((col ^ row ^ offset) & ~skip) % (2 * stride) == stride:
                route.append((row * grid_size + col, row * grid_size + (col ^ stride)))
    return route


def local(traces, recv_live, missing, wavelet):
    tile = traces.shape[1]
    grid_size = lax.axis_size("row")
    misses = missing.shape[1]
    order = recv_live.shape[0]
    row_index = lax.axis_index("row")
    col_index = lax.axis_index("col")
    whole, hops = mirror_routes(grid_size)

    def move(block, route):
        return lax.ppermute(block, ("row", "col"), route)

    def transpose(block):
        return move(block, whole)

    def transpose_round(block):
        if hops is None:
            return [move(block, whole)]
        near, first, second = hops
        return [move(move(block, first), second), move(block, near)]

    direct, round_about = cut_window(traces)
    arrived = [[transpose(direct)], transpose_round(round_about)]
    if CHUNKS == 1:
        arrived = [arrived]
    else:
        arrived = [arrived[:1], arrived[1:]]

    miss_row = lax.dynamic_index_in_dim(missing, row_index, 0, keepdims=False)
    miss_col = lax.dynamic_index_in_dim(missing, col_index, 0, keepdims=False)
    as_lanes = lambda m: jnp.pad(m, (0, LANES - misses), constant_values=-1)[None]
    miss_col_lanes = as_lanes(miss_col)
    positions = jnp.arange(tile, dtype=jnp.int32)
    live_row = jnp.all(positions[:, None] != miss_row[None, :], axis=1)
    live8 = jnp.broadcast_to(live_row.astype(jnp.float32)[None], (8, tile))
    recv_mask = (recv_live == 1).astype(jnp.bfloat16)
    recv_row = lax.dynamic_slice_in_dim(recv_mask, row_index * tile, WIN)
    recv_row8 = jnp.broadcast_to(recv_row[None], (8, WIN))
    recv_col = lax.dynamic_slice_in_dim(recv_mask, col_index * tile, tile)
    recv_col8 = jnp.broadcast_to(recv_col[None], (8, tile))

    picked = pick_columns(traces, miss_col_lanes, recv_col8, live8, misses)
    extra = [transpose(picked[0]), functools.reduce(jnp.add, transpose_round(picked[1]))]
    picked, extra = lax.optimization_barrier((picked, extra))
    apart = row_index ^ col_index
    strides = [2**bit for bit in range(grid_size.bit_length() - 1)]
    terms, extra_terms = [], []
    for chunk in range(CHUNKS):
        window = fill_window(chunk, arrived[chunk], picked, miss_col_lanes, recv_row8)
        up, down = [window], [window]
        sums = []

        def hop(distance):
            ends = [(i, i + 1) for i in range(distance - 1, grid_size - 1)]
            back = [(i + 1, i) for i in range(grid_size - distance)]
            up.append(lax.ppermute(up[-1], "row", ends))
            down.append(lax.ppermute(down[-1], "row", back))

        def add_up(total, offset, strides, skip):
            for stride in strides:
                total = total + move(total, sum_route(offset, grid_size, stride, skip))
            return total

        def last(total, offset, skip):
            return move(total, sum_route(offset, grid_size, strides[-1], skip))

        def options(offset):
            return sources_of(up, down, offset, grid_size, row_index)

        hop(1)
        hop(2)
        _, (block0,) = options(0)
        pick1, sources1 = options(1)
        odd = apart & 1
        everything = [block0] + sources1
        keep, sent = products(
            traces,
            recv_col8,
            [
                (jnp.where(odd == 1, 1 + pick1, 0), everything),
                (jnp.where(odd == 1, 0, 1 + pick1), everything),
            ],
        )
        other_core = [(i, i ^ 1) for i in range(grid_size)]
        total = add_up(keep + lax.ppermute(sent, "col", other_core), 0, strides[1:-1], 1)
        for distance in range(3, grid_size):
            hop(distance)
        sums = [(0, 1, apart // 2 == 0, total)]
        mask = recv_col8
        for offset in range(2, grid_size):
            if offset == grid_size - 1:
                totals = [total for *_, total in sums]
                mask, totals = lax.optimization_barrier((mask, totals))
                sums = [(*rest, total) for (*rest, _), total in zip(sums, totals)]
            (total,) = products(traces, mask, [options(offset)])
            total = add_up(total, offset, strides[:-1], 0)
            sums.append((offset, 0, apart == offset, total))
        early = None
        for offset, skip, mine, total in sums[:-1]:
            term = jnp.where(mine, total, 0.0) + last(total, offset, skip)
            early = term if early is None else early + term
        total = sums[-1][-1]
        terms.append((total, early, last(total, grid_size - 1, 0)))
        group = [(pick, apart ^ offset, sources) for offset in range(grid_size)
                 for pick, sources in [options(offset)]]
        rest = extra_products(extra, group)
        for stride in strides:
            pairs = [(i, i ^ stride) for i in range(grid_size)]
            arrive = lax.ppermute(rest[1::2], "col", pairs)
            rest = rest[0::2] + arrive
        extra_terms.append((rest[0],))
    wave = wavelet * (1.0 / math.sqrt(order))
    flag = (apart == grid_size - 1).astype(jnp.float32)[None]
    return finish(wave, flag, miss_row, recv_col8, traces, extra, terms + extra_terms)


def solution(mesh):
    in_specs = (P("freq", "row", "col"), P("freq"), P("freq", None), P("freq"))
    out_specs = P("freq", "row", "col")
    return jax.shard_map(local, mesh=mesh, in_specs=in_specs, out_specs=out_specs, check_vma=False)
```

```python
import functools
import math

import jax
import jax.numpy as jnp
from jax import lax
from jax.experimental import pallas as pl
from jax.experimental.pallas import tpu as pltpu
from jax.sharding import PartitionSpec as P

WIN = 128
LANES = 128
CHUNKS = 1
WIDTH = WIN // CHUNKS
VMEM_LIMIT = 48 * 2**20
VMEM = pl.BlockSpec(memory_space=pltpu.VMEM)
SMEM = pl.BlockSpec(memory_space=pltpu.SMEM)


def params():
    return pltpu.CompilerParams(vmem_limit_bytes=VMEM_LIMIT)


def cost(flops, accessed):
    return pl.CostEstimate(
        flops=int(flops) // 64, bytes_accessed=int(accessed) // 64, transcendentals=0
    )


def row_block(rows):
    for size in (512, 384, 256, 128):
        if rows % size == 0:
            return size
    return rows


def one_hot(positions_row, rows, dtype):
    lanes = positions_row.shape[1]
    row_ids = lax.broadcasted_iota(jnp.int32, (rows, lanes), 0)
    return jnp.where(row_ids == positions_row, 1.0, 0.0).astype(dtype)


def pack(real_part, imag_part):
    if CHUNKS == 1:
        return [jnp.concatenate([real_part, imag_part], axis=1)]
    first = lax.broadcasted_iota(jnp.int32, real_part.shape, 1) < WIDTH
    low = jnp.where(first, real_part, pltpu.roll(imag_part, WIDTH, 1))
    high = jnp.where(first, pltpu.roll(real_part, WIDTH, 1), imag_part)
    return [low, high]


def unpack(chunks):
    if CHUNKS == 1:
        return chunks[0][:, :WIN], chunks[0][:, WIN:]
    low, high = chunks
    first = lax.broadcasted_iota(jnp.int32, low.shape, 1) < WIDTH
    real_part = jnp.where(first, low, pltpu.roll(high, WIDTH, 1))
    imag_part = jnp.where(first, pltpu.roll(low, WIDTH, 1), high)
    return real_part, imag_part


def halves(real_part, imag_part):
    return [real_part, imag_part] if CHUNKS == 1 else pack(real_part, imag_part)


def cut_kernel(traces_ref, *out_refs):
    parts = halves(traces_ref[0].astype(jnp.float32), traces_ref[1].astype(jnp.float32))
    for out_ref, part in zip(out_refs, parts):
        out_ref[...] = part.astype(jnp.bfloat16)


def cut_window(traces):
    rows = traces.shape[1]
    return pl.pallas_call(
        cut_kernel,
        grid=(1,),
        in_specs=[pl.BlockSpec((2, rows, WIN), lambda i: (0, 0, 0))],
        out_specs=[pl.BlockSpec((rows, WIN), lambda i: (0, 0))] * 2,
        out_shape=[jax.ShapeDtypeStruct((rows, WIN), jnp.bfloat16)] * 2,
        compiler_params=params(),
        cost_estimate=cost(rows * WIN, 8 * rows * WIN),
        name="cut_window",
    )(traces)


def pick_kernel(traces_ref, miss_ref, recv_ref, live_ref, real_ref, imag_ref, hot_ref):
    @pl.when(pl.program_id(0) == 0)
    def _():
        hot = one_hot(miss_ref[...], hot_ref.shape[0], jnp.bfloat16)
        alive = jnp.dot(recv_ref[...], hot, preferred_element_type=jnp.float32)
        hot_ref[...] = hot * alive[0:1].astype(jnp.bfloat16)

    misses = real_ref.shape[0]
    for part, out_ref in enumerate((real_ref, imag_ref)):
        picked = jnp.dot(traces_ref[part], hot_ref[...], preferred_element_type=jnp.float32)
        turned = picked.T * live_ref[0:1, :]
        out_ref[...] = turned[:misses].astype(jnp.bfloat16)


def pick_columns(traces, miss_lanes, recv8, live8, misses):
    _, rows, cols = traces.shape
    block = row_block(rows)
    return pl.pallas_call(
        pick_kernel,
        grid=(rows // block,),
        in_specs=[
            pl.BlockSpec((2, block, cols), lambda i: (0, i, 0)),
            pl.BlockSpec((1, LANES), lambda i: (0, 0)),
            pl.BlockSpec((8, cols), lambda i: (0, 0)),
            pl.BlockSpec((8, block), lambda i: (0, i)),
        ],
        out_specs=[pl.BlockSpec((misses, block), lambda i: (0, i))] * 2,
        out_shape=[jax.ShapeDtypeStruct((misses, rows), jnp.bfloat16)] * 2,
        scratch_shapes=[pltpu.VMEM((cols, LANES), jnp.bfloat16)],
        compiler_params=params(),
        cost_estimate=cost(4 * rows * cols * 2 * LANES, 4 * rows * cols),
        name="pick_columns",
    )(traces, miss_lanes, recv8, live8)


def fill_kernel(counts, first_half, real_ref, imag_ref, miss_ref, recv_ref, *refs):
    out_ref = refs[-1]
    rows = out_ref.shape[0]
    misses = real_ref.shape[0]
    hot = one_hot(miss_ref[...], rows, jnp.float32)
    dead = jnp.max(hot, axis=1, keepdims=True)
    hot = hot[:, :misses].astype(jnp.bfloat16)
    patches = halves(real_ref[...].astype(jnp.float32), imag_ref[...].astype(jnp.float32))
    mask = recv_ref[...].astype(jnp.float32)
    mask = halves(mask, mask)[0][0:1, :]
    used = 0
    for index, count in enumerate(counts):
        arrived = refs[used][...].astype(jnp.float32)
        for more in refs[used + 1:used + count]:
            arrived = arrived + more[...].astype(jnp.float32)
        used += count
        patch = patches[first_half + index].astype(jnp.bfloat16)
        moved = jnp.dot(hot, patch, preferred_element_type=jnp.float32)
        filled = arrived * ((1.0 - dead) * mask) + moved
        out_ref[:, index * WIN:(index + 1) * WIN] = filled.astype(jnp.bfloat16)


def fill_window(first_half, arrived, picked, miss_lanes, recv8):
    rows = arrived[0][0].shape[0]
    misses = picked[0].shape[0]
    counts = tuple(len(group) for group in arrived)
    flat = [part for group in arrived for part in group]
    lanes = len(counts) * WIN
    whole = pl.BlockSpec((rows, WIN), lambda i: (0, 0))
    return pl.pallas_call(
        functools.partial(fill_kernel, counts, first_half),
        grid=(1,),
        in_specs=[
            pl.BlockSpec((misses, WIN), lambda i: (0, 0)),
            pl.BlockSpec((misses, WIN), lambda i: (0, 0)),
            pl.BlockSpec((1, LANES), lambda i: (0, 0)),
            pl.BlockSpec((8, WIN), lambda i: (0, 0)),
        ]
        + [whole] * len(flat),
        out_specs=pl.BlockSpec((rows, lanes), lambda i: (0, 0)),
        out_shape=jax.ShapeDtypeStruct((rows, lanes), jnp.bfloat16),
        compiler_params=params(),
        cost_estimate=cost(4 * rows * LANES * lanes, 8 * rows * lanes),
        name="fill_window",
    )(*picked, miss_lanes, recv8, *flat)


def complex_rows(real_rows, imag_rows, right):
    first = jnp.dot(real_rows, right, preferred_element_type=jnp.float32)
    second = jnp.dot(imag_rows, right, preferred_element_type=jnp.float32)
    if CHUNKS == 1:
        real_part = first[:, :WIN] - second[:, WIN:]
        imag_part = first[:, WIN:] + second[:, :WIN]
        return jnp.concatenate([real_part, imag_part], axis=1)
    turned = pltpu.roll(second, WIDTH, 1)
    low = lax.broadcasted_iota(jnp.int32, first.shape, 1) < WIDTH
    return first + jnp.where(low, -turned, turned)


def choose(out_ref, pick, refs):
    for index, ref in enumerate(refs):

        @pl.when(pick == index)
        def _():
            out_ref[...] = ref[...]


def product_kernel(counts, pick_ref, recv_ref, *refs):
    tiles, refs = refs[:4], refs[4:]
    total, places = sum(counts), len(counts)
    out_refs, right_refs = refs[total:total + places], refs[total + places:]

    @pl.when(pl.program_id(0) == 0)
    def _():
        used = 0
        for place, count in enumerate(counts):
            choose(right_refs[place], pick_ref[place], refs[used:used + count])
            used += count

    recv = recv_ref[0:1, :]
    half = tiles[0].shape[1]
    for side in range(2):
        real_rows, imag_rows = (tiles[2 * part + side][0] * recv for part in range(2))
        for out_ref, right_ref in zip(out_refs, right_refs):
            out_ref[side * half:(side + 1) * half, :] = complex_rows(
                real_rows, imag_rows, right_ref[...]
            )


def products(traces, recv8, groups):
    _, rows, cols = traces.shape
    lanes = groups[0][1][0].shape[1]
    counts = tuple(len(sources) for _, sources in groups)
    flat = [source for _, sources in groups for source in sources]
    picks = jnp.stack([pick for pick, _ in groups]).astype(jnp.int32)
    block = row_block(rows)
    quarter = lambda part, side: pl.BlockSpec(
        (1, block // 2, cols), lambda i: (part, 2 * i + side, 0)
    )
    return pl.pallas_call(
        functools.partial(product_kernel, counts),
        grid=(rows // block,),
        in_specs=[
            SMEM,
            pl.BlockSpec((8, cols), lambda i: (0, 0)),
        ]
        + [quarter(part, side) for part in range(2) for side in range(2)]
        + [pl.BlockSpec((cols, lanes), lambda i: (0, 0))] * len(flat),
        out_specs=[pl.BlockSpec((block, lanes), lambda i: (i, 0))] * len(groups),
        out_shape=[jax.ShapeDtypeStruct((rows, lanes), jnp.float32)] * len(groups),
        scratch_shapes=[pltpu.VMEM((cols, lanes), jnp.bfloat16)] * len(groups),
        compiler_params=params(),
        cost_estimate=cost(8 * rows * cols * lanes * len(groups), 4 * rows * lanes),
        name="products",
    )(picks, recv8, *[traces] * 4, *flat)


def extra_kernel(counts, pick_ref, real_ref, imag_ref, *refs):
    out_ref, right_ref = refs[-2:]
    used = 0
    for place, count in enumerate(counts):
        choose(right_ref, pick_ref[2 * place], refs[used:used + count])
        used += count
        out_ref[pick_ref[2 * place + 1]] = complex_rows(real_ref[...], imag_ref[...], right_ref[...])


def extra_products(rows, groups):
    misses, cols = rows[0].shape
    lanes = groups[0][2][0].shape[1]
    counts = tuple(len(sources) for _, _, sources in groups)
    flat = [source for _, _, sources in groups for source in sources]
    picks = jnp.stack([x for pick, place, _ in groups for x in (pick, place)]).astype(jnp.int32)
    return pl.pallas_call(
        functools.partial(extra_kernel, counts),
        in_specs=[SMEM] + [VMEM] * (2 + len(flat)),
        out_specs=VMEM,
        out_shape=jax.ShapeDtypeStruct((len(groups), misses, lanes), jnp.float32),
        scratch_shapes=[pltpu.VMEM((cols, lanes), jnp.bfloat16)],
        compiler_params=params(),
        cost_estimate=cost(8 * misses * cols * lanes * len(groups), 4 * cols * lanes),
        name="extra_products",
    )(picks, *rows, *flat)


def finish_kernel(counts, wave_ref, flag_ref, miss_ref, recv_ref, tile_ref, real_ref, imag_ref, *refs):
    out_ref, row_ref = refs[-2:]
    totals = []
    used = 0
    for count in counts:
        total = refs[used][...]
        if count > 1:
            total = total * flag_ref[0]
        for ref in refs[used + 1:used + count]:
            total = total + ref[...]
        used += count
        totals.append(total)

    def write(target, window, chunks):
        real_part, imag_part = unpack(chunks)
        real_pred = real_part * wave_ref[0] - imag_part * wave_ref[1]
        imag_pred = imag_part * wave_ref[0] + real_part * wave_ref[1]
        target[0] = window[0] - real_pred
        target[1] = window[1] - imag_pred

    recv = recv_ref[0:1, :].astype(jnp.float32)
    write(out_ref, [tile_ref[part].astype(jnp.float32) * recv for part in range(2)], totals[:CHUNKS])
    write(row_ref, [ref[...].astype(jnp.float32) for ref in (real_ref, imag_ref)], totals[CHUNKS:])

    def place(m, carry):
        for part in range(2):
            out_ref[part, pl.ds(miss_ref[m], 1), :] = row_ref[part, pl.ds(m, 1), :]
        return carry

    lax.fori_loop(0, row_ref.shape[1], place, 0, unroll=8)


def finish(wave, flag, miss, recv8, traces, extra, terms):
    _, rows, _ = traces.shape
    misses = extra[0].shape[0]
    counts = tuple(len(group) for group in terms)
    flat = [term for group in terms for term in group]
    window = lambda size: pl.BlockSpec((2, size, WIN), lambda i: (0, 0, 0))
    return pl.pallas_call(
        functools.partial(finish_kernel, counts),
        grid=(1,),
        in_specs=[SMEM, SMEM, SMEM, pl.BlockSpec((8, WIN), lambda i: (0, 0)), window(rows)]
        + [pl.BlockSpec((misses, WIN), lambda i: (0, 0))] * 2
        + [VMEM] * len(flat),
        out_specs=window(rows),
        out_shape=jax.ShapeDtypeStruct((2, rows, WIN), jnp.float32),
        scratch_shapes=[pltpu.VMEM((2, misses, WIN), jnp.float32)],
        compiler_params=params(),
        cost_estimate=cost(20 * rows * WIN, 40 * rows * WIN),
        name="finish",
    )(wave, flag, miss, recv8, traces, *extra, *flat)


def mirror_routes(grid_size):
    cells = [(a, b) for a in range(grid_size) for b in range(grid_size)]
    index = lambda row, col: row * grid_size + col
    whole = [(index(a, b), index(b, a)) for a, b in cells]
    near = [(index(a, b), index(b, a)) for a, b in cells if a // 2 == b // 2]
    far = [(a, b) for a, b in cells if a // 2 != b // 2]
    hop = lambda a, b: index(a, a // 2 * 2 + b % 2)
    first = [(index(a, b), hop(a, b)) for a, b in far]
    second = [(hop(a, b), index(b, a)) for a, b in far]
    if len({target for _, target in first}) < len(first):
        return whole, None
    return whole, (near, first, second)


def sources_of(up, down, offset, grid_size, row_index):
    places, sources = [], []
    for row in range(grid_size):
        other = row ^ offset
        source = up[row - other] if other < row else down[other - row]
        known = [index for index, seen in enumerate(sources) if seen is source]
        places.append(known[0] if known else len(sources))
        if not known:
            sources.append(source)
    pick = jnp.zeros((), jnp.int32)
    for row, place in enumerate(places):
        pick = jnp.where(row_index == row, place, pick)
    return pick, sources


def sum_route(offset, grid_size, stride, skip):
    route = []
    for row in range(grid_size):
        for col in range(grid_size):
            if ((col ^ row ^ offset) & ~skip) % (2 * stride) == stride:
                route.append((row * grid_size + col, row * grid_size + (col ^ stride)))
    return route


def local(traces, recv_live, missing, wavelet):
    tile = traces.shape[1]
    grid_size = lax.axis_size("row")
    misses = missing.shape[1]
    order = recv_live.shape[0]
    row_index = lax.axis_index("row")
    col_index = lax.axis_index("col")
    whole, hops = mirror_routes(grid_size)

    def move(block, route):
        return lax.ppermute(block, ("row", "col"), route)

    def transpose(block):
        return move(block, whole)

    def transpose_round(block):
        if hops is None:
            return [move(block, whole)]
        near, first, second = hops
        return [move(move(block, first), second), move(block, near)]

    direct, round_about = cut_window(traces)
    arrived = [[transpose(direct)], transpose_round(round_about)]
    if CHUNKS == 1:
        arrived = [arrived]
    else:
        arrived = [arrived[:1], arrived[1:]]

    miss_row = lax.dynamic_index_in_dim(missing, row_index, 0, keepdims=False)
    miss_col = lax.dynamic_index_in_dim(missing, col_index, 0, keepdims=False)
    as_lanes = lambda m: jnp.pad(m, (0, LANES - misses), constant_values=-1)[None]
    miss_col_lanes = as_lanes(miss_col)
    positions = jnp.arange(tile, dtype=jnp.int32)
    live_row = jnp.all(positions[:, None] != miss_row[None, :], axis=1)
    live8 = jnp.broadcast_to(live_row.astype(jnp.float32)[None], (8, tile))
    recv_mask = (recv_live == 1).astype(jnp.bfloat16)
    recv_row = lax.dynamic_slice_in_dim(recv_mask, row_index * tile, WIN)
    recv_row8 = jnp.broadcast_to(recv_row[None], (8, WIN))
    recv_col = lax.dynamic_slice_in_dim(recv_mask, col_index * tile, tile)
    recv_col8 = jnp.broadcast_to(recv_col[None], (8, tile))

    picked = pick_columns(traces, miss_col_lanes, recv_col8, live8, misses)
    extra = transpose(jnp.concatenate(picked))
    extra = [extra[:misses], extra[misses:]]
    apart = row_index ^ col_index
    strides = [2**bit for bit in range(grid_size.bit_length() - 1)]
    terms, extra_terms = [], []
    for chunk in range(CHUNKS):
        window = fill_window(chunk, arrived[chunk], picked, miss_col_lanes, recv_row8)
        up, down = [window], [window]
        sums = []

        def hop(distance):
            ends = [(i, i + 1) for i in range(distance - 1, grid_size - 1)]
            back = [(i + 1, i) for i in range(grid_size - distance)]
            up.append(lax.ppermute(up[-1], "row", ends))
            down.append(lax.ppermute(down[-1], "row", back))

        def add_up(total, offset, strides, skip):
            for stride in strides:
                total = total + move(total, sum_route(offset, grid_size, stride, skip))
            return total

        def last(total, offset, skip):
            return move(total, sum_route(offset, grid_size, strides[-1], skip))

        def options(offset):
            return sources_of(up, down, offset, grid_size, row_index)

        hop(1)
        hop(2)
        _, (block0,) = options(0)
        pick1, sources1 = options(1)
        odd = apart & 1
        everything = [block0] + sources1
        keep, sent = products(
            traces,
            recv_col8,
            [
                (jnp.where(odd == 1, 1 + pick1, 0), everything),
                (jnp.where(odd == 1, 0, 1 + pick1), everything),
            ],
        )
        other_core = [(i, i ^ 1) for i in range(grid_size)]
        total = add_up(keep + lax.ppermute(sent, "col", other_core), 0, strides[1:-1], 1)
        for distance in range(3, grid_size):
            hop(distance)
        sums = [(0, 1, apart // 2 == 0, total)]
        mask = recv_col8
        for offset in range(2, grid_size):
            if offset == grid_size - 1:
                *rest, total = sums[0]
                mask, total, extra = lax.optimization_barrier((mask, total, extra))
                sums[0] = (*rest, total)
            (total,) = products(traces, mask, [options(offset)])
            total = add_up(total, offset, strides[:-1], 0)
            sums.append((offset, 0, apart == offset, total))
        early = None
        for offset, skip, mine, total in sums[:-1]:
            term = jnp.where(mine, total, 0.0) + last(total, offset, skip)
            early = term if early is None else early + term
        total = sums[-1][-1]
        terms.append((total, early, last(total, grid_size - 1, 0)))
        group = [(pick, apart ^ offset, sources) for offset in range(grid_size)
                 for pick, sources in [options(offset)]]
        rest = extra_products(extra, group)
        for stride in strides:
            pairs = [(i, i ^ stride) for i in range(grid_size)]
            arrive = lax.ppermute(rest[1::2], "col", pairs)
            rest = rest[0::2] + arrive
        extra_terms.append((rest[0],))
    wave = wavelet * (1.0 / math.sqrt(order))
    flag = (apart == grid_size - 1).astype(jnp.float32)[None]
    return finish(wave, flag, miss_row, recv_col8, traces, extra, terms + extra_terms)


def solution(mesh):
    in_specs = (P("freq", "row", "col"), P("freq"), P("freq", None), P("freq"))
    out_specs = P("freq", "row", "col")
    return jax.shard_map(local, mesh=mesh, in_specs=in_specs, out_specs=out_specs, check_vma=False)
```

```python
import functools
import math

import jax
import jax.numpy as jnp
from jax import lax
from jax.experimental import pallas as pl
from jax.experimental.pallas import tpu as pltpu
from jax.sharding import PartitionSpec as P

WIN = 128
LANES = 128
CHUNKS = 1
WIDTH = WIN // CHUNKS
VMEM_LIMIT = 48 * 2**20
VMEM = pl.BlockSpec(memory_space=pltpu.VMEM)
SMEM = pl.BlockSpec(memory_space=pltpu.SMEM)


def params():
    return pltpu.CompilerParams(vmem_limit_bytes=VMEM_LIMIT)


def cost(flops, accessed):
    return pl.CostEstimate(
        flops=int(flops) // 64, bytes_accessed=int(accessed) // 64, transcendentals=0
    )


def row_block(rows):
    for size in (512, 384, 256, 128):
        if rows % size == 0:
            return size
    return rows


def one_hot(positions_row, rows, dtype):
    lanes = positions_row.shape[1]
    row_ids = lax.broadcasted_iota(jnp.int32, (rows, lanes), 0)
    return jnp.where(row_ids == positions_row, 1.0, 0.0).astype(dtype)


def pack(real_part, imag_part):
    if CHUNKS == 1:
        return [jnp.concatenate([real_part, imag_part], axis=1)]
    first = lax.broadcasted_iota(jnp.int32, real_part.shape, 1) < WIDTH
    low = jnp.where(first, real_part, pltpu.roll(imag_part, WIDTH, 1))
    high = jnp.where(first, pltpu.roll(real_part, WIDTH, 1), imag_part)
    return [low, high]


def unpack(chunks):
    if CHUNKS == 1:
        return chunks[0][:, :WIN], chunks[0][:, WIN:]
    low, high = chunks
    first = lax.broadcasted_iota(jnp.int32, low.shape, 1) < WIDTH
    real_part = jnp.where(first, low, pltpu.roll(high, WIDTH, 1))
    imag_part = jnp.where(first, pltpu.roll(low, WIDTH, 1), high)
    return real_part, imag_part


def halves(real_part, imag_part):
    return [real_part, imag_part] if CHUNKS == 1 else pack(real_part, imag_part)


def cut_kernel(traces_ref, *out_refs):
    parts = halves(traces_ref[0].astype(jnp.float32), traces_ref[1].astype(jnp.float32))
    for out_ref, part in zip(out_refs, parts):
        out_ref[...] = part.astype(jnp.bfloat16)


def cut_window(traces):
    rows = traces.shape[1]
    return pl.pallas_call(
        cut_kernel,
        grid=(1,),
        in_specs=[pl.BlockSpec((2, rows, WIN), lambda i: (0, 0, 0))],
        out_specs=[pl.BlockSpec((rows, WIN), lambda i: (0, 0))] * 2,
        out_shape=[jax.ShapeDtypeStruct((rows, WIN), jnp.bfloat16)] * 2,
        compiler_params=params(),
        cost_estimate=cost(rows * WIN, 8 * rows * WIN),
        name="cut_window",
    )(traces)


def pick_kernel(traces_ref, miss_ref, recv_ref, live_ref, real_ref, imag_ref, hot_ref):
    @pl.when(pl.program_id(0) == 0)
    def _():
        hot = one_hot(miss_ref[...], hot_ref.shape[0], jnp.bfloat16)
        alive = jnp.dot(recv_ref[...], hot, preferred_element_type=jnp.float32)
        hot_ref[...] = hot * alive[0:1].astype(jnp.bfloat16)

    misses = real_ref.shape[0]
    for part, out_ref in enumerate((real_ref, imag_ref)):
        picked = jnp.dot(traces_ref[part], hot_ref[...], preferred_element_type=jnp.float32)
        turned = picked.T * live_ref[0:1, :]
        out_ref[...] = turned[:misses].astype(jnp.bfloat16)


def pick_columns(traces, miss_lanes, recv8, live8, misses):
    _, rows, cols = traces.shape
    block = row_block(rows)
    return pl.pallas_call(
        pick_kernel,
        grid=(rows // block,),
        in_specs=[
            pl.BlockSpec((2, block, cols), lambda i: (0, i, 0)),
            pl.BlockSpec((1, LANES), lambda i: (0, 0)),
            pl.BlockSpec((8, cols), lambda i: (0, 0)),
            pl.BlockSpec((8, block), lambda i: (0, i)),
        ],
        out_specs=[pl.BlockSpec((misses, block), lambda i: (0, i))] * 2,
        out_shape=[jax.ShapeDtypeStruct((misses, rows), jnp.bfloat16)] * 2,
        scratch_shapes=[pltpu.VMEM((cols, LANES), jnp.bfloat16)],
        compiler_params=params(),
        cost_estimate=cost(4 * rows * cols * 2 * LANES, 4 * rows * cols),
        name="pick_columns",
    )(traces, miss_lanes, recv8, live8)


def fill_kernel(counts, first_half, real_ref, imag_ref, miss_ref, recv_ref, *refs):
    out_ref = refs[-1]
    rows = out_ref.shape[0]
    misses = real_ref.shape[0]
    hot = one_hot(miss_ref[...], rows, jnp.float32)
    dead = jnp.max(hot, axis=1, keepdims=True)
    hot = hot[:, :misses].astype(jnp.bfloat16)
    patches = halves(real_ref[...].astype(jnp.float32), imag_ref[...].astype(jnp.float32))
    mask = recv_ref[...].astype(jnp.float32)
    mask = halves(mask, mask)[0][0:1, :]
    used = 0
    for index, count in enumerate(counts):
        arrived = refs[used][...].astype(jnp.float32)
        for more in refs[used + 1:used + count]:
            arrived = arrived + more[...].astype(jnp.float32)
        used += count
        patch = patches[first_half + index].astype(jnp.bfloat16)
        moved = jnp.dot(hot, patch, preferred_element_type=jnp.float32)
        filled = arrived * ((1.0 - dead) * mask) + moved
        out_ref[:, index * WIN:(index + 1) * WIN] = filled.astype(jnp.bfloat16)


def fill_window(first_half, arrived, picked, miss_lanes, recv8):
    rows = arrived[0][0].shape[0]
    misses = picked[0].shape[0]
    counts = tuple(len(group) for group in arrived)
    flat = [part for group in arrived for part in group]
    lanes = len(counts) * WIN
    whole = pl.BlockSpec((rows, WIN), lambda i: (0, 0))
    return pl.pallas_call(
        functools.partial(fill_kernel, counts, first_half),
        grid=(1,),
        in_specs=[
            pl.BlockSpec((misses, WIN), lambda i: (0, 0)),
            pl.BlockSpec((misses, WIN), lambda i: (0, 0)),
            pl.BlockSpec((1, LANES), lambda i: (0, 0)),
            pl.BlockSpec((8, WIN), lambda i: (0, 0)),
        ]
        + [whole] * len(flat),
        out_specs=pl.BlockSpec((rows, lanes), lambda i: (0, 0)),
        out_shape=jax.ShapeDtypeStruct((rows, lanes), jnp.bfloat16),
        compiler_params=params(),
        cost_estimate=cost(4 * rows * LANES * lanes, 8 * rows * lanes),
        name="fill_window",
    )(*picked, miss_lanes, recv8, *flat)


def complex_rows(real_rows, imag_rows, right):
    first = jnp.dot(real_rows, right, preferred_element_type=jnp.float32)
    second = jnp.dot(imag_rows, right, preferred_element_type=jnp.float32)
    if CHUNKS == 1:
        real_part = first[:, :WIN] - second[:, WIN:]
        imag_part = first[:, WIN:] + second[:, :WIN]
        return jnp.concatenate([real_part, imag_part], axis=1)
    turned = pltpu.roll(second, WIDTH, 1)
    low = lax.broadcasted_iota(jnp.int32, first.shape, 1) < WIDTH
    return first + jnp.where(low, -turned, turned)


def choose(out_ref, pick, refs):
    for index, ref in enumerate(refs):

        @pl.when(pick == index)
        def _():
            out_ref[...] = ref[...]


def product_kernel(counts, pick_ref, recv_ref, *refs):
    tiles, refs = refs[:4], refs[4:]
    total, places = sum(counts), len(counts)
    out_refs, right_refs = refs[total:total + places], refs[total + places:-1]
    sem = refs[-1]

    @pl.when(pl.program_id(0) == 0)
    def _():
        used = 0
        for place, count in enumerate(counts):
            for index, ref in enumerate(refs[used:used + count]):

                @pl.when(pick_ref[place] == index)
                def _():
                    copy = pltpu.make_async_copy(ref, right_refs[place], sem.at[place])
                    copy.start()
                    copy.wait()

            used += count

    recv = recv_ref[0:1, :]
    half = tiles[0].shape[1]
    for side in range(2):
        real_rows, imag_rows = (tiles[2 * part + side][0] * recv for part in range(2))
        for out_ref, right_ref in zip(out_refs, right_refs):
            out_ref[side * half:(side + 1) * half, :] = complex_rows(
                real_rows, imag_rows, right_ref[...]
            )


def products(traces, recv8, groups):
    _, rows, cols = traces.shape
    lanes = groups[0][1][0].shape[1]
    counts = tuple(len(sources) for _, sources in groups)
    flat = [source for _, sources in groups for source in sources]
    picks = jnp.stack([pick for pick, _ in groups]).astype(jnp.int32)
    block = row_block(rows)
    quarter = lambda part, side: pl.BlockSpec(
        (1, block // 2, cols), lambda i: (part, 2 * i + side, 0)
    )
    return pl.pallas_call(
        functools.partial(product_kernel, counts),
        grid=(rows // block,),
        in_specs=[
            SMEM,
            pl.BlockSpec((8, cols), lambda i: (0, 0)),
        ]
        + [quarter(part, side) for part in range(2) for side in range(2)]
        + [pl.BlockSpec(memory_space=pl.ANY)] * len(flat),
        out_specs=[pl.BlockSpec((block, lanes), lambda i: (i, 0))] * len(groups),
        out_shape=[jax.ShapeDtypeStruct((rows, lanes), jnp.float32)] * len(groups),
        scratch_shapes=[pltpu.VMEM((cols, lanes), jnp.bfloat16)] * len(groups)
        + [pltpu.SemaphoreType.DMA((len(groups),))],
        compiler_params=params(),
        cost_estimate=cost(8 * rows * cols * lanes * len(groups), 4 * rows * lanes),
        name="products",
    )(picks, recv8, *[traces] * 4, *flat)


def extra_kernel(counts, pick_ref, real_ref, imag_ref, *refs):
    out_ref, right_ref = refs[-2:]
    used = 0
    for place, count in enumerate(counts):
        choose(right_ref, pick_ref[2 * place], refs[used:used + count])
        used += count
        out_ref[pick_ref[2 * place + 1]] = complex_rows(real_ref[...], imag_ref[...], right_ref[...])


def extra_products(rows, groups):
    misses, cols = rows[0].shape
    lanes = groups[0][2][0].shape[1]
    counts = tuple(len(sources) for _, _, sources in groups)
    flat = [source for _, _, sources in groups for source in sources]
    picks = jnp.stack([x for pick, place, _ in groups for x in (pick, place)]).astype(jnp.int32)
    return pl.pallas_call(
        functools.partial(extra_kernel, counts),
        in_specs=[SMEM] + [VMEM] * (2 + len(flat)),
        out_specs=VMEM,
        out_shape=jax.ShapeDtypeStruct((len(groups), misses, lanes), jnp.float32),
        scratch_shapes=[pltpu.VMEM((cols, lanes), jnp.bfloat16)],
        compiler_params=params(),
        cost_estimate=cost(8 * misses * cols * lanes * len(groups), 4 * cols * lanes),
        name="extra_products",
    )(picks, *rows, *flat)


def finish_kernel(counts, wave_ref, flag_ref, miss_ref, recv_ref, tile_ref, real_ref, imag_ref, *refs):
    out_ref, row_ref = refs[-2:]
    totals = []
    used = 0
    for count in counts:
        total = refs[used][...]
        if count > 1:
            total = total * flag_ref[0]
        for index, ref in enumerate(refs[used + 1:used + count], 1):
            total = total + (ref[...] * flag_ref[index] if index < count // 2 else ref[...])
        used += count
        totals.append(total)

    def write(target, window, chunks):
        real_part, imag_part = unpack(chunks)
        real_pred = real_part * wave_ref[0] - imag_part * wave_ref[1]
        imag_pred = imag_part * wave_ref[0] + real_part * wave_ref[1]
        target[0] = window[0] - real_pred
        target[1] = window[1] - imag_pred

    recv = recv_ref[0:1, :].astype(jnp.float32)
    write(out_ref, [tile_ref[part].astype(jnp.float32) * recv for part in range(2)], totals[:CHUNKS])
    write(row_ref, [ref[...].astype(jnp.float32) for ref in (real_ref, imag_ref)], totals[CHUNKS:])

    def place(m, carry):
        for part in range(2):
            out_ref[part, pl.ds(miss_ref[m], 1), :] = row_ref[part, pl.ds(m, 1), :]
        return carry

    lax.fori_loop(0, row_ref.shape[1], place, 0, unroll=8)


def finish(wave, flag, miss, recv8, traces, extra, terms):
    _, rows, _ = traces.shape
    misses = extra[0].shape[0]
    counts = tuple(len(group) for group in terms)
    flat = [term for group in terms for term in group]
    window = lambda size: pl.BlockSpec((2, size, WIN), lambda i: (0, 0, 0))
    return pl.pallas_call(
        functools.partial(finish_kernel, counts),
        grid=(1,),
        in_specs=[SMEM, SMEM, SMEM, pl.BlockSpec((8, WIN), lambda i: (0, 0)), window(rows)]
        + [pl.BlockSpec((misses, WIN), lambda i: (0, 0))] * 2
        + [VMEM] * len(flat),
        out_specs=window(rows),
        out_shape=jax.ShapeDtypeStruct((2, rows, WIN), jnp.float32),
        scratch_shapes=[pltpu.VMEM((2, misses, WIN), jnp.float32)],
        compiler_params=params(),
        cost_estimate=cost(20 * rows * WIN, 40 * rows * WIN),
        name="finish",
    )(wave, flag, miss, recv8, traces, *extra, *flat)


def mirror_routes(grid_size):
    cells = [(a, b) for a in range(grid_size) for b in range(grid_size)]
    index = lambda row, col: row * grid_size + col
    whole = [(index(a, b), index(b, a)) for a, b in cells]
    near = [(index(a, b), index(b, a)) for a, b in cells if a // 2 == b // 2]
    far = [(a, b) for a, b in cells if a // 2 != b // 2]
    hop = lambda a, b: index(a, a // 2 * 2 + b % 2)
    first = [(index(a, b), hop(a, b)) for a, b in far]
    second = [(hop(a, b), index(b, a)) for a, b in far]
    if len({target for _, target in first}) < len(first):
        return whole, None
    return whole, (near, first, second)


def sources_of(up, down, offset, grid_size, row_index):
    places, sources = [], []
    for row in range(grid_size):
        other = row ^ offset
        source = up[row - other] if other < row else down[other - row]
        known = [index for index, seen in enumerate(sources) if seen is source]
        places.append(known[0] if known else len(sources))
        if not known:
            sources.append(source)
    pick = jnp.zeros((), jnp.int32)
    for row, place in enumerate(places):
        pick = jnp.where(row_index == row, place, pick)
    return pick, sources


def sum_route(offset, grid_size, stride, skip):
    route = []
    for row in range(grid_size):
        for col in range(grid_size):
            if ((col ^ row ^ offset) & ~skip) % (2 * stride) == stride:
                route.append((row * grid_size + col, row * grid_size + (col ^ stride)))
    return route


def local(traces, recv_live, missing, wavelet):
    tile = traces.shape[1]
    grid_size = lax.axis_size("row")
    misses = missing.shape[1]
    order = recv_live.shape[0]
    row_index = lax.axis_index("row")
    col_index = lax.axis_index("col")
    whole, hops = mirror_routes(grid_size)

    def move(block, route):
        return lax.ppermute(block, ("row", "col"), route)

    def transpose(block):
        return move(block, whole)

    def transpose_round(block):
        if hops is None:
            return [move(block, whole)]
        near, first, second = hops
        return [move(move(block, first), second), move(block, near)]

    direct, round_about = cut_window(traces)
    arrived = [[transpose(direct)], transpose_round(round_about)]
    if CHUNKS == 1:
        arrived = [arrived]
    else:
        arrived = [arrived[:1], arrived[1:]]

    miss_row = lax.dynamic_index_in_dim(missing, row_index, 0, keepdims=False)
    miss_col = lax.dynamic_index_in_dim(missing, col_index, 0, keepdims=False)
    as_lanes = lambda m: jnp.pad(m, (0, LANES - misses), constant_values=-1)[None]
    miss_col_lanes = as_lanes(miss_col)
    positions = jnp.arange(tile, dtype=jnp.int32)
    live_row = jnp.all(positions[:, None] != miss_row[None, :], axis=1)
    live8 = jnp.broadcast_to(live_row.astype(jnp.float32)[None], (8, tile))
    recv_mask = (recv_live == 1).astype(jnp.bfloat16)
    recv_row = lax.dynamic_slice_in_dim(recv_mask, row_index * tile, WIN)
    recv_row8 = jnp.broadcast_to(recv_row[None], (8, WIN))
    recv_col = lax.dynamic_slice_in_dim(recv_mask, col_index * tile, tile)
    recv_col8 = jnp.broadcast_to(recv_col[None], (8, tile))

    picked = pick_columns(traces, miss_col_lanes, recv_col8, live8, misses)
    extra = None
    apart = row_index ^ col_index
    strides = [2**bit for bit in range(grid_size.bit_length() - 1)]
    terms, extra_terms = [], []
    for chunk in range(CHUNKS):
        window = fill_window(chunk, arrived[chunk], picked, miss_col_lanes, recv_row8)
        up, down = [window], [window]
        sums = []

        def hop(distance):
            ends = [(i, i + 1) for i in range(distance - 1, grid_size - 1)]
            back = [(i + 1, i) for i in range(grid_size - distance)]
            up.append(lax.ppermute(up[-1], "row", ends))
            down.append(lax.ppermute(down[-1], "row", back))

        def add_up(total, offset, strides, skip):
            for stride in strides:
                total = total + move(total, sum_route(offset, grid_size, stride, skip))
            return total

        def last(total, offset, skip):
            return move(total, sum_route(offset, grid_size, strides[-1], skip))

        def options(offset):
            return sources_of(up, down, offset, grid_size, row_index)

        hop(1)
        hop(2)
        if extra is None:
            both, up[-1], down[-1] = lax.optimization_barrier(
                (jnp.concatenate(picked), up[-1], down[-1])
            )
            both = transpose(both)
            extra = [both[:misses], both[misses:]]
        _, (block0,) = options(0)
        pick1, sources1 = options(1)
        odd = apart & 1
        everything = [block0] + sources1
        keep, sent = products(
            traces,
            recv_col8,
            [
                (jnp.where(odd == 1, 1 + pick1, 0), everything),
                (jnp.where(odd == 1, 0, 1 + pick1), everything),
            ],
        )
        other_core = [(i, i ^ 1) for i in range(grid_size)]
        total = add_up(keep + lax.ppermute(sent, "col", other_core), 0, strides[1:-1], 1)
        for distance in range(3, grid_size):
            hop(distance)
        sums = [(0, 1, apart // 2 == 0, total)]
        first = last(total, 0, 1)
        mask = recv_col8
        for offset in range(2, grid_size):
            if offset == grid_size - 1:
                mask, first, extra = lax.optimization_barrier((mask, first, extra))
            (total,) = products(traces, mask, [options(offset)])
            total = add_up(total, offset, strides[:-1], 0)
            sums.append((offset, 0, apart == offset, total))
        got = [first] + [last(total, offset, skip) for offset, skip, _, total in sums[1:]]
        extra, _ = lax.optimization_barrier((extra, sums[-1][-1]))
        terms.append([total for *_, total in sums] + got)
        flags = [mine for _, _, mine, _ in sums]
        group = [(pick, apart ^ offset, sources) for offset in range(grid_size)
                 for pick, sources in [options(offset)]]
        rest = extra_products(extra, group)
        for stride in strides:
            pairs = [(i, i ^ stride) for i in range(grid_size)]
            arrive = lax.ppermute(rest[1::2], "col", pairs)
            rest = rest[0::2] + arrive
        extra_terms.append((rest[0],))
    wave = wavelet * (1.0 / math.sqrt(order))
    flag = jnp.stack(flags).astype(jnp.float32)
    return finish(wave, flag, miss_row, recv_col8, traces, extra, terms + extra_terms)


def solution(mesh):
    in_specs = (P("freq", "row", "col"), P("freq"), P("freq", None), P("freq"))
    out_specs = P("freq", "row", "col")
    return jax.shard_map(local, mesh=mesh, in_specs=in_specs, out_specs=out_specs, check_vma=False)
```

```python
import functools
import math

import jax
import jax.numpy as jnp
from jax import lax
from jax.experimental import pallas as pl
from jax.experimental.pallas import tpu as pltpu
from jax.sharding import PartitionSpec as P

WIN = 128
LANES = 128
CHUNKS = 1
WIDTH = WIN // CHUNKS
TINY = 1e-30
HALF_TOP = 32768.0
VMEM_LIMIT = 48 * 2**20
VMEM = pl.BlockSpec(memory_space=pltpu.VMEM)
SMEM = pl.BlockSpec(memory_space=pltpu.SMEM)


def params():
    return pltpu.CompilerParams(vmem_limit_bytes=VMEM_LIMIT)


def cost(flops, accessed):
    return pl.CostEstimate(
        flops=int(flops) // 64, bytes_accessed=int(accessed) // 64, transcendentals=0
    )


def row_block(rows):
    for size in (512, 384, 256, 128):
        if rows % size == 0:
            return size
    return rows


def one_hot(positions_row, rows, dtype):
    lanes = positions_row.shape[1]
    row_ids = lax.broadcasted_iota(jnp.int32, (rows, lanes), 0)
    return jnp.where(row_ids == positions_row, 1.0, 0.0).astype(dtype)


def pack(real_part, imag_part):
    if CHUNKS == 1:
        return [jnp.concatenate([real_part, imag_part], axis=1)]
    first = lax.broadcasted_iota(jnp.int32, real_part.shape, 1) < WIDTH
    low = jnp.where(first, real_part, pltpu.roll(imag_part, WIDTH, 1))
    high = jnp.where(first, pltpu.roll(real_part, WIDTH, 1), imag_part)
    return [low, high]


def unpack(chunks):
    if CHUNKS == 1:
        return chunks[0][:, :WIN], chunks[0][:, WIN:]
    low, high = chunks
    first = lax.broadcasted_iota(jnp.int32, low.shape, 1) < WIDTH
    real_part = jnp.where(first, low, pltpu.roll(high, WIDTH, 1))
    imag_part = jnp.where(first, pltpu.roll(low, WIDTH, 1), high)
    return real_part, imag_part


def halves(real_part, imag_part):
    return [real_part, imag_part] if CHUNKS == 1 else pack(real_part, imag_part)


def cut_kernel(traces_ref, *out_refs):
    parts = halves(traces_ref[0].astype(jnp.float32), traces_ref[1].astype(jnp.float32))
    for out_ref, part in zip(out_refs, parts):
        out_ref[...] = part.astype(jnp.bfloat16)


def cut_window(traces):
    rows = traces.shape[1]
    return pl.pallas_call(
        cut_kernel,
        grid=(1,),
        in_specs=[pl.BlockSpec((2, rows, WIN), lambda i: (0, 0, 0))],
        out_specs=[pl.BlockSpec((rows, WIN), lambda i: (0, 0))] * 2,
        out_shape=[jax.ShapeDtypeStruct((rows, WIN), jnp.bfloat16)] * 2,
        compiler_params=params(),
        cost_estimate=cost(rows * WIN, 8 * rows * WIN),
        name="cut_window",
    )(traces)


def pick_kernel(traces_ref, miss_ref, recv_ref, live_ref, real_ref, imag_ref, hot_ref):
    @pl.when(pl.program_id(0) == 0)
    def _():
        hot = one_hot(miss_ref[...], hot_ref.shape[0], jnp.bfloat16)
        alive = jnp.dot(recv_ref[...], hot, preferred_element_type=jnp.float32)
        hot_ref[...] = hot * alive[0:1].astype(jnp.bfloat16)

    misses = real_ref.shape[0]
    for part, out_ref in enumerate((real_ref, imag_ref)):
        picked = jnp.dot(traces_ref[part], hot_ref[...], preferred_element_type=jnp.float32)
        turned = picked.T * live_ref[0:1, :]
        out_ref[...] = turned[:misses].astype(jnp.bfloat16)


def pick_columns(traces, miss_lanes, recv8, live8, misses):
    _, rows, cols = traces.shape
    block = row_block(rows)
    return pl.pallas_call(
        pick_kernel,
        grid=(rows // block,),
        in_specs=[
            pl.BlockSpec((2, block, cols), lambda i: (0, i, 0)),
            pl.BlockSpec((1, LANES), lambda i: (0, 0)),
            pl.BlockSpec((8, cols), lambda i: (0, 0)),
            pl.BlockSpec((8, block), lambda i: (0, i)),
        ],
        out_specs=[pl.BlockSpec((misses, block), lambda i: (0, i))] * 2,
        out_shape=[jax.ShapeDtypeStruct((misses, rows), jnp.bfloat16)] * 2,
        scratch_shapes=[pltpu.VMEM((cols, LANES), jnp.bfloat16)],
        compiler_params=params(),
        cost_estimate=cost(4 * rows * cols * 2 * LANES, 4 * rows * cols),
        name="pick_columns",
    )(traces, miss_lanes, recv8, live8)


def fill_kernel(counts, first_half, real_ref, imag_ref, miss_ref, recv_ref, *refs):
    out_ref = refs[-1]
    rows = out_ref.shape[0]
    misses = real_ref.shape[0]
    hot = one_hot(miss_ref[...], rows, jnp.float32)
    dead = jnp.max(hot, axis=1, keepdims=True)
    hot = hot[:, :misses].astype(jnp.bfloat16)
    patches = halves(real_ref[...].astype(jnp.float32), imag_ref[...].astype(jnp.float32))
    mask = recv_ref[...].astype(jnp.float32)
    mask = halves(mask, mask)[0][0:1, :]
    used = 0
    for index, count in enumerate(counts):
        arrived = refs[used][...].astype(jnp.float32)
        for more in refs[used + 1:used + count]:
            arrived = arrived + more[...].astype(jnp.float32)
        used += count
        patch = patches[first_half + index].astype(jnp.bfloat16)
        moved = jnp.dot(hot, patch, preferred_element_type=jnp.float32)
        filled = arrived * ((1.0 - dead) * mask) + moved
        out_ref[:, index * WIN:(index + 1) * WIN] = filled.astype(jnp.bfloat16)


def fill_window(first_half, arrived, picked, miss_lanes, recv8):
    rows = arrived[0][0].shape[0]
    misses = picked[0].shape[0]
    counts = tuple(len(group) for group in arrived)
    flat = [part for group in arrived for part in group]
    lanes = len(counts) * WIN
    whole = pl.BlockSpec((rows, WIN), lambda i: (0, 0))
    return pl.pallas_call(
        functools.partial(fill_kernel, counts, first_half),
        grid=(1,),
        in_specs=[
            pl.BlockSpec((misses, WIN), lambda i: (0, 0)),
            pl.BlockSpec((misses, WIN), lambda i: (0, 0)),
            pl.BlockSpec((1, LANES), lambda i: (0, 0)),
            pl.BlockSpec((8, WIN), lambda i: (0, 0)),
        ]
        + [whole] * len(flat),
        out_specs=pl.BlockSpec((rows, lanes), lambda i: (0, 0)),
        out_shape=jax.ShapeDtypeStruct((rows, lanes), jnp.bfloat16),
        compiler_params=params(),
        cost_estimate=cost(4 * rows * LANES * lanes, 8 * rows * lanes),
        name="fill_window",
    )(*picked, miss_lanes, recv8, *flat)


def complex_rows(real_rows, imag_rows, right):
    first = jnp.dot(real_rows, right, preferred_element_type=jnp.float32)
    second = jnp.dot(imag_rows, right, preferred_element_type=jnp.float32)
    if CHUNKS == 1:
        real_part = first[:, :WIN] - second[:, WIN:]
        imag_part = first[:, WIN:] + second[:, :WIN]
        return jnp.concatenate([real_part, imag_part], axis=1)
    turned = pltpu.roll(second, WIDTH, 1)
    low = lax.broadcasted_iota(jnp.int32, first.shape, 1) < WIDTH
    return first + jnp.where(low, -turned, turned)


def choose(out_ref, pick, refs):
    for index, ref in enumerate(refs):

        @pl.when(pick == index)
        def _():
            out_ref[...] = ref[...]


def product_kernel(counts, pick_ref, recv_ref, *refs):
    tiles, refs = refs[:4], refs[4:]
    total, places = sum(counts), len(counts)
    out_refs, right_refs = refs[total:total + places], refs[total + places:-1]
    sem = refs[-1]

    @pl.when(pl.program_id(0) == 0)
    def _():
        used = 0
        for place, count in enumerate(counts):
            for index, ref in enumerate(refs[used:used + count]):

                @pl.when(pick_ref[place] == index)
                def _():
                    copy = pltpu.make_async_copy(ref, right_refs[place], sem.at[place])
                    copy.start()
                    copy.wait()

            used += count

    recv = recv_ref[0:1, :]
    half = tiles[0].shape[1]
    for side in range(2):
        real_rows, imag_rows = (tiles[2 * part + side][0] * recv for part in range(2))
        for out_ref, right_ref in zip(out_refs, right_refs):
            out_ref[side * half:(side + 1) * half, :] = complex_rows(
                real_rows, imag_rows, right_ref[...]
            )


def products(traces, recv8, groups):
    _, rows, cols = traces.shape
    lanes = groups[0][1][0].shape[1]
    counts = tuple(len(sources) for _, sources in groups)
    flat = [source for _, sources in groups for source in sources]
    picks = jnp.stack([pick for pick, _ in groups]).astype(jnp.int32)
    block = row_block(rows)
    quarter = lambda part, side: pl.BlockSpec(
        (1, block // 2, cols), lambda i: (part, 2 * i + side, 0)
    )
    return pl.pallas_call(
        functools.partial(product_kernel, counts),
        grid=(rows // block,),
        in_specs=[
            SMEM,
            pl.BlockSpec((8, cols), lambda i: (0, 0)),
        ]
        + [quarter(part, side) for part in range(2) for side in range(2)]
        + [pl.BlockSpec(memory_space=pl.ANY)] * len(flat),
        out_specs=[pl.BlockSpec((block, lanes), lambda i: (i, 0))] * len(groups),
        out_shape=[jax.ShapeDtypeStruct((rows, lanes), jnp.float32)] * len(groups),
        scratch_shapes=[pltpu.VMEM((cols, lanes), jnp.bfloat16)] * len(groups)
        + [pltpu.SemaphoreType.DMA((len(groups),))],
        compiler_params=params(),
        cost_estimate=cost(8 * rows * cols * lanes * len(groups), 4 * rows * lanes),
        name="products",
    )(picks, recv8, *[traces] * 4, *flat)


def extra_kernel(counts, pick_ref, real_ref, imag_ref, *refs):
    out_ref, right_ref = refs[-2:]
    used = 0
    for place, count in enumerate(counts):
        choose(right_ref, pick_ref[2 * place], refs[used:used + count])
        used += count
        out_ref[pick_ref[2 * place + 1]] = complex_rows(real_ref[...], imag_ref[...], right_ref[...])


def extra_products(rows, groups):
    misses, cols = rows[0].shape
    lanes = groups[0][2][0].shape[1]
    counts = tuple(len(sources) for _, _, sources in groups)
    flat = [source for _, _, sources in groups for source in sources]
    picks = jnp.stack([x for pick, place, _ in groups for x in (pick, place)]).astype(jnp.int32)
    return pl.pallas_call(
        functools.partial(extra_kernel, counts),
        in_specs=[SMEM] + [VMEM] * (2 + len(flat)),
        out_specs=VMEM,
        out_shape=jax.ShapeDtypeStruct((len(groups), misses, lanes), jnp.float32),
        scratch_shapes=[pltpu.VMEM((cols, lanes), jnp.bfloat16)],
        compiler_params=params(),
        cost_estimate=cost(8 * misses * cols * lanes * len(groups), 4 * cols * lanes),
        name="extra_products",
    )(picks, *rows, *flat)


def finish_kernel(wave_ref, miss_ref, recv_ref, tile_ref, real_ref, imag_ref, *refs):
    out_ref, row_ref = refs[-2:]
    totals = [ref[...] for ref in refs[:-2]]

    def write(target, window, chunks):
        real_part, imag_part = unpack(chunks)
        real_pred = real_part * wave_ref[0] - imag_part * wave_ref[1]
        imag_pred = imag_part * wave_ref[0] + real_part * wave_ref[1]
        target[0] = window[0] - real_pred
        target[1] = window[1] - imag_pred

    recv = recv_ref[0:1, :].astype(jnp.float32)
    write(out_ref, [tile_ref[part].astype(jnp.float32) * recv for part in range(2)], totals[:CHUNKS])
    write(row_ref, [ref[...].astype(jnp.float32) for ref in (real_ref, imag_ref)], totals[CHUNKS:])

    def place(m, carry):
        for part in range(2):
            out_ref[part, pl.ds(miss_ref[m], 1), :] = row_ref[part, pl.ds(m, 1), :]
        return carry

    lax.fori_loop(0, row_ref.shape[1], place, 0, unroll=8)


def finish(wave, miss, recv8, traces, extra, terms):
    _, rows, _ = traces.shape
    misses = extra[0].shape[0]
    flat = [term for group in terms for term in group]
    window = lambda size: pl.BlockSpec((2, size, WIN), lambda i: (0, 0, 0))
    return pl.pallas_call(
        finish_kernel,
        grid=(1,),
        in_specs=[SMEM, SMEM, pl.BlockSpec((8, WIN), lambda i: (0, 0)), window(rows)]
        + [pl.BlockSpec((misses, WIN), lambda i: (0, 0))] * 2
        + [VMEM] * len(flat),
        out_specs=window(rows),
        out_shape=jax.ShapeDtypeStruct((2, rows, WIN), jnp.float32),
        scratch_shapes=[pltpu.VMEM((2, misses, WIN), jnp.float32)],
        compiler_params=params(),
        cost_estimate=cost(20 * rows * WIN, 40 * rows * WIN),
        name="finish",
    )(wave, miss, recv8, traces, *extra, *flat)


def mirror_routes(grid_size):
    cells = [(a, b) for a in range(grid_size) for b in range(grid_size)]
    index = lambda row, col: row * grid_size + col
    whole = [(index(a, b), index(b, a)) for a, b in cells]
    near = [(index(a, b), index(b, a)) for a, b in cells if a // 2 == b // 2]
    far = [(a, b) for a, b in cells if a // 2 != b // 2]
    hop = lambda a, b: index(a, a // 2 * 2 + b % 2)
    first = [(index(a, b), hop(a, b)) for a, b in far]
    second = [(hop(a, b), index(b, a)) for a, b in far]
    if len({target for _, target in first}) < len(first):
        return whole, None
    return whole, (near, first, second)


def sources_of(up, down, offset, grid_size, row_index):
    places, sources = [], []
    for row in range(grid_size):
        other = row ^ offset
        source = up[row - other] if other < row else down[other - row]
        known = [index for index, seen in enumerate(sources) if seen is source]
        places.append(known[0] if known else len(sources))
        if not known:
            sources.append(source)
    pick = jnp.zeros((), jnp.int32)
    for row, place in enumerate(places):
        pick = jnp.where(row_index == row, place, pick)
    return pick, sources


def sum_route(offset, grid_size, stride, skip):
    route = []
    for row in range(grid_size):
        for col in range(grid_size):
            if ((col ^ row ^ offset) & ~skip) % (2 * stride) == stride:
                route.append((row * grid_size + col, row * grid_size + (col ^ stride)))
    return route


def local(traces, recv_live, missing, wavelet):
    tile = traces.shape[1]
    grid_size = lax.axis_size("row")
    misses = missing.shape[1]
    order = recv_live.shape[0]
    row_index = lax.axis_index("row")
    col_index = lax.axis_index("col")
    whole, hops = mirror_routes(grid_size)

    def move(block, route):
        return lax.ppermute(block, ("row", "col"), route)

    def transpose(block):
        return move(block, whole)

    def transpose_round(block):
        if hops is None:
            return [move(block, whole)]
        near, first, second = hops
        return [move(move(block, first), second), move(block, near)]

    direct, round_about = cut_window(traces)
    arrived = [[transpose(direct)], transpose_round(round_about)]
    if CHUNKS == 1:
        arrived = [arrived]
    else:
        arrived = [arrived[:1], arrived[1:]]

    miss_row = lax.dynamic_index_in_dim(missing, row_index, 0, keepdims=False)
    miss_col = lax.dynamic_index_in_dim(missing, col_index, 0, keepdims=False)
    as_lanes = lambda m: jnp.pad(m, (0, LANES - misses), constant_values=-1)[None]
    miss_col_lanes = as_lanes(miss_col)
    positions = jnp.arange(tile, dtype=jnp.int32)
    live_row = jnp.all(positions[:, None] != miss_row[None, :], axis=1)
    live8 = jnp.broadcast_to(live_row.astype(jnp.float32)[None], (8, tile))
    recv_mask = (recv_live == 1).astype(jnp.bfloat16)
    recv_row = lax.dynamic_slice_in_dim(recv_mask, row_index * tile, WIN)
    recv_row8 = jnp.broadcast_to(recv_row[None], (8, WIN))
    recv_col = lax.dynamic_slice_in_dim(recv_mask, col_index * tile, tile)
    recv_col8 = jnp.broadcast_to(recv_col[None], (8, tile))

    picked = pick_columns(traces, miss_col_lanes, recv_col8, live8, misses)
    both = transpose(jnp.concatenate(picked))
    extra = [both[:misses], both[misses:]]
    apart = row_index ^ col_index
    strides = [2**bit for bit in range(grid_size.bit_length() - 1)]
    terms, extra_terms = [], []
    for chunk in range(CHUNKS):
        window = fill_window(chunk, arrived[chunk], picked, miss_col_lanes, recv_row8)
        up, down = [window], [window]
        sums = []

        def hop(distance):
            ends = [(i, i + 1) for i in range(distance - 1, grid_size - 1)]
            back = [(i + 1, i) for i in range(grid_size - distance)]
            up.append(lax.ppermute(up[-1], "row", ends))
            down.append(lax.ppermute(down[-1], "row", back))

        def add_up(total, offset, strides, skip):
            for stride in strides:
                total = total + move(total, sum_route(offset, grid_size, stride, skip))
            return total

        def shrink(total):
            unit = jnp.maximum(jnp.max(jnp.abs(total)), TINY) * (1.0 / HALF_TOP)
            sent = (total * (1.0 / unit)).astype(jnp.float16)
            return sent, jnp.broadcast_to(unit, (1, LANES))

        def last(shrunk, offset, skip):
            route = sum_route(offset, grid_size, strides[-1], skip)
            return [move(part, route) for part in shrunk]

        def options(offset):
            return sources_of(up, down, offset, grid_size, row_index)

        hop(1)
        extra, up[-1], down[-1] = lax.optimization_barrier((extra, up[-1], down[-1]))
        hop(2)
        _, (block0,) = options(0)
        pick1, sources1 = options(1)
        odd = apart & 1
        everything = [block0] + sources1
        keep, sent = products(
            traces,
            recv_col8,
            [
                (jnp.where(odd == 1, 1 + pick1, 0), everything),
                (jnp.where(odd == 1, 0, 1 + pick1), everything),
            ],
        )
        other_core = [(i, i ^ 1) for i in range(grid_size)]
        total = add_up(keep + lax.ppermute(sent, "col", other_core), 0, strides[1:-1], 1)
        shrunk, up[-1], down[-1] = lax.optimization_barrier((shrink(total), up[-1], down[-1]))
        for distance in range(3, grid_size):
            hop(distance)
        sums = [(0, 1, apart // 2 == 0, total)]
        got = [last(shrunk, 0, 1)]
        mask = recv_col8
        for offset in range(2, grid_size):
            if offset == grid_size - 1:
                mask, got[0] = lax.optimization_barrier((mask, got[0]))
            (total,) = products(traces, mask, [options(offset)])
            total = add_up(total, offset, strides[:-1], 0)
            sums.append((offset, 0, apart == offset, total))
            got.append(last(shrink(total), offset, 0))
        extra, got[-1][1] = lax.optimization_barrier((extra, got[-1][1]))
        whole_sum = None
        for (*_, mine, part), (sent, units) in zip(sums, got):
            term = jnp.where(mine, part, 0.0) + sent.astype(jnp.float32) * units[0, 0]
            whole_sum = term if whole_sum is None else whole_sum + term
        terms.append((whole_sum,))
        group = [(pick, apart ^ offset, sources) for offset in range(grid_size)
                 for pick, sources in [options(offset)]]
        rest = extra_products(extra, group)
        for stride in strides:
            pairs = [(i, i ^ stride) for i in range(grid_size)]
            arrive = lax.ppermute(rest[1::2], "col", pairs)
            rest = rest[0::2] + arrive
        extra_terms.append((rest[0],))
    wave = wavelet * (1.0 / math.sqrt(order))
    return finish(wave, miss_row, recv_col8, traces, extra, terms + extra_terms)


def solution(mesh):
    in_specs = (P("freq", "row", "col"), P("freq"), P("freq", None), P("freq"))
    out_specs = P("freq", "row", "col")
    return jax.shard_map(local, mesh=mesh, in_specs=in_specs, out_specs=out_specs, check_vma=False)
```

```python
import functools
import math

import jax
import jax.numpy as jnp
from jax import lax
from jax.experimental import pallas as pl
from jax.experimental.pallas import tpu as pltpu
from jax.sharding import PartitionSpec as P

WIN = 128
LANES = 128
CHUNKS = 1
WIDTH = WIN // CHUNKS
TINY = 1e-30
HALF_TOP = 32768.0
VMEM_LIMIT = 48 * 2**20
VMEM = pl.BlockSpec(memory_space=pltpu.VMEM)
SMEM = pl.BlockSpec(memory_space=pltpu.SMEM)


def params():
    return pltpu.CompilerParams(vmem_limit_bytes=VMEM_LIMIT)


def cost(flops, accessed):
    return pl.CostEstimate(
        flops=int(flops) // 64, bytes_accessed=int(accessed) // 64, transcendentals=0
    )


def row_block(rows):
    for size in (512, 384, 256, 128):
        if rows % size == 0:
            return size
    return rows


def one_hot(positions_row, rows, dtype):
    lanes = positions_row.shape[1]
    row_ids = lax.broadcasted_iota(jnp.int32, (rows, lanes), 0)
    return jnp.where(row_ids == positions_row, 1.0, 0.0).astype(dtype)


def pack(real_part, imag_part):
    if CHUNKS == 1:
        return [jnp.concatenate([real_part, imag_part], axis=1)]
    first = lax.broadcasted_iota(jnp.int32, real_part.shape, 1) < WIDTH
    low = jnp.where(first, real_part, pltpu.roll(imag_part, WIDTH, 1))
    high = jnp.where(first, pltpu.roll(real_part, WIDTH, 1), imag_part)
    return [low, high]


def unpack(chunks):
    if CHUNKS == 1:
        return chunks[0][:, :WIN], chunks[0][:, WIN:]
    low, high = chunks
    first = lax.broadcasted_iota(jnp.int32, low.shape, 1) < WIDTH
    real_part = jnp.where(first, low, pltpu.roll(high, WIDTH, 1))
    imag_part = jnp.where(first, pltpu.roll(low, WIDTH, 1), high)
    return real_part, imag_part


def halves(real_part, imag_part):
    return [real_part, imag_part] if CHUNKS == 1 else pack(real_part, imag_part)


def cut_kernel(traces_ref, *out_refs):
    parts = halves(traces_ref[0].astype(jnp.float32), traces_ref[1].astype(jnp.float32))
    for out_ref, part in zip(out_refs, parts):
        out_ref[...] = part.astype(jnp.bfloat16)


def cut_window(traces):
    rows = traces.shape[1]
    return pl.pallas_call(
        cut_kernel,
        grid=(1,),
        in_specs=[pl.BlockSpec((2, rows, WIN), lambda i: (0, 0, 0))],
        out_specs=[pl.BlockSpec((rows, WIN), lambda i: (0, 0))] * 2,
        out_shape=[jax.ShapeDtypeStruct((rows, WIN), jnp.bfloat16)] * 2,
        compiler_params=params(),
        cost_estimate=cost(rows * WIN, 8 * rows * WIN),
        name="cut_window",
    )(traces)


def pick_kernel(traces_ref, miss_ref, recv_ref, live_ref, real_ref, imag_ref, hot_ref):
    @pl.when(pl.program_id(0) == 0)
    def _():
        hot = one_hot(miss_ref[...], hot_ref.shape[0], jnp.bfloat16)
        alive = jnp.dot(recv_ref[...], hot, preferred_element_type=jnp.float32)
        hot_ref[...] = hot * alive[0:1].astype(jnp.bfloat16)

    misses = real_ref.shape[0]
    for part, out_ref in enumerate((real_ref, imag_ref)):
        picked = jnp.dot(traces_ref[part], hot_ref[...], preferred_element_type=jnp.float32)
        turned = picked.T * live_ref[0:1, :]
        out_ref[...] = turned[:misses].astype(jnp.bfloat16)


def pick_columns(traces, miss_lanes, recv8, live8, misses):
    _, rows, cols = traces.shape
    block = row_block(rows)
    return pl.pallas_call(
        pick_kernel,
        grid=(rows // block,),
        in_specs=[
            pl.BlockSpec((2, block, cols), lambda i: (0, i, 0)),
            pl.BlockSpec((1, LANES), lambda i: (0, 0)),
            pl.BlockSpec((8, cols), lambda i: (0, 0)),
            pl.BlockSpec((8, block), lambda i: (0, i)),
        ],
        out_specs=[pl.BlockSpec((misses, block), lambda i: (0, i))] * 2,
        out_shape=[jax.ShapeDtypeStruct((misses, rows), jnp.bfloat16)] * 2,
        scratch_shapes=[pltpu.VMEM((cols, LANES), jnp.bfloat16)],
        compiler_params=params(),
        cost_estimate=cost(4 * rows * cols * 2 * LANES, 4 * rows * cols),
        name="pick_columns",
    )(traces, miss_lanes, recv8, live8)


def fill_kernel(counts, first_half, real_ref, imag_ref, miss_ref, recv_ref, *refs):
    out_ref = refs[-1]
    rows = out_ref.shape[0]
    misses = real_ref.shape[0]
    hot = one_hot(miss_ref[...], rows, jnp.float32)
    dead = jnp.max(hot, axis=1, keepdims=True)
    hot = hot[:, :misses].astype(jnp.bfloat16)
    patches = halves(real_ref[...].astype(jnp.float32), imag_ref[...].astype(jnp.float32))
    mask = recv_ref[...].astype(jnp.float32)
    mask = halves(mask, mask)[0][0:1, :]
    used = 0
    for index, count in enumerate(counts):
        arrived = refs[used][...].astype(jnp.float32)
        for more in refs[used + 1:used + count]:
            arrived = arrived + more[...].astype(jnp.float32)
        used += count
        patch = patches[first_half + index].astype(jnp.bfloat16)
        moved = jnp.dot(hot, patch, preferred_element_type=jnp.float32)
        filled = arrived * ((1.0 - dead) * mask) + moved
        out_ref[:, index * WIN:(index + 1) * WIN] = filled.astype(jnp.bfloat16)


def fill_window(first_half, arrived, picked, miss_lanes, recv8):
    rows = arrived[0][0].shape[0]
    misses = picked[0].shape[0]
    counts = tuple(len(group) for group in arrived)
    flat = [part for group in arrived for part in group]
    lanes = len(counts) * WIN
    whole = pl.BlockSpec((rows, WIN), lambda i: (0, 0))
    return pl.pallas_call(
        functools.partial(fill_kernel, counts, first_half),
        grid=(1,),
        in_specs=[
            pl.BlockSpec((misses, WIN), lambda i: (0, 0)),
            pl.BlockSpec((misses, WIN), lambda i: (0, 0)),
            pl.BlockSpec((1, LANES), lambda i: (0, 0)),
            pl.BlockSpec((8, WIN), lambda i: (0, 0)),
        ]
        + [whole] * len(flat),
        out_specs=pl.BlockSpec((rows, lanes), lambda i: (0, 0)),
        out_shape=jax.ShapeDtypeStruct((rows, lanes), jnp.bfloat16),
        compiler_params=params(),
        cost_estimate=cost(4 * rows * LANES * lanes, 8 * rows * lanes),
        name="fill_window",
    )(*picked, miss_lanes, recv8, *flat)


def complex_rows(real_rows, imag_rows, right):
    first = jnp.dot(real_rows, right, preferred_element_type=jnp.float32)
    second = jnp.dot(imag_rows, right, preferred_element_type=jnp.float32)
    if CHUNKS == 1:
        real_part = first[:, :WIN] - second[:, WIN:]
        imag_part = first[:, WIN:] + second[:, :WIN]
        return jnp.concatenate([real_part, imag_part], axis=1)
    turned = pltpu.roll(second, WIDTH, 1)
    low = lax.broadcasted_iota(jnp.int32, first.shape, 1) < WIDTH
    return first + jnp.where(low, -turned, turned)


def choose(out_ref, pick, refs):
    for index, ref in enumerate(refs):

        @pl.when(pick == index)
        def _():
            out_ref[...] = ref[...]


def product_kernel(counts, pick_ref, recv_ref, *refs):
    tiles, refs = refs[:4], refs[4:]
    total, places = sum(counts), len(counts)
    out_refs, right_refs = refs[total:total + places], refs[total + places:-1]
    sem = refs[-1]

    @pl.when(pl.program_id(0) == 0)
    def _():
        used = 0
        for place, count in enumerate(counts):
            for index, ref in enumerate(refs[used:used + count]):

                @pl.when(pick_ref[place] == index)
                def _():
                    copy = pltpu.make_async_copy(ref, right_refs[place], sem.at[place])
                    copy.start()
                    copy.wait()

            used += count

    recv = recv_ref[0:1, :]
    half = tiles[0].shape[1]
    for side in range(2):
        real_rows, imag_rows = (tiles[2 * part + side][0] * recv for part in range(2))
        for out_ref, right_ref in zip(out_refs, right_refs):
            out_ref[side * half:(side + 1) * half, :] = complex_rows(
                real_rows, imag_rows, right_ref[...]
            )


def products(traces, recv8, groups):
    _, rows, cols = traces.shape
    lanes = groups[0][1][0].shape[1]
    counts = tuple(len(sources) for _, sources in groups)
    flat = [source for _, sources in groups for source in sources]
    picks = jnp.stack([pick for pick, _ in groups]).astype(jnp.int32)
    block = row_block(rows)
    quarter = lambda part, side: pl.BlockSpec(
        (1, block // 2, cols), lambda i: (part, 2 * i + side, 0)
    )
    return pl.pallas_call(
        functools.partial(product_kernel, counts),
        grid=(rows // block,),
        in_specs=[
            SMEM,
            pl.BlockSpec((8, cols), lambda i: (0, 0)),
        ]
        + [quarter(part, side) for part in range(2) for side in range(2)]
        + [pl.BlockSpec(memory_space=pl.ANY)] * len(flat),
        out_specs=[pl.BlockSpec((block, lanes), lambda i: (i, 0))] * len(groups),
        out_shape=[jax.ShapeDtypeStruct((rows, lanes), jnp.float32)] * len(groups),
        scratch_shapes=[pltpu.VMEM((cols, lanes), jnp.bfloat16)] * len(groups)
        + [pltpu.SemaphoreType.DMA((len(groups),))],
        compiler_params=params(),
        cost_estimate=cost(8 * rows * cols * lanes * len(groups), 4 * rows * lanes),
        name="products",
    )(picks, recv8, *[traces] * 4, *flat)


def extra_kernel(counts, pick_ref, real_ref, imag_ref, *refs):
    out_ref, right_ref = refs[-2:]
    used = 0
    for place, count in enumerate(counts):
        choose(right_ref, pick_ref[2 * place], refs[used:used + count])
        used += count
        out_ref[pick_ref[2 * place + 1]] = complex_rows(real_ref[...], imag_ref[...], right_ref[...])


def extra_products(rows, groups):
    misses, cols = rows[0].shape
    lanes = groups[0][2][0].shape[1]
    counts = tuple(len(sources) for _, _, sources in groups)
    flat = [source for _, _, sources in groups for source in sources]
    picks = jnp.stack([x for pick, place, _ in groups for x in (pick, place)]).astype(jnp.int32)
    return pl.pallas_call(
        functools.partial(extra_kernel, counts),
        in_specs=[SMEM] + [VMEM] * (2 + len(flat)),
        out_specs=VMEM,
        out_shape=jax.ShapeDtypeStruct((len(groups), misses, lanes), jnp.float32),
        scratch_shapes=[pltpu.VMEM((cols, lanes), jnp.bfloat16)],
        compiler_params=params(),
        cost_estimate=cost(8 * misses * cols * lanes * len(groups), 4 * cols * lanes),
        name="extra_products",
    )(picks, *rows, *flat)


def finish_kernel(wave_ref, miss_ref, recv_ref, tile_ref, real_ref, imag_ref, *refs):
    out_ref, row_ref = refs[-2:]
    totals = [ref[...] for ref in refs[:-2]]

    def write(target, window, chunks):
        real_part, imag_part = unpack(chunks)
        real_pred = real_part * wave_ref[0] - imag_part * wave_ref[1]
        imag_pred = imag_part * wave_ref[0] + real_part * wave_ref[1]
        target[0] = window[0] - real_pred
        target[1] = window[1] - imag_pred

    recv = recv_ref[0:1, :].astype(jnp.float32)
    write(out_ref, [tile_ref[part].astype(jnp.float32) * recv for part in range(2)], totals[:CHUNKS])
    write(row_ref, [ref[...].astype(jnp.float32) for ref in (real_ref, imag_ref)], totals[CHUNKS:])

    def place(m, carry):
        for part in range(2):
            out_ref[part, pl.ds(miss_ref[m], 1), :] = row_ref[part, pl.ds(m, 1), :]
        return carry

    lax.fori_loop(0, row_ref.shape[1], place, 0, unroll=8)


def finish(wave, miss, recv8, traces, extra, terms):
    _, rows, _ = traces.shape
    misses = extra[0].shape[0]
    flat = [term for group in terms for term in group]
    window = lambda size: pl.BlockSpec((2, size, WIN), lambda i: (0, 0, 0))
    return pl.pallas_call(
        finish_kernel,
        grid=(1,),
        in_specs=[SMEM, SMEM, pl.BlockSpec((8, WIN), lambda i: (0, 0)), window(rows)]
        + [pl.BlockSpec((misses, WIN), lambda i: (0, 0))] * 2
        + [VMEM] * len(flat),
        out_specs=window(rows),
        out_shape=jax.ShapeDtypeStruct((2, rows, WIN), jnp.float32),
        scratch_shapes=[pltpu.VMEM((2, misses, WIN), jnp.float32)],
        compiler_params=params(),
        cost_estimate=cost(20 * rows * WIN, 40 * rows * WIN),
        name="finish",
    )(wave, miss, recv8, traces, *extra, *flat)


def mirror_routes(grid_size):
    cells = [(a, b) for a in range(grid_size) for b in range(grid_size)]
    index = lambda row, col: row * grid_size + col
    whole = [(index(a, b), index(b, a)) for a, b in cells]
    near = [(index(a, b), index(b, a)) for a, b in cells if a // 2 == b // 2]
    far = [(a, b) for a, b in cells if a // 2 != b // 2]
    hop = lambda a, b: index(a, a // 2 * 2 + b % 2)
    first = [(index(a, b), hop(a, b)) for a, b in far]
    second = [(hop(a, b), index(b, a)) for a, b in far]
    if len({target for _, target in first}) < len(first):
        return whole, None
    return whole, (near, first, second)


def sources_of(up, down, offset, grid_size, row_index):
    places, sources = [], []
    for row in range(grid_size):
        other = row ^ offset
        source = up[row - other] if other < row else down[other - row]
        known = [index for index, seen in enumerate(sources) if seen is source]
        places.append(known[0] if known else len(sources))
        if not known:
            sources.append(source)
    pick = jnp.zeros((), jnp.int32)
    for row, place in enumerate(places):
        pick = jnp.where(row_index == row, place, pick)
    return pick, sources


def sum_route(offset, grid_size, stride, skip):
    route = []
    for row in range(grid_size):
        for col in range(grid_size):
            if ((col ^ row ^ offset) & ~skip) % (2 * stride) == stride:
                route.append((row * grid_size + col, row * grid_size + (col ^ stride)))
    return route


def local(traces, recv_live, missing, wavelet):
    tile = traces.shape[1]
    grid_size = lax.axis_size("row")
    misses = missing.shape[1]
    order = recv_live.shape[0]
    row_index = lax.axis_index("row")
    col_index = lax.axis_index("col")
    whole, hops = mirror_routes(grid_size)

    def move(block, route):
        return lax.ppermute(block, ("row", "col"), route)

    def transpose(block):
        return move(block, whole)

    def transpose_round(block):
        if hops is None:
            return [move(block, whole)]
        near, first, second = hops
        return [move(move(block, first), second), move(block, near)]

    direct, round_about = cut_window(traces)
    arrived = [[transpose(direct)], transpose_round(round_about)]
    if CHUNKS == 1:
        arrived = [arrived]
    else:
        arrived = [arrived[:1], arrived[1:]]

    miss_row = lax.dynamic_index_in_dim(missing, row_index, 0, keepdims=False)
    miss_col = lax.dynamic_index_in_dim(missing, col_index, 0, keepdims=False)
    as_lanes = lambda m: jnp.pad(m, (0, LANES - misses), constant_values=-1)[None]
    miss_col_lanes = as_lanes(miss_col)
    positions = jnp.arange(tile, dtype=jnp.int32)
    live_row = jnp.all(positions[:, None] != miss_row[None, :], axis=1)
    live8 = jnp.broadcast_to(live_row.astype(jnp.float32)[None], (8, tile))
    recv_mask = (recv_live == 1).astype(jnp.bfloat16)
    recv_row = lax.dynamic_slice_in_dim(recv_mask, row_index * tile, WIN)
    recv_row8 = jnp.broadcast_to(recv_row[None], (8, WIN))
    recv_col = lax.dynamic_slice_in_dim(recv_mask, col_index * tile, tile)
    recv_col8 = jnp.broadcast_to(recv_col[None], (8, tile))

    picked = pick_columns(traces, miss_col_lanes, recv_col8, live8, misses)
    both = transpose(jnp.concatenate(picked))
    extra = [both[:misses], both[misses:]]
    apart = row_index ^ col_index
    strides = [2**bit for bit in range(grid_size.bit_length() - 1)]
    terms, extra_terms = [], []
    for chunk in range(CHUNKS):
        window = fill_window(chunk, arrived[chunk], picked, miss_col_lanes, recv_row8)
        up, down = [window], [window]
        sums = []

        def hop(distance):
            ends = [(i, i + 1) for i in range(distance - 1, grid_size - 1)]
            back = [(i + 1, i) for i in range(grid_size - distance)]
            up.append(lax.ppermute(up[-1], "row", ends))
            down.append(lax.ppermute(down[-1], "row", back))

        def add_up(total, offset, strides, skip):
            for stride in strides:
                total = total + move(total, sum_route(offset, grid_size, stride, skip))
            return total

        def shrink(total):
            unit = jnp.maximum(jnp.max(jnp.abs(total)), TINY) * (1.0 / HALF_TOP)
            sent = (total * (1.0 / unit)).astype(jnp.float16)
            return sent, jnp.broadcast_to(unit, (1, LANES))

        def last(shrunk, offset, skip):
            route = sum_route(offset, grid_size, strides[-1], skip)
            return [move(part, route) for part in shrunk]

        def options(offset):
            return sources_of(up, down, offset, grid_size, row_index)

        hop(1)
        extra, up[-1], down[-1] = lax.optimization_barrier((extra, up[-1], down[-1]))
        hop(2)
        other_core = [(i, i ^ 1) for i in range(grid_size)]
        odd = apart & 1

        def pair_sum(first, mask):
            pick0, sources0 = options(first)
            pick1, sources1 = options(first + 1)
            pick1 = pick1 + len(sources0)
            both_sources = sources0 + sources1
            keep, sent = products(
                traces,
                mask,
                [
                    (jnp.where(odd == 1, pick1, pick0), both_sources),
                    (jnp.where(odd == 1, pick0, pick1), both_sources),
                ],
            )
            return add_up(keep + lax.ppermute(sent, "col", other_core), first, strides[1:-1], 1)

        sums = [pair_sum(0, recv_col8)]
        shrunk, up[-1], down[-1] = lax.optimization_barrier((shrink(sums[0]), up[-1], down[-1]))
        for distance in range(3, grid_size):
            hop(distance)
        got = [last(shrunk, 0, 1)]
        mask = recv_col8
        for first in range(2, grid_size, 2):
            if first == grid_size - 2:
                group = [(pick, apart ^ offset, sources) for offset in range(grid_size)
                         for pick, sources in [options(offset)]]
                rest = extra_products(extra, group)
                mask, got[0], rest = lax.optimization_barrier((mask, got[0], rest))
            sums.append(pair_sum(first, mask))
            got.append(last(shrink(sums[-1]), first, 1))
        whole_sum = None
        for index, (part, (sent, units)) in enumerate(zip(sums, got)):
            mine = apart // 2 == index
            term = jnp.where(mine, part, 0.0) + sent.astype(jnp.float32) * units[0, 0]
            whole_sum = term if whole_sum is None else whole_sum + term
        terms.append((whole_sum,))
        for stride in strides:
            pairs = [(i, i ^ stride) for i in range(grid_size)]
            arrive = lax.ppermute(rest[1::2], "col", pairs)
            rest = rest[0::2] + arrive
        extra_terms.append((rest[0],))
    wave = wavelet * (1.0 / math.sqrt(order))
    return finish(wave, miss_row, recv_col8, traces, extra, terms + extra_terms)


def solution(mesh):
    in_specs = (P("freq", "row", "col"), P("freq"), P("freq", None), P("freq"))
    out_specs = P("freq", "row", "col")
    return jax.shard_map(local, mesh=mesh, in_specs=in_specs, out_specs=out_specs, check_vma=False)
```

```python
import functools
import math

import jax
import jax.numpy as jnp
from jax import lax
from jax.experimental import pallas as pl
from jax.experimental.pallas import tpu as pltpu
from jax.sharding import PartitionSpec as P

WIN = 128
LANES = 128
CHUNKS = 1
WIDTH = WIN // CHUNKS
TINY = 1e-30
HALF_TOP = 32768.0
VMEM_LIMIT = 48 * 2**20
VMEM = pl.BlockSpec(memory_space=pltpu.VMEM)
SMEM = pl.BlockSpec(memory_space=pltpu.SMEM)


def params():
    return pltpu.CompilerParams(vmem_limit_bytes=VMEM_LIMIT)


def cost(flops, accessed):
    return pl.CostEstimate(
        flops=int(flops) // 64, bytes_accessed=int(accessed) // 64, transcendentals=0
    )


def row_block(rows):
    for size in (512, 384, 256, 128):
        if rows % size == 0:
            return size
    return rows


def one_hot(positions_row, rows, dtype):
    lanes = positions_row.shape[1]
    row_ids = lax.broadcasted_iota(jnp.int32, (rows, lanes), 0)
    return jnp.where(row_ids == positions_row, 1.0, 0.0).astype(dtype)


def pack(real_part, imag_part):
    if CHUNKS == 1:
        return [jnp.concatenate([real_part, imag_part], axis=1)]
    first = lax.broadcasted_iota(jnp.int32, real_part.shape, 1) < WIDTH
    low = jnp.where(first, real_part, pltpu.roll(imag_part, WIDTH, 1))
    high = jnp.where(first, pltpu.roll(real_part, WIDTH, 1), imag_part)
    return [low, high]


def unpack(chunks):
    if CHUNKS == 1:
        return chunks[0][:, :WIN], chunks[0][:, WIN:]
    low, high = chunks
    first = lax.broadcasted_iota(jnp.int32, low.shape, 1) < WIDTH
    real_part = jnp.where(first, low, pltpu.roll(high, WIDTH, 1))
    imag_part = jnp.where(first, pltpu.roll(low, WIDTH, 1), high)
    return real_part, imag_part


def halves(real_part, imag_part):
    return [real_part, imag_part] if CHUNKS == 1 else pack(real_part, imag_part)


def cut_kernel(traces_ref, *out_refs):
    parts = halves(traces_ref[0].astype(jnp.float32), traces_ref[1].astype(jnp.float32))
    for out_ref, part in zip(out_refs, parts):
        out_ref[...] = part.astype(jnp.bfloat16)


def cut_window(traces):
    rows = traces.shape[1]
    return pl.pallas_call(
        cut_kernel,
        grid=(1,),
        in_specs=[pl.BlockSpec((2, rows, WIN), lambda i: (0, 0, 0))],
        out_specs=[pl.BlockSpec((rows, WIN), lambda i: (0, 0))] * 2,
        out_shape=[jax.ShapeDtypeStruct((rows, WIN), jnp.bfloat16)] * 2,
        compiler_params=params(),
        cost_estimate=cost(rows * WIN, 8 * rows * WIN),
        name="cut_window",
    )(traces)


def pick_kernel(traces_ref, miss_ref, recv_ref, live_ref, real_ref, imag_ref, hot_ref):
    @pl.when(pl.program_id(0) == 0)
    def _():
        hot = one_hot(miss_ref[...], hot_ref.shape[0], jnp.bfloat16)
        alive = jnp.dot(recv_ref[...], hot, preferred_element_type=jnp.float32)
        hot_ref[...] = hot * alive[0:1].astype(jnp.bfloat16)

    misses = real_ref.shape[0]
    for part, out_ref in enumerate((real_ref, imag_ref)):
        picked = jnp.dot(traces_ref[part], hot_ref[...], preferred_element_type=jnp.float32)
        turned = picked.T * live_ref[0:1, :]
        out_ref[...] = turned[:misses].astype(jnp.bfloat16)


def pick_columns(traces, miss_lanes, recv8, live8, misses):
    _, rows, cols = traces.shape
    block = row_block(rows)
    return pl.pallas_call(
        pick_kernel,
        grid=(rows // block,),
        in_specs=[
            pl.BlockSpec((2, block, cols), lambda i: (0, i, 0)),
            pl.BlockSpec((1, LANES), lambda i: (0, 0)),
            pl.BlockSpec((8, cols), lambda i: (0, 0)),
            pl.BlockSpec((8, block), lambda i: (0, i)),
        ],
        out_specs=[pl.BlockSpec((misses, block), lambda i: (0, i))] * 2,
        out_shape=[jax.ShapeDtypeStruct((misses, rows), jnp.bfloat16)] * 2,
        scratch_shapes=[pltpu.VMEM((cols, LANES), jnp.bfloat16)],
        compiler_params=params(),
        cost_estimate=cost(4 * rows * cols * 2 * LANES, 4 * rows * cols),
        name="pick_columns",
    )(traces, miss_lanes, recv8, live8)


def fill_kernel(counts, first_half, real_ref, imag_ref, miss_ref, recv_ref, *refs):
    out_ref = refs[-1]
    rows = out_ref.shape[0]
    misses = real_ref.shape[0]
    hot = one_hot(miss_ref[...], rows, jnp.float32)
    dead = jnp.max(hot, axis=1, keepdims=True)
    hot = hot[:, :misses].astype(jnp.bfloat16)
    patches = halves(real_ref[...].astype(jnp.float32), imag_ref[...].astype(jnp.float32))
    mask = recv_ref[...].astype(jnp.float32)
    mask = halves(mask, mask)[0][0:1, :]
    used = 0
    for index, count in enumerate(counts):
        arrived = refs[used][...].astype(jnp.float32)
        for more in refs[used + 1:used + count]:
            arrived = arrived + more[...].astype(jnp.float32)
        used += count
        patch = patches[first_half + index].astype(jnp.bfloat16)
        moved = jnp.dot(hot, patch, preferred_element_type=jnp.float32)
        filled = arrived * ((1.0 - dead) * mask) + moved
        out_ref[:, index * WIN:(index + 1) * WIN] = filled.astype(jnp.bfloat16)


def fill_window(first_half, arrived, picked, miss_lanes, recv8):
    rows = arrived[0][0].shape[0]
    misses = picked[0].shape[0]
    counts = tuple(len(group) for group in arrived)
    flat = [part for group in arrived for part in group]
    lanes = len(counts) * WIN
    whole = pl.BlockSpec((rows, WIN), lambda i: (0, 0))
    return pl.pallas_call(
        functools.partial(fill_kernel, counts, first_half),
        grid=(1,),
        in_specs=[
            pl.BlockSpec((misses, WIN), lambda i: (0, 0)),
            pl.BlockSpec((misses, WIN), lambda i: (0, 0)),
            pl.BlockSpec((1, LANES), lambda i: (0, 0)),
            pl.BlockSpec((8, WIN), lambda i: (0, 0)),
        ]
        + [whole] * len(flat),
        out_specs=pl.BlockSpec((rows, lanes), lambda i: (0, 0)),
        out_shape=jax.ShapeDtypeStruct((rows, lanes), jnp.bfloat16),
        compiler_params=params(),
        cost_estimate=cost(4 * rows * LANES * lanes, 8 * rows * lanes),
        name="fill_window",
    )(*picked, miss_lanes, recv8, *flat)


def complex_rows(real_rows, imag_rows, right):
    first = jnp.dot(real_rows, right, preferred_element_type=jnp.float32)
    second = jnp.dot(imag_rows, right, preferred_element_type=jnp.float32)
    if CHUNKS == 1:
        real_part = first[:, :WIN] - second[:, WIN:]
        imag_part = first[:, WIN:] + second[:, :WIN]
        return jnp.concatenate([real_part, imag_part], axis=1)
    turned = pltpu.roll(second, WIDTH, 1)
    low = lax.broadcasted_iota(jnp.int32, first.shape, 1) < WIDTH
    return first + jnp.where(low, -turned, turned)


def choose(out_ref, pick, refs):
    for index, ref in enumerate(refs):

        @pl.when(pick == index)
        def _():
            out_ref[...] = ref[...]


def product_kernel(counts, pick_ref, recv_ref, *refs):
    tiles, refs = refs[:4], refs[4:]
    total, places = sum(counts), len(counts)
    out_refs, right_refs = refs[total:total + places], refs[total + places:-1]
    sem = refs[-1]

    @pl.when(pl.program_id(0) == 0)
    def _():
        used = 0
        for place, count in enumerate(counts):
            for index, ref in enumerate(refs[used:used + count]):

                @pl.when(pick_ref[place] == index)
                def _():
                    copy = pltpu.make_async_copy(ref, right_refs[place], sem.at[place])
                    copy.start()
                    copy.wait()

            used += count

    recv = recv_ref[0:1, :]
    half = tiles[0].shape[1]
    for side in range(2):
        real_rows, imag_rows = (tiles[2 * part + side][0] * recv for part in range(2))
        for out_ref, right_ref in zip(out_refs, right_refs):
            out_ref[side * half:(side + 1) * half, :] = complex_rows(
                real_rows, imag_rows, right_ref[...]
            )


def products(traces, recv8, groups):
    _, rows, cols = traces.shape
    lanes = groups[0][1][0].shape[1]
    counts = tuple(len(sources) for _, sources in groups)
    flat = [source for _, sources in groups for source in sources]
    picks = jnp.stack([pick for pick, _ in groups]).astype(jnp.int32)
    block = row_block(rows)
    quarter = lambda part, side: pl.BlockSpec(
        (1, block // 2, cols), lambda i: (part, 2 * i + side, 0)
    )
    return pl.pallas_call(
        functools.partial(product_kernel, counts),
        grid=(rows // block,),
        in_specs=[
            SMEM,
            pl.BlockSpec((8, cols), lambda i: (0, 0)),
        ]
        + [quarter(part, side) for part in range(2) for side in range(2)]
        + [pl.BlockSpec(memory_space=pl.ANY)] * len(flat),
        out_specs=[pl.BlockSpec((block, lanes), lambda i: (i, 0))] * len(groups),
        out_shape=[jax.ShapeDtypeStruct((rows, lanes), jnp.float32)] * len(groups),
        scratch_shapes=[pltpu.VMEM((cols, lanes), jnp.bfloat16)] * len(groups)
        + [pltpu.SemaphoreType.DMA((len(groups),))],
        compiler_params=params(),
        cost_estimate=cost(8 * rows * cols * lanes * len(groups), 4 * rows * lanes),
        name="products",
    )(picks, recv8, *[traces] * 4, *flat)


def extra_kernel(counts, pick_ref, real_ref, imag_ref, *refs):
    out_ref, right_ref = refs[-2:]
    used = 0
    for place, count in enumerate(counts):
        choose(right_ref, pick_ref[2 * place], refs[used:used + count])
        used += count
        out_ref[pick_ref[2 * place + 1]] = complex_rows(real_ref[...], imag_ref[...], right_ref[...])


def extra_products(rows, groups):
    misses, cols = rows[0].shape
    lanes = groups[0][2][0].shape[1]
    counts = tuple(len(sources) for _, _, sources in groups)
    flat = [source for _, _, sources in groups for source in sources]
    picks = jnp.stack([x for pick, place, _ in groups for x in (pick, place)]).astype(jnp.int32)
    return pl.pallas_call(
        functools.partial(extra_kernel, counts),
        in_specs=[SMEM] + [VMEM] * (2 + len(flat)),
        out_specs=VMEM,
        out_shape=jax.ShapeDtypeStruct((len(groups), misses, lanes), jnp.float32),
        scratch_shapes=[pltpu.VMEM((cols, lanes), jnp.bfloat16)],
        compiler_params=params(),
        cost_estimate=cost(8 * misses * cols * lanes * len(groups), 4 * cols * lanes),
        name="extra_products",
    )(picks, *rows, *flat)


def finish_kernel(wave_ref, miss_ref, recv_ref, tile_ref, real_ref, imag_ref, *refs):
    out_ref, row_ref = refs[-2:]
    totals = [ref[...] for ref in refs[:-2]]

    def write(target, window, chunks):
        real_part, imag_part = unpack(chunks)
        real_pred = real_part * wave_ref[0] - imag_part * wave_ref[1]
        imag_pred = imag_part * wave_ref[0] + real_part * wave_ref[1]
        target[0] = window[0] - real_pred
        target[1] = window[1] - imag_pred

    recv = recv_ref[0:1, :].astype(jnp.float32)
    write(out_ref, [tile_ref[part].astype(jnp.float32) * recv for part in range(2)], totals[:CHUNKS])
    write(row_ref, [ref[...].astype(jnp.float32) for ref in (real_ref, imag_ref)], totals[CHUNKS:])

    def place(m, carry):
        for part in range(2):
            out_ref[part, pl.ds(miss_ref[m], 1), :] = row_ref[part, pl.ds(m, 1), :]
        return carry

    lax.fori_loop(0, row_ref.shape[1], place, 0, unroll=8)


def finish(wave, miss, recv8, traces, extra, terms):
    _, rows, _ = traces.shape
    misses = extra[0].shape[0]
    flat = [term for group in terms for term in group]
    window = lambda size: pl.BlockSpec((2, size, WIN), lambda i: (0, 0, 0))
    return pl.pallas_call(
        finish_kernel,
        grid=(1,),
        in_specs=[SMEM, SMEM, pl.BlockSpec((8, WIN), lambda i: (0, 0)), window(rows)]
        + [pl.BlockSpec((misses, WIN), lambda i: (0, 0))] * 2
        + [VMEM] * len(flat),
        out_specs=window(rows),
        out_shape=jax.ShapeDtypeStruct((2, rows, WIN), jnp.float32),
        scratch_shapes=[pltpu.VMEM((2, misses, WIN), jnp.float32)],
        compiler_params=params(),
        cost_estimate=cost(20 * rows * WIN, 40 * rows * WIN),
        name="finish",
    )(wave, miss, recv8, traces, *extra, *flat)


def mirror_routes(grid_size):
    cells = [(a, b) for a in range(grid_size) for b in range(grid_size)]
    index = lambda row, col: row * grid_size + col
    whole = [(index(a, b), index(b, a)) for a, b in cells]
    near = [(index(a, b), index(b, a)) for a, b in cells if a // 2 == b // 2]
    far = [(a, b) for a, b in cells if a // 2 != b // 2]
    hop = lambda a, b: index(a, a // 2 * 2 + b % 2)
    first = [(index(a, b), hop(a, b)) for a, b in far]
    second = [(hop(a, b), index(b, a)) for a, b in far]
    if len({target for _, target in first}) < len(first):
        return whole, None
    return whole, (near, first, second)


def sources_of(up, down, offset, grid_size, row_index):
    places, sources = [], []
    for row in range(grid_size):
        other = row ^ offset
        source = up[row - other] if other < row else down[other - row]
        known = [index for index, seen in enumerate(sources) if seen is source]
        places.append(known[0] if known else len(sources))
        if not known:
            sources.append(source)
    pick = jnp.zeros((), jnp.int32)
    for row, place in enumerate(places):
        pick = jnp.where(row_index == row, place, pick)
    return pick, sources


def sum_route(offset, grid_size, stride, skip):
    route = []
    for row in range(grid_size):
        for col in range(grid_size):
            if ((col ^ row ^ offset) & ~skip) % (2 * stride) == stride:
                route.append((row * grid_size + col, row * grid_size + (col ^ stride)))
    return route


def local(traces, recv_live, missing, wavelet):
    tile = traces.shape[1]
    grid_size = lax.axis_size("row")
    misses = missing.shape[1]
    order = recv_live.shape[0]
    row_index = lax.axis_index("row")
    col_index = lax.axis_index("col")
    whole, hops = mirror_routes(grid_size)

    def move(block, route):
        return lax.ppermute(block, ("row", "col"), route)

    def transpose(block):
        return move(block, whole)

    def rounds(block):
        if hops is None:
            return [move(block, whole)], None
        return [move(block, hops[0])], move(block, hops[1])

    def arrive_round(near, half_way):
        return near if half_way is None else near + [move(half_way, hops[2])]

    direct, round_about = cut_window(traces)
    first_arrival = transpose(direct)
    near, half_way = rounds(round_about)
    miss_row = lax.dynamic_index_in_dim(missing, row_index, 0, keepdims=False)
    miss_col = lax.dynamic_index_in_dim(missing, col_index, 0, keepdims=False)
    as_lanes = lambda m: jnp.pad(m, (0, LANES - misses), constant_values=-1)[None]
    miss_col_lanes = as_lanes(miss_col)
    positions = jnp.arange(tile, dtype=jnp.int32)
    live_row = jnp.all(positions[:, None] != miss_row[None, :], axis=1)
    live8 = jnp.broadcast_to(live_row.astype(jnp.float32)[None], (8, tile))
    recv_mask = (recv_live == 1).astype(jnp.bfloat16)
    recv_row = lax.dynamic_slice_in_dim(recv_mask, row_index * tile, WIN)
    recv_row8 = jnp.broadcast_to(recv_row[None], (8, WIN))
    recv_col = lax.dynamic_slice_in_dim(recv_mask, col_index * tile, tile)
    recv_col8 = jnp.broadcast_to(recv_col[None], (8, tile))

    picked = pick_columns(traces, miss_col_lanes, recv_col8, live8, misses)
    if half_way is not None:
        picked, half_way = lax.optimization_barrier((picked, half_way))
    arrived = [[first_arrival], arrive_round(near, half_way)]
    arrived = [arrived] if CHUNKS == 1 else [arrived[:1], arrived[1:]]
    extra = [transpose(picked[0]), functools.reduce(jnp.add, arrive_round(*rounds(picked[1])))]
    apart = row_index ^ col_index
    strides = [2**bit for bit in range(grid_size.bit_length() - 1)]
    terms, extra_terms = [], []
    for chunk in range(CHUNKS):
        window = fill_window(chunk, arrived[chunk], picked, miss_col_lanes, recv_row8)
        up, down = [window], [window]
        sums = []

        def hop(distance):
            ends = [(i, i + 1) for i in range(distance - 1, grid_size - 1)]
            back = [(i + 1, i) for i in range(grid_size - distance)]
            up.append(lax.ppermute(up[-1], "row", ends))
            down.append(lax.ppermute(down[-1], "row", back))

        def add_up(total, offset, strides, skip):
            for stride in strides:
                total = total + move(total, sum_route(offset, grid_size, stride, skip))
            return total

        def shrink(total):
            unit = jnp.maximum(jnp.max(jnp.abs(total)), TINY) * (1.0 / HALF_TOP)
            sent = (total * (1.0 / unit)).astype(jnp.float16)
            return sent, jnp.broadcast_to(unit, (1, LANES))

        def last(shrunk, offset, skip):
            route = sum_route(offset, grid_size, strides[-1], skip)
            return [move(part, route) for part in shrunk]

        def options(offset):
            return sources_of(up, down, offset, grid_size, row_index)

        hop(1)
        extra, up[-1], down[-1] = lax.optimization_barrier((extra, up[-1], down[-1]))
        hop(2)
        other_core = [(i, i ^ 1) for i in range(grid_size)]
        odd = apart & 1

        def pair_sum(first, mask):
            pick0, sources0 = options(first)
            pick1, sources1 = options(first + 1)
            pick1 = pick1 + len(sources0)
            both_sources = sources0 + sources1
            keep, sent = products(
                traces,
                mask,
                [
                    (jnp.where(odd == 1, pick1, pick0), both_sources),
                    (jnp.where(odd == 1, pick0, pick1), both_sources),
                ],
            )
            return add_up(keep + lax.ppermute(sent, "col", other_core), first, strides[1:-1], 1)

        sums = [pair_sum(0, recv_col8)]
        shrunk, up[-1], down[-1] = lax.optimization_barrier((shrink(sums[0]), up[-1], down[-1]))
        for distance in range(3, grid_size):
            hop(distance)
        got = [last(shrunk, 0, 1)]
        mask = recv_col8
        for first in range(2, grid_size, 2):
            if first == grid_size - 2:
                group = [(pick, apart ^ offset, sources) for offset in range(grid_size)
                         for pick, sources in [options(offset)]]
                rest = extra_products(extra, group)
                mask, got[0], rest = lax.optimization_barrier((mask, got[0], rest))
            sums.append(pair_sum(first, mask))
            got.append(last(shrink(sums[-1]), first, 1))
        whole_sum = None
        for index, (part, (sent, units)) in enumerate(zip(sums, got)):
            mine = apart // 2 == index
            term = jnp.where(mine, part, 0.0) + sent.astype(jnp.float32) * units[0, 0]
            whole_sum = term if whole_sum is None else whole_sum + term
        terms.append((whole_sum,))
        for stride in strides:
            pairs = [(i, i ^ stride) for i in range(grid_size)]
            arrive = lax.ppermute(rest[1::2], "col", pairs)
            rest = rest[0::2] + arrive
        extra_terms.append((rest[0],))
    wave = wavelet * (1.0 / math.sqrt(order))
    return finish(wave, miss_row, recv_col8, traces, extra, terms + extra_terms)


def solution(mesh):
    in_specs = (P("freq", "row", "col"), P("freq"), P("freq", None), P("freq"))
    out_specs = P("freq", "row", "col")
    return jax.shard_map(local, mesh=mesh, in_specs=in_specs, out_specs=out_specs, check_vma=False)
```

```python
import functools
import math

import jax
import jax.numpy as jnp
from jax import lax
from jax.experimental import pallas as pl
from jax.experimental.pallas import tpu as pltpu
from jax.sharding import PartitionSpec as P

WIN = 128
LANES = 128
CHUNKS = 1
WIDTH = WIN // CHUNKS
TINY = 1e-30
HALF_TOP = 32768.0
VMEM_LIMIT = 48 * 2**20
VMEM = pl.BlockSpec(memory_space=pltpu.VMEM)
SMEM = pl.BlockSpec(memory_space=pltpu.SMEM)


def params():
    return pltpu.CompilerParams(vmem_limit_bytes=VMEM_LIMIT)


def cost(flops, accessed):
    return pl.CostEstimate(
        flops=int(flops) // 64, bytes_accessed=int(accessed) // 64, transcendentals=0
    )


def row_block(rows):
    for size in (512, 384, 256, 128):
        if rows % size == 0:
            return size
    return rows


def one_hot(positions_row, rows, dtype):
    lanes = positions_row.shape[1]
    row_ids = lax.broadcasted_iota(jnp.int32, (rows, lanes), 0)
    return jnp.where(row_ids == positions_row, 1.0, 0.0).astype(dtype)


def pack(real_part, imag_part):
    if CHUNKS == 1:
        return [jnp.concatenate([real_part, imag_part], axis=1)]
    first = lax.broadcasted_iota(jnp.int32, real_part.shape, 1) < WIDTH
    low = jnp.where(first, real_part, pltpu.roll(imag_part, WIDTH, 1))
    high = jnp.where(first, pltpu.roll(real_part, WIDTH, 1), imag_part)
    return [low, high]


def unpack(chunks):
    if CHUNKS == 1:
        return chunks[0][:, :WIN], chunks[0][:, WIN:]
    low, high = chunks
    first = lax.broadcasted_iota(jnp.int32, low.shape, 1) < WIDTH
    real_part = jnp.where(first, low, pltpu.roll(high, WIDTH, 1))
    imag_part = jnp.where(first, pltpu.roll(low, WIDTH, 1), high)
    return real_part, imag_part


def cut_kernel(traces_ref, direct_ref, rest_ref):
    rows = traces_ref.shape[1]
    top = rows - rest_ref.shape[0]
    direct_ref[:rows] = traces_ref[0]
    direct_ref[rows:] = traces_ref[1, :top]
    rest_ref[...] = traces_ref[1, top:]


def cut_window(traces):
    rows = traces.shape[1]
    rest = rows // 3 * 2
    sizes = (2 * rows - rest, rest)
    return pl.pallas_call(
        cut_kernel,
        grid=(1,),
        in_specs=[pl.BlockSpec((2, rows, WIN), lambda i: (0, 0, 0))],
        out_specs=[pl.BlockSpec((size, WIN), lambda i: (0, 0)) for size in sizes],
        out_shape=[jax.ShapeDtypeStruct((size, WIN), jnp.bfloat16) for size in sizes],
        compiler_params=params(),
        cost_estimate=cost(rows * WIN, 8 * rows * WIN),
        name="cut_window",
    )(traces)


def pick_kernel(traces_ref, miss_ref, recv_ref, live_ref, real_ref, imag_ref, hot_ref):
    @pl.when(pl.program_id(0) == 0)
    def _():
        hot = one_hot(miss_ref[...], hot_ref.shape[0], jnp.bfloat16)
        alive = jnp.dot(recv_ref[...], hot, preferred_element_type=jnp.float32)
        hot_ref[...] = hot * alive[0:1].astype(jnp.bfloat16)

    misses = real_ref.shape[0]
    for part, out_ref in enumerate((real_ref, imag_ref)):
        picked = jnp.dot(traces_ref[part], hot_ref[...], preferred_element_type=jnp.float32)
        turned = picked.T * live_ref[0:1, :]
        out_ref[...] = turned[:misses].astype(jnp.bfloat16)


def pick_columns(traces, miss_lanes, recv8, live8, misses):
    _, rows, cols = traces.shape
    block = row_block(rows)
    return pl.pallas_call(
        pick_kernel,
        grid=(rows // block,),
        in_specs=[
            pl.BlockSpec((2, block, cols), lambda i: (0, i, 0)),
            pl.BlockSpec((1, LANES), lambda i: (0, 0)),
            pl.BlockSpec((8, cols), lambda i: (0, 0)),
            pl.BlockSpec((8, block), lambda i: (0, i)),
        ],
        out_specs=[pl.BlockSpec((misses, block), lambda i: (0, i))] * 2,
        out_shape=[jax.ShapeDtypeStruct((misses, rows), jnp.bfloat16)] * 2,
        scratch_shapes=[pltpu.VMEM((cols, LANES), jnp.bfloat16)],
        compiler_params=params(),
        cost_estimate=cost(4 * rows * cols * 2 * LANES, 4 * rows * cols),
        name="pick_columns",
    )(traces, miss_lanes, recv8, live8)


def fill_kernel(real_ref, imag_ref, miss_ref, recv_ref, direct_ref, *refs):
    rest_refs, out_ref = refs[:-1], refs[-1]
    rows = out_ref.shape[0]
    misses = real_ref.shape[0]
    hot = one_hot(miss_ref[...], rows, jnp.float32)
    keep = (1.0 - jnp.max(hot, axis=1, keepdims=True)) * recv_ref[0:1, :].astype(jnp.float32)
    hot = hot[:, :misses].astype(jnp.bfloat16)
    rest = rest_refs[0][...].astype(jnp.float32)
    for more in rest_refs[1:]:
        rest = rest + more[...].astype(jnp.float32)
    direct = direct_ref[...].astype(jnp.float32)
    arrived = [direct[:rows], jnp.concatenate([direct[rows:], rest], axis=0)]
    for part, patch_ref in enumerate((real_ref, imag_ref)):
        moved = jnp.dot(hot, patch_ref[...], preferred_element_type=jnp.float32)
        filled = arrived[part] * keep + moved
        out_ref[:, part * WIN:(part + 1) * WIN] = filled.astype(jnp.bfloat16)


def fill_window(direct, rest, picked, miss_lanes, recv8):
    misses = picked[0].shape[0]
    whole = lambda array: pl.BlockSpec(array.shape, lambda i: (0, 0))
    patch = pl.BlockSpec((misses, WIN), lambda i: (0, 0))
    rows = (direct.shape[0] + rest[0].shape[0]) // 2
    return pl.pallas_call(
        fill_kernel,
        grid=(1,),
        in_specs=[patch, patch, whole(miss_lanes), whole(recv8), whole(direct)]
        + [whole(piece) for piece in rest],
        out_specs=pl.BlockSpec((rows, 2 * WIN), lambda i: (0, 0)),
        out_shape=jax.ShapeDtypeStruct((rows, 2 * WIN), jnp.bfloat16),
        compiler_params=params(),
        cost_estimate=cost(8 * rows * LANES * WIN, 16 * rows * WIN),
        name="fill_window",
    )(*picked, miss_lanes, recv8, direct, *rest)


def complex_rows(real_rows, imag_rows, right):
    first = jnp.dot(real_rows, right, preferred_element_type=jnp.float32)
    second = jnp.dot(imag_rows, right, preferred_element_type=jnp.float32)
    if CHUNKS == 1:
        real_part = first[:, :WIN] - second[:, WIN:]
        imag_part = first[:, WIN:] + second[:, :WIN]
        return jnp.concatenate([real_part, imag_part], axis=1)
    turned = pltpu.roll(second, WIDTH, 1)
    low = lax.broadcasted_iota(jnp.int32, first.shape, 1) < WIDTH
    return first + jnp.where(low, -turned, turned)


def choose(out_ref, pick, refs):
    for index, ref in enumerate(refs):

        @pl.when(pick == index)
        def _():
            out_ref[...] = ref[...]


def product_kernel(counts, pick_ref, recv_ref, *refs):
    tiles, refs = refs[:4], refs[4:]
    total, places = sum(counts), len(counts)
    out_refs, right_refs = refs[total:total + places], refs[total + places:-1]
    sem = refs[-1]

    @pl.when(pl.program_id(0) == 0)
    def _():
        used = 0
        for place, count in enumerate(counts):
            for index, ref in enumerate(refs[used:used + count]):

                @pl.when(pick_ref[place] == index)
                def _():
                    copy = pltpu.make_async_copy(ref, right_refs[place], sem.at[place])
                    copy.start()
                    copy.wait()

            used += count

    recv = recv_ref[0:1, :]
    half = tiles[0].shape[1]
    for side in range(2):
        real_rows, imag_rows = (tiles[2 * part + side][0] * recv for part in range(2))
        for out_ref, right_ref in zip(out_refs, right_refs):
            out_ref[side * half:(side + 1) * half, :] = complex_rows(
                real_rows, imag_rows, right_ref[...]
            )


def products(traces, recv8, groups):
    _, rows, cols = traces.shape
    lanes = groups[0][1][0].shape[1]
    counts = tuple(len(sources) for _, sources in groups)
    flat = [source for _, sources in groups for source in sources]
    picks = jnp.stack([pick for pick, _ in groups]).astype(jnp.int32)
    block = row_block(rows)
    quarter = lambda part, side: pl.BlockSpec(
        (1, block // 2, cols), lambda i: (part, 2 * i + side, 0)
    )
    return pl.pallas_call(
        functools.partial(product_kernel, counts),
        grid=(rows // block,),
        in_specs=[
            SMEM,
            pl.BlockSpec((8, cols), lambda i: (0, 0)),
        ]
        + [quarter(part, side) for part in range(2) for side in range(2)]
        + [pl.BlockSpec(memory_space=pl.ANY)] * len(flat),
        out_specs=[pl.BlockSpec((block, lanes), lambda i: (i, 0))] * len(groups),
        out_shape=[jax.ShapeDtypeStruct((rows, lanes), jnp.float32)] * len(groups),
        scratch_shapes=[pltpu.VMEM((cols, lanes), jnp.bfloat16)] * len(groups)
        + [pltpu.SemaphoreType.DMA((len(groups),))],
        compiler_params=params(),
        cost_estimate=cost(8 * rows * cols * lanes * len(groups), 4 * rows * lanes),
        name="products",
    )(picks, recv8, *[traces] * 4, *flat)


def extra_kernel(counts, pick_ref, real_ref, imag_ref, *refs):
    out_ref, right_ref = refs[-2:]
    used = 0
    for place, count in enumerate(counts):
        choose(right_ref, pick_ref[2 * place], refs[used:used + count])
        used += count
        out_ref[pick_ref[2 * place + 1]] = complex_rows(real_ref[...], imag_ref[...], right_ref[...])


def extra_products(rows, groups):
    misses, cols = rows[0].shape
    lanes = groups[0][2][0].shape[1]
    counts = tuple(len(sources) for _, _, sources in groups)
    flat = [source for _, _, sources in groups for source in sources]
    picks = jnp.stack([x for pick, place, _ in groups for x in (pick, place)]).astype(jnp.int32)
    return pl.pallas_call(
        functools.partial(extra_kernel, counts),
        in_specs=[SMEM] + [VMEM] * (2 + len(flat)),
        out_specs=VMEM,
        out_shape=jax.ShapeDtypeStruct((len(groups), misses, lanes), jnp.float32),
        scratch_shapes=[pltpu.VMEM((cols, lanes), jnp.bfloat16)],
        compiler_params=params(),
        cost_estimate=cost(8 * misses * cols * lanes * len(groups), 4 * cols * lanes),
        name="extra_products",
    )(picks, *rows, *flat)


def finish_kernel(wave_ref, miss_ref, recv_ref, tile_ref, real_ref, imag_ref, *refs):
    out_ref, row_ref = refs[-2:]
    totals = [ref[...] for ref in refs[:-2]]

    def write(target, window, chunks):
        real_part, imag_part = unpack(chunks)
        real_pred = real_part * wave_ref[0] - imag_part * wave_ref[1]
        imag_pred = imag_part * wave_ref[0] + real_part * wave_ref[1]
        target[0] = window[0] - real_pred
        target[1] = window[1] - imag_pred

    recv = recv_ref[0:1, :].astype(jnp.float32)
    write(out_ref, [tile_ref[part].astype(jnp.float32) * recv for part in range(2)], totals[:CHUNKS])
    write(row_ref, [ref[...].astype(jnp.float32) for ref in (real_ref, imag_ref)], totals[CHUNKS:])

    def place(m, carry):
        for part in range(2):
            out_ref[part, pl.ds(miss_ref[m], 1), :] = row_ref[part, pl.ds(m, 1), :]
        return carry

    lax.fori_loop(0, row_ref.shape[1], place, 0, unroll=8)


def finish(wave, miss, recv8, traces, extra, terms):
    _, rows, _ = traces.shape
    misses = extra[0].shape[0]
    flat = [term for group in terms for term in group]
    window = lambda size: pl.BlockSpec((2, size, WIN), lambda i: (0, 0, 0))
    return pl.pallas_call(
        finish_kernel,
        grid=(1,),
        in_specs=[SMEM, SMEM, pl.BlockSpec((8, WIN), lambda i: (0, 0)), window(rows)]
        + [pl.BlockSpec((misses, WIN), lambda i: (0, 0))] * 2
        + [VMEM] * len(flat),
        out_specs=window(rows),
        out_shape=jax.ShapeDtypeStruct((2, rows, WIN), jnp.float32),
        scratch_shapes=[pltpu.VMEM((2, misses, WIN), jnp.float32)],
        compiler_params=params(),
        cost_estimate=cost(20 * rows * WIN, 40 * rows * WIN),
        name="finish",
    )(wave, miss, recv8, traces, *extra, *flat)


def mirror_routes(grid_size):
    cells = [(a, b) for a in range(grid_size) for b in range(grid_size)]
    index = lambda row, col: row * grid_size + col
    whole = [(index(a, b), index(b, a)) for a, b in cells]
    near = [(index(a, b), index(b, a)) for a, b in cells if a // 2 == b // 2]
    far = [(a, b) for a, b in cells if a // 2 != b // 2]
    hop = lambda a, b: index(a, a // 2 * 2 + b % 2)
    first = [(index(a, b), hop(a, b)) for a, b in far]
    second = [(hop(a, b), index(b, a)) for a, b in far]
    if len({target for _, target in first}) < len(first):
        return whole, None
    return whole, (near, first, second)


def sources_of(up, down, offset, grid_size, row_index):
    places, sources = [], []
    for row in range(grid_size):
        other = row ^ offset
        source = up[row - other] if other < row else down[other - row]
        known = [index for index, seen in enumerate(sources) if seen is source]
        places.append(known[0] if known else len(sources))
        if not known:
            sources.append(source)
    pick = jnp.zeros((), jnp.int32)
    for row, place in enumerate(places):
        pick = jnp.where(row_index == row, place, pick)
    return pick, sources


def sum_route(offset, grid_size, stride, skip):
    route = []
    for row in range(grid_size):
        for col in range(grid_size):
            if ((col ^ row ^ offset) & ~skip) % (2 * stride) == stride:
                route.append((row * grid_size + col, row * grid_size + (col ^ stride)))
    return route


def local(traces, recv_live, missing, wavelet):
    tile = traces.shape[1]
    grid_size = lax.axis_size("row")
    misses = missing.shape[1]
    order = recv_live.shape[0]
    row_index = lax.axis_index("row")
    col_index = lax.axis_index("col")
    whole, hops = mirror_routes(grid_size)

    def move(block, route):
        return lax.ppermute(block, ("row", "col"), route)

    def transpose(block):
        return move(block, whole)

    direct, rest = cut_window(traces)
    direct = transpose(direct)
    if hops is None:
        rest = [move(rest, whole)]
    else:
        near, first, second = hops
        rest = [move(move(rest, first), second), move(rest, near)]

    miss_row = lax.dynamic_index_in_dim(missing, row_index, 0, keepdims=False)
    miss_col = lax.dynamic_index_in_dim(missing, col_index, 0, keepdims=False)
    as_lanes = lambda m: jnp.pad(m, (0, LANES - misses), constant_values=-1)[None]
    miss_col_lanes = as_lanes(miss_col)
    positions = jnp.arange(tile, dtype=jnp.int32)
    live_row = jnp.all(positions[:, None] != miss_row[None, :], axis=1)
    live8 = jnp.broadcast_to(live_row.astype(jnp.float32)[None], (8, tile))
    recv_mask = (recv_live == 1).astype(jnp.bfloat16)
    recv_row = lax.dynamic_slice_in_dim(recv_mask, row_index * tile, WIN)
    recv_row8 = jnp.broadcast_to(recv_row[None], (8, WIN))
    recv_col = lax.dynamic_slice_in_dim(recv_mask, col_index * tile, tile)
    recv_col8 = jnp.broadcast_to(recv_col[None], (8, tile))

    picked = pick_columns(traces, miss_col_lanes, recv_col8, live8, misses)
    both = transpose(jnp.concatenate(picked))
    extra = [both[:misses], both[misses:]]
    apart = row_index ^ col_index
    strides = [2**bit for bit in range(grid_size.bit_length() - 1)]
    terms, extra_terms = [], []
    for chunk in range(CHUNKS):
        window = fill_window(direct, rest, picked, miss_col_lanes, recv_row8)
        up, down = [window], [window]
        sums = []

        def hop(distance):
            ends = [(i, i + 1) for i in range(distance - 1, grid_size - 1)]
            back = [(i + 1, i) for i in range(grid_size - distance)]
            up.append(lax.ppermute(up[-1], "row", ends))
            down.append(lax.ppermute(down[-1], "row", back))

        def add_up(total, offset, strides, skip):
            for stride in strides:
                total = total + move(total, sum_route(offset, grid_size, stride, skip))
            return total

        def shrink(total):
            unit = jnp.maximum(jnp.max(jnp.abs(total)), TINY) * (1.0 / HALF_TOP)
            sent = (total * (1.0 / unit)).astype(jnp.float16)
            return sent, jnp.broadcast_to(unit, (1, LANES))

        def last(shrunk, offset, skip):
            route = sum_route(offset, grid_size, strides[-1], skip)
            return [move(part, route) for part in shrunk]

        def options(offset):
            return sources_of(up, down, offset, grid_size, row_index)

        hop(1)
        extra, up[-1], down[-1] = lax.optimization_barrier((extra, up[-1], down[-1]))
        hop(2)
        other_core = [(i, i ^ 1) for i in range(grid_size)]
        odd = apart & 1

        def pair_sum(first, mask):
            pick0, sources0 = options(first)
            pick1, sources1 = options(first + 1)
            pick1 = pick1 + len(sources0)
            both_sources = sources0 + sources1
            keep, sent = products(
                traces,
                mask,
                [
                    (jnp.where(odd == 1, pick1, pick0), both_sources),
                    (jnp.where(odd == 1, pick0, pick1), both_sources),
                ],
            )
            return add_up(keep + lax.ppermute(sent, "col", other_core), first, strides[1:-1], 1)

        sums = [pair_sum(0, recv_col8)]
        shrunk, up[-1], down[-1] = lax.optimization_barrier((shrink(sums[0]), up[-1], down[-1]))
        for distance in range(3, grid_size):
            hop(distance)
        got = [last(shrunk, 0, 1)]
        mask = recv_col8
        for first in range(2, grid_size, 2):
            if first == grid_size - 2:
                group = [(pick, apart ^ offset, sources) for offset in range(grid_size)
                         for pick, sources in [options(offset)]]
                rest = extra_products(extra, group)
                mask, got[0], rest = lax.optimization_barrier((mask, got[0], rest))
            sums.append(pair_sum(first, mask))
            got.append(last(shrink(sums[-1]), first, 1))
        whole_sum = None
        for index, (part, (sent, units)) in enumerate(zip(sums, got)):
            mine = apart // 2 == index
            term = jnp.where(mine, part, 0.0) + sent.astype(jnp.float32) * units[0, 0]
            whole_sum = term if whole_sum is None else whole_sum + term
        terms.append((whole_sum,))
        for stride in strides:
            pairs = [(i, i ^ stride) for i in range(grid_size)]
            arrive = lax.ppermute(rest[1::2], "col", pairs)
            rest = rest[0::2] + arrive
        extra_terms.append((rest[0],))
    wave = wavelet * (1.0 / math.sqrt(order))
    return finish(wave, miss_row, recv_col8, traces, extra, terms + extra_terms)


def solution(mesh):
    in_specs = (P("freq", "row", "col"), P("freq"), P("freq", None), P("freq"))
    out_specs = P("freq", "row", "col")
    return jax.shard_map(local, mesh=mesh, in_specs=in_specs, out_specs=out_specs, check_vma=False)
```

```python
import functools
import math

import jax
import jax.numpy as jnp
from jax import lax
from jax.experimental import pallas as pl
from jax.experimental.pallas import tpu as pltpu
from jax.sharding import PartitionSpec as P

WIN = 128
LANES = 128
CHUNKS = 1
WIDTH = WIN // CHUNKS
TINY = 1e-30
HALF_TOP = 32768.0
VMEM_LIMIT = 48 * 2**20
VMEM = pl.BlockSpec(memory_space=pltpu.VMEM)
SMEM = pl.BlockSpec(memory_space=pltpu.SMEM)


def params():
    return pltpu.CompilerParams(vmem_limit_bytes=VMEM_LIMIT)


def cost(flops, accessed):
    return pl.CostEstimate(
        flops=int(flops) // 64, bytes_accessed=int(accessed) // 64, transcendentals=0
    )


def row_block(rows):
    for size in (512, 384, 256, 128):
        if rows % size == 0:
            return size
    return rows


def one_hot(positions_row, rows, dtype):
    lanes = positions_row.shape[1]
    row_ids = lax.broadcasted_iota(jnp.int32, (rows, lanes), 0)
    return jnp.where(row_ids == positions_row, 1.0, 0.0).astype(dtype)


def pack(real_part, imag_part):
    if CHUNKS == 1:
        return [jnp.concatenate([real_part, imag_part], axis=1)]
    first = lax.broadcasted_iota(jnp.int32, real_part.shape, 1) < WIDTH
    low = jnp.where(first, real_part, pltpu.roll(imag_part, WIDTH, 1))
    high = jnp.where(first, pltpu.roll(real_part, WIDTH, 1), imag_part)
    return [low, high]


def unpack(chunks):
    if CHUNKS == 1:
        return chunks[0][:, :WIN], chunks[0][:, WIN:]
    low, high = chunks
    first = lax.broadcasted_iota(jnp.int32, low.shape, 1) < WIDTH
    real_part = jnp.where(first, low, pltpu.roll(high, WIDTH, 1))
    imag_part = jnp.where(first, pltpu.roll(low, WIDTH, 1), high)
    return real_part, imag_part


def halves(real_part, imag_part):
    return [real_part, imag_part] if CHUNKS == 1 else pack(real_part, imag_part)


def cut_kernel(traces_ref, *out_refs):
    parts = halves(traces_ref[0].astype(jnp.float32), traces_ref[1].astype(jnp.float32))
    for out_ref, part in zip(out_refs, parts):
        out_ref[...] = part.astype(jnp.bfloat16)


def cut_window(traces):
    rows = traces.shape[1]
    return pl.pallas_call(
        cut_kernel,
        grid=(1,),
        in_specs=[pl.BlockSpec((2, rows, WIN), lambda i: (0, 0, 0))],
        out_specs=[pl.BlockSpec((rows, WIN), lambda i: (0, 0))] * 2,
        out_shape=[jax.ShapeDtypeStruct((rows, WIN), jnp.bfloat16)] * 2,
        compiler_params=params(),
        cost_estimate=cost(rows * WIN, 8 * rows * WIN),
        name="cut_window",
    )(traces)


def pick_kernel(traces_ref, miss_ref, recv_ref, live_ref, real_ref, imag_ref, hot_ref):
    @pl.when(pl.program_id(0) == 0)
    def _():
        hot = one_hot(miss_ref[...], hot_ref.shape[0], jnp.bfloat16)
        alive = jnp.dot(recv_ref[...], hot, preferred_element_type=jnp.float32)
        hot_ref[...] = hot * alive[0:1].astype(jnp.bfloat16)

    misses = real_ref.shape[0]
    for part, out_ref in enumerate((real_ref, imag_ref)):
        picked = jnp.dot(traces_ref[part], hot_ref[...], preferred_element_type=jnp.float32)
        turned = picked.T * live_ref[0:1, :]
        out_ref[...] = turned[:misses].astype(jnp.bfloat16)


def pick_columns(traces, miss_lanes, recv8, live8, misses):
    _, rows, cols = traces.shape
    block = row_block(rows)
    return pl.pallas_call(
        pick_kernel,
        grid=(rows // block,),
        in_specs=[
            pl.BlockSpec((2, block, cols), lambda i: (0, i, 0)),
            pl.BlockSpec((1, LANES), lambda i: (0, 0)),
            pl.BlockSpec((8, cols), lambda i: (0, 0)),
            pl.BlockSpec((8, block), lambda i: (0, i)),
        ],
        out_specs=[pl.BlockSpec((misses, block), lambda i: (0, i))] * 2,
        out_shape=[jax.ShapeDtypeStruct((misses, rows), jnp.bfloat16)] * 2,
        scratch_shapes=[pltpu.VMEM((cols, LANES), jnp.bfloat16)],
        compiler_params=params(),
        cost_estimate=cost(4 * rows * cols * 2 * LANES, 4 * rows * cols),
        name="pick_columns",
    )(traces, miss_lanes, recv8, live8)


def fill_kernel(counts, first_half, real_ref, imag_ref, miss_ref, recv_ref, *refs):
    out_ref = refs[-1]
    rows = out_ref.shape[0]
    misses = real_ref.shape[0]
    hot = one_hot(miss_ref[...], rows, jnp.float32)
    dead = jnp.max(hot, axis=1, keepdims=True)
    hot = hot[:, :misses].astype(jnp.bfloat16)
    patches = halves(real_ref[...].astype(jnp.float32), imag_ref[...].astype(jnp.float32))
    mask = recv_ref[...].astype(jnp.float32)
    mask = halves(mask, mask)[0][0:1, :]
    used = 0
    for index, count in enumerate(counts):
        arrived = refs[used][...].astype(jnp.float32)
        for more in refs[used + 1:used + count]:
            arrived = arrived + more[...].astype(jnp.float32)
        used += count
        patch = patches[first_half + index].astype(jnp.bfloat16)
        moved = jnp.dot(hot, patch, preferred_element_type=jnp.float32)
        filled = arrived * ((1.0 - dead) * mask) + moved
        out_ref[:, index * WIN:(index + 1) * WIN] = filled.astype(jnp.bfloat16)


def fill_window(first_half, arrived, picked, miss_lanes, recv8):
    rows = arrived[0][0].shape[0]
    misses = picked[0].shape[0]
    counts = tuple(len(group) for group in arrived)
    flat = [part for group in arrived for part in group]
    lanes = len(counts) * WIN
    whole = pl.BlockSpec((rows, WIN), lambda i: (0, 0))
    return pl.pallas_call(
        functools.partial(fill_kernel, counts, first_half),
        grid=(1,),
        in_specs=[
            pl.BlockSpec((misses, WIN), lambda i: (0, 0)),
            pl.BlockSpec((misses, WIN), lambda i: (0, 0)),
            pl.BlockSpec((1, LANES), lambda i: (0, 0)),
            pl.BlockSpec((8, WIN), lambda i: (0, 0)),
        ]
        + [whole] * len(flat),
        out_specs=pl.BlockSpec((rows, lanes), lambda i: (0, 0)),
        out_shape=jax.ShapeDtypeStruct((rows, lanes), jnp.bfloat16),
        compiler_params=params(),
        cost_estimate=cost(4 * rows * LANES * lanes, 8 * rows * lanes),
        name="fill_window",
    )(*picked, miss_lanes, recv8, *flat)


def complex_rows(real_rows, imag_rows, right):
    first = jnp.dot(real_rows, right, preferred_element_type=jnp.float32)
    second = jnp.dot(imag_rows, right, preferred_element_type=jnp.float32)
    if CHUNKS == 1:
        real_part = first[:, :WIN] - second[:, WIN:]
        imag_part = first[:, WIN:] + second[:, :WIN]
        return jnp.concatenate([real_part, imag_part], axis=1)
    turned = pltpu.roll(second, WIDTH, 1)
    low = lax.broadcasted_iota(jnp.int32, first.shape, 1) < WIDTH
    return first + jnp.where(low, -turned, turned)


def choose(out_ref, pick, refs):
    for index, ref in enumerate(refs):

        @pl.when(pick == index)
        def _():
            out_ref[...] = ref[...]


def product_kernel(counts, pick_ref, recv_ref, *refs):
    tiles, refs = refs[:4], refs[4:]
    total, places = sum(counts), len(counts)
    out_refs, right_refs = refs[total:total + places], refs[total + places:-1]
    sem = refs[-1]

    @pl.when(pl.program_id(0) == 0)
    def _():
        used = 0
        for place, count in enumerate(counts):
            for index, ref in enumerate(refs[used:used + count]):

                @pl.when(pick_ref[place] == index)
                def _():
                    copy = pltpu.make_async_copy(ref, right_refs[place], sem.at[place])
                    copy.start()
                    copy.wait()

            used += count

    recv = recv_ref[0:1, :]
    half = tiles[0].shape[1]
    for side in range(2):
        real_rows, imag_rows = (tiles[2 * part + side][0] * recv for part in range(2))
        for out_ref, right_ref in zip(out_refs, right_refs):
            out_ref[side * half:(side + 1) * half, :] = complex_rows(
                real_rows, imag_rows, right_ref[...]
            )


def products(traces, recv8, groups):
    _, rows, cols = traces.shape
    lanes = groups[0][1][0].shape[1]
    counts = tuple(len(sources) for _, sources in groups)
    flat = [source for _, sources in groups for source in sources]
    picks = jnp.stack([pick for pick, _ in groups]).astype(jnp.int32)
    block = row_block(rows)
    quarter = lambda part, side: pl.BlockSpec(
        (1, block // 2, cols), lambda i: (part, 2 * i + side, 0)
    )
    return pl.pallas_call(
        functools.partial(product_kernel, counts),
        grid=(rows // block,),
        in_specs=[
            SMEM,
            pl.BlockSpec((8, cols), lambda i: (0, 0)),
        ]
        + [quarter(part, side) for part in range(2) for side in range(2)]
        + [pl.BlockSpec(memory_space=pl.ANY)] * len(flat),
        out_specs=[pl.BlockSpec((block, lanes), lambda i: (i, 0))] * len(groups),
        out_shape=[jax.ShapeDtypeStruct((rows, lanes), jnp.float32)] * len(groups),
        scratch_shapes=[pltpu.VMEM((cols, lanes), jnp.bfloat16)] * len(groups)
        + [pltpu.SemaphoreType.DMA((len(groups),))],
        compiler_params=params(),
        cost_estimate=cost(8 * rows * cols * lanes * len(groups), 4 * rows * lanes),
        name="products",
    )(picks, recv8, *[traces] * 4, *flat)


def extra_kernel(counts, pick_ref, real_ref, imag_ref, *refs):
    out_ref, right_ref = refs[-2:]
    used = 0
    for place, count in enumerate(counts):
        choose(right_ref, pick_ref[2 * place], refs[used:used + count])
        used += count
        out_ref[pick_ref[2 * place + 1]] = complex_rows(real_ref[...], imag_ref[...], right_ref[...])


def extra_products(rows, groups):
    misses, cols = rows[0].shape
    lanes = groups[0][2][0].shape[1]
    counts = tuple(len(sources) for _, _, sources in groups)
    flat = [source for _, _, sources in groups for source in sources]
    picks = jnp.stack([x for pick, place, _ in groups for x in (pick, place)]).astype(jnp.int32)
    return pl.pallas_call(
        functools.partial(extra_kernel, counts),
        in_specs=[SMEM] + [VMEM] * (2 + len(flat)),
        out_specs=VMEM,
        out_shape=jax.ShapeDtypeStruct((len(groups), misses, lanes), jnp.float32),
        scratch_shapes=[pltpu.VMEM((cols, lanes), jnp.bfloat16)],
        compiler_params=params(),
        cost_estimate=cost(8 * misses * cols * lanes * len(groups), 4 * cols * lanes),
        name="extra_products",
    )(picks, *rows, *flat)


def finish_kernel(wave_ref, miss_ref, recv_ref, tile_ref, real_ref, imag_ref, *refs):
    out_ref, row_ref = refs[-2:]
    totals = [ref[...] for ref in refs[:-2]]

    def write(target, window, chunks):
        real_part, imag_part = unpack(chunks)
        real_pred = real_part * wave_ref[0] - imag_part * wave_ref[1]
        imag_pred = imag_part * wave_ref[0] + real_part * wave_ref[1]
        target[0] = window[0] - real_pred
        target[1] = window[1] - imag_pred

    recv = recv_ref[0:1, :].astype(jnp.float32)
    write(out_ref, [tile_ref[part].astype(jnp.float32) * recv for part in range(2)], totals[:CHUNKS])
    write(row_ref, [ref[...].astype(jnp.float32) for ref in (real_ref, imag_ref)], totals[CHUNKS:])

    def place(m, carry):
        for part in range(2):
            out_ref[part, pl.ds(miss_ref[m], 1), :] = row_ref[part, pl.ds(m, 1), :]
        return carry

    lax.fori_loop(0, row_ref.shape[1], place, 0, unroll=8)


def finish(wave, miss, recv8, traces, extra, terms):
    _, rows, _ = traces.shape
    misses = extra[0].shape[0]
    flat = [term for group in terms for term in group]
    window = lambda size: pl.BlockSpec((2, size, WIN), lambda i: (0, 0, 0))
    return pl.pallas_call(
        finish_kernel,
        grid=(1,),
        in_specs=[SMEM, SMEM, pl.BlockSpec((8, WIN), lambda i: (0, 0)), window(rows)]
        + [pl.BlockSpec((misses, WIN), lambda i: (0, 0))] * 2
        + [VMEM] * len(flat),
        out_specs=window(rows),
        out_shape=jax.ShapeDtypeStruct((2, rows, WIN), jnp.float32),
        scratch_shapes=[pltpu.VMEM((2, misses, WIN), jnp.float32)],
        compiler_params=params(),
        cost_estimate=cost(20 * rows * WIN, 40 * rows * WIN),
        name="finish",
    )(wave, miss, recv8, traces, *extra, *flat)


def mirror_routes(grid_size):
    cells = [(a, b) for a in range(grid_size) for b in range(grid_size)]
    index = lambda row, col: row * grid_size + col
    whole = [(index(a, b), index(b, a)) for a, b in cells]
    near = [(index(a, b), index(b, a)) for a, b in cells if a // 2 == b // 2]
    far = [(a, b) for a, b in cells if a // 2 != b // 2]
    hop = lambda a, b: index(a, a // 2 * 2 + b % 2)
    first = [(index(a, b), hop(a, b)) for a, b in far]
    second = [(hop(a, b), index(b, a)) for a, b in far]
    if len({target for _, target in first}) < len(first):
        return whole, None
    return whole, (near, first, second)


def sources_of(up, down, offset, grid_size, row_index):
    places, sources = [], []
    for row in range(grid_size):
        other = row ^ offset
        source = up[row - other] if other < row else down[other - row]
        known = [index for index, seen in enumerate(sources) if seen is source]
        places.append(known[0] if known else len(sources))
        if not known:
            sources.append(source)
    pick = jnp.zeros((), jnp.int32)
    for row, place in enumerate(places):
        pick = jnp.where(row_index == row, place, pick)
    return pick, sources


def sum_route(offset, grid_size, stride, skip):
    route = []
    for row in range(grid_size):
        for col in range(grid_size):
            if ((col ^ row ^ offset) & ~skip) % (2 * stride) == stride:
                route.append((row * grid_size + col, row * grid_size + (col ^ stride)))
    return route


def local(traces, recv_live, missing, wavelet):
    tile = traces.shape[1]
    grid_size = lax.axis_size("row")
    misses = missing.shape[1]
    order = recv_live.shape[0]
    row_index = lax.axis_index("row")
    col_index = lax.axis_index("col")
    whole, hops = mirror_routes(grid_size)

    def move(block, route):
        return lax.ppermute(block, ("row", "col"), route)

    def transpose(block):
        return move(block, whole)

    def transpose_round(block):
        if hops is None:
            return [move(block, whole)]
        near, first, second = hops
        return [move(move(block, first), second), move(block, near)]

    direct, round_about = cut_window(traces)
    arrived = [[transpose(direct)], transpose_round(round_about)]
    if CHUNKS == 1:
        arrived = [arrived]
    else:
        arrived = [arrived[:1], arrived[1:]]

    miss_row = lax.dynamic_index_in_dim(missing, row_index, 0, keepdims=False)
    miss_col = lax.dynamic_index_in_dim(missing, col_index, 0, keepdims=False)
    as_lanes = lambda m: jnp.pad(m, (0, LANES - misses), constant_values=-1)[None]
    miss_col_lanes = as_lanes(miss_col)
    positions = jnp.arange(tile, dtype=jnp.int32)
    live_row = jnp.all(positions[:, None] != miss_row[None, :], axis=1)
    live8 = jnp.broadcast_to(live_row.astype(jnp.float32)[None], (8, tile))
    recv_mask = (recv_live == 1).astype(jnp.bfloat16)
    recv_row = lax.dynamic_slice_in_dim(recv_mask, row_index * tile, WIN)
    recv_row8 = jnp.broadcast_to(recv_row[None], (8, WIN))
    recv_col = lax.dynamic_slice_in_dim(recv_mask, col_index * tile, tile)
    recv_col8 = jnp.broadcast_to(recv_col[None], (8, tile))

    picked = pick_columns(traces, miss_col_lanes, recv_col8, live8, misses)
    both = jnp.concatenate(picked)
    apart = row_index ^ col_index
    strides = [2**bit for bit in range(grid_size.bit_length() - 1)]
    terms, extra_terms = [], []
    for chunk in range(CHUNKS):
        window = fill_window(chunk, arrived[chunk], picked, miss_col_lanes, recv_row8)
        up, down = [window], [window]
        sums = []

        def hop(distance):
            ends = [(i, i + 1) for i in range(distance - 1, grid_size - 1)]
            back = [(i + 1, i) for i in range(grid_size - distance)]
            up.append(lax.ppermute(up[-1], "row", ends))
            down.append(lax.ppermute(down[-1], "row", back))

        def add_up(total, offset, strides, skip):
            for stride in strides:
                total = total + move(total, sum_route(offset, grid_size, stride, skip))
            return total

        def shrink(total):
            unit = jnp.maximum(jnp.max(jnp.abs(total)), TINY) * (1.0 / HALF_TOP)
            sent = (total * (1.0 / unit)).astype(jnp.float16)
            return sent, jnp.broadcast_to(unit, (1, LANES))

        def last(shrunk, offset, skip):
            route = sum_route(offset, grid_size, strides[-1], skip)
            return [move(part, route) for part in shrunk]

        def options(offset):
            return sources_of(up, down, offset, grid_size, row_index)

        hop(1)
        both, up[-1], down[-1] = lax.optimization_barrier((both, up[-1], down[-1]))
        both = transpose(both)
        extra = [both[:misses], both[misses:]]
        hop(2)
        other_core = [(i, i ^ 1) for i in range(grid_size)]
        odd = apart & 1

        def pair_sum(first, mask):
            pick0, sources0 = options(first)
            pick1, sources1 = options(first + 1)
            pick1 = pick1 + len(sources0)
            both_sources = sources0 + sources1
            keep, sent = products(
                traces,
                mask,
                [
                    (jnp.where(odd == 1, pick1, pick0), both_sources),
                    (jnp.where(odd == 1, pick0, pick1), both_sources),
                ],
            )
            return add_up(keep + lax.ppermute(sent, "col", other_core), first, strides[1:-1], 1)

        extra, mask = lax.optimization_barrier((extra, recv_col8))
        sums = [pair_sum(0, mask)]
        shrunk = shrink(sums[0])
        for distance in range(3, grid_size):
            hop(distance)
        got = []
        mask = recv_col8
        for first in range(2, grid_size, 2):
            if first == grid_size - 2:
                group = [(pick, apart ^ offset, sources) for offset in range(grid_size)
                         for pick, sources in [options(offset)]]
                rest = extra_products(extra, group)
                mask, shrunk, rest = lax.optimization_barrier((mask, shrunk, rest))
                got.insert(0, last(shrunk, 0, 1))
            sums.append(pair_sum(first, mask))
            got.append(last(shrink(sums[-1]), first, 1))
        whole_sum = None
        for index, (part, (sent, units)) in enumerate(zip(sums, got)):
            mine = apart // 2 == index
            term = jnp.where(mine, part, 0.0) + sent.astype(jnp.float32) * units[0, 0]
            whole_sum = term if whole_sum is None else whole_sum + term
        terms.append((whole_sum,))
        for stride in strides:
            pairs = [(i, i ^ stride) for i in range(grid_size)]
            arrive = lax.ppermute(rest[1::2], "col", pairs)
            rest = rest[0::2] + arrive
        extra_terms.append((rest[0],))
    wave = wavelet * (1.0 / math.sqrt(order))
    return finish(wave, miss_row, recv_col8, traces, extra, terms + extra_terms)


def solution(mesh):
    in_specs = (P("freq", "row", "col"), P("freq"), P("freq", None), P("freq"))
    out_specs = P("freq", "row", "col")
    return jax.shard_map(local, mesh=mesh, in_specs=in_specs, out_specs=out_specs, check_vma=False)
```

```python
import functools
import math

import jax
import jax.numpy as jnp
from jax import lax
from jax.experimental import pallas as pl
from jax.experimental.pallas import tpu as pltpu
from jax.sharding import PartitionSpec as P

WIN = 128
LANES = 128
CHUNKS = 1
WIDTH = WIN // CHUNKS
TINY = 1e-30
HALF_TOP = 32768.0
VMEM_LIMIT = 48 * 2**20
VMEM = pl.BlockSpec(memory_space=pltpu.VMEM)
SMEM = pl.BlockSpec(memory_space=pltpu.SMEM)


def params():
    return pltpu.CompilerParams(vmem_limit_bytes=VMEM_LIMIT)


def cost(flops, accessed):
    return pl.CostEstimate(
        flops=int(flops) // 64, bytes_accessed=int(accessed) // 64, transcendentals=0
    )


def row_block(rows):
    for size in (512, 384, 256, 128):
        if rows % size == 0:
            return size
    return rows


def one_hot(positions_row, rows, dtype):
    lanes = positions_row.shape[1]
    row_ids = lax.broadcasted_iota(jnp.int32, (rows, lanes), 0)
    return jnp.where(row_ids == positions_row, 1.0, 0.0).astype(dtype)


def pack(real_part, imag_part):
    if CHUNKS == 1:
        return [jnp.concatenate([real_part, imag_part], axis=1)]
    first = lax.broadcasted_iota(jnp.int32, real_part.shape, 1) < WIDTH
    low = jnp.where(first, real_part, pltpu.roll(imag_part, WIDTH, 1))
    high = jnp.where(first, pltpu.roll(real_part, WIDTH, 1), imag_part)
    return [low, high]


def unpack(chunks):
    if CHUNKS == 1:
        return chunks[0][:, :WIN], chunks[0][:, WIN:]
    low, high = chunks
    first = lax.broadcasted_iota(jnp.int32, low.shape, 1) < WIDTH
    real_part = jnp.where(first, low, pltpu.roll(high, WIDTH, 1))
    imag_part = jnp.where(first, pltpu.roll(low, WIDTH, 1), high)
    return real_part, imag_part


def halves(real_part, imag_part):
    return [real_part, imag_part] if CHUNKS == 1 else pack(real_part, imag_part)


def cut_kernel(traces_ref, *out_refs):
    parts = halves(traces_ref[0].astype(jnp.float32), traces_ref[1].astype(jnp.float32))
    for out_ref, part in zip(out_refs, parts):
        out_ref[...] = part.astype(jnp.bfloat16)


def cut_window(traces):
    rows = traces.shape[1]
    return pl.pallas_call(
        cut_kernel,
        grid=(1,),
        in_specs=[pl.BlockSpec((2, rows, WIN), lambda i: (0, 0, 0))],
        out_specs=[pl.BlockSpec((rows, WIN), lambda i: (0, 0))] * 2,
        out_shape=[jax.ShapeDtypeStruct((rows, WIN), jnp.bfloat16)] * 2,
        compiler_params=params(),
        cost_estimate=cost(rows * WIN, 8 * rows * WIN),
        name="cut_window",
    )(traces)


def pick_kernel(traces_ref, miss_ref, recv_ref, live_ref, real_ref, imag_ref, hot_ref):
    @pl.when(pl.program_id(0) == 0)
    def _():
        hot = one_hot(miss_ref[...], hot_ref.shape[0], jnp.bfloat16)
        alive = jnp.dot(recv_ref[...], hot, preferred_element_type=jnp.float32)
        hot_ref[...] = hot * alive[0:1].astype(jnp.bfloat16)

    misses = real_ref.shape[0]
    for part, out_ref in enumerate((real_ref, imag_ref)):
        picked = jnp.dot(traces_ref[part], hot_ref[...], preferred_element_type=jnp.float32)
        turned = picked.T * live_ref[0:1, :]
        out_ref[...] = turned[:misses].astype(jnp.bfloat16)


def pick_columns(traces, miss_lanes, recv8, live8, misses):
    _, rows, cols = traces.shape
    block = row_block(rows)
    return pl.pallas_call(
        pick_kernel,
        grid=(rows // block,),
        in_specs=[
            pl.BlockSpec((2, block, cols), lambda i: (0, i, 0)),
            pl.BlockSpec((1, LANES), lambda i: (0, 0)),
            pl.BlockSpec((8, cols), lambda i: (0, 0)),
            pl.BlockSpec((8, block), lambda i: (0, i)),
        ],
        out_specs=[pl.BlockSpec((misses, block), lambda i: (0, i))] * 2,
        out_shape=[jax.ShapeDtypeStruct((misses, rows), jnp.bfloat16)] * 2,
        scratch_shapes=[pltpu.VMEM((cols, LANES), jnp.bfloat16)],
        compiler_params=params(),
        cost_estimate=cost(4 * rows * cols * 2 * LANES, 4 * rows * cols),
        name="pick_columns",
    )(traces, miss_lanes, recv8, live8)


def fill_kernel(counts, first_half, real_ref, imag_ref, miss_ref, recv_ref, *refs):
    out_ref = refs[-1]
    rows = out_ref.shape[0]
    misses = real_ref.shape[0]
    hot = one_hot(miss_ref[...], rows, jnp.float32)
    dead = jnp.max(hot, axis=1, keepdims=True)
    hot = hot[:, :misses].astype(jnp.bfloat16)
    patches = halves(real_ref[...].astype(jnp.float32), imag_ref[...].astype(jnp.float32))
    mask = recv_ref[...].astype(jnp.float32)
    mask = halves(mask, mask)[0][0:1, :]
    used = 0
    for index, count in enumerate(counts):
        arrived = refs[used][...].astype(jnp.float32)
        for more in refs[used + 1:used + count]:
            arrived = arrived + more[...].astype(jnp.float32)
        used += count
        patch = patches[first_half + index].astype(jnp.bfloat16)
        moved = jnp.dot(hot, patch, preferred_element_type=jnp.float32)
        filled = arrived * ((1.0 - dead) * mask) + moved
        out_ref[:, index * WIN:(index + 1) * WIN] = filled.astype(jnp.bfloat16)


def fill_window(first_half, arrived, picked, miss_lanes, recv8):
    rows = arrived[0][0].shape[0]
    misses = picked[0].shape[0]
    counts = tuple(len(group) for group in arrived)
    flat = [part for group in arrived for part in group]
    lanes = len(counts) * WIN
    whole = pl.BlockSpec((rows, WIN), lambda i: (0, 0))
    return pl.pallas_call(
        functools.partial(fill_kernel, counts, first_half),
        grid=(1,),
        in_specs=[
            pl.BlockSpec((misses, WIN), lambda i: (0, 0)),
            pl.BlockSpec((misses, WIN), lambda i: (0, 0)),
            pl.BlockSpec((1, LANES), lambda i: (0, 0)),
            pl.BlockSpec((8, WIN), lambda i: (0, 0)),
        ]
        + [whole] * len(flat),
        out_specs=pl.BlockSpec((rows, lanes), lambda i: (0, 0)),
        out_shape=jax.ShapeDtypeStruct((rows, lanes), jnp.bfloat16),
        compiler_params=params(),
        cost_estimate=cost(4 * rows * LANES * lanes, 8 * rows * lanes),
        name="fill_window",
    )(*picked, miss_lanes, recv8, *flat)


def complex_rows(real_rows, imag_rows, right):
    first = jnp.dot(real_rows, right, preferred_element_type=jnp.float32)
    second = jnp.dot(imag_rows, right, preferred_element_type=jnp.float32)
    if CHUNKS == 1:
        real_part = first[:, :WIN] - second[:, WIN:]
        imag_part = first[:, WIN:] + second[:, :WIN]
        return jnp.concatenate([real_part, imag_part], axis=1)
    turned = pltpu.roll(second, WIDTH, 1)
    low = lax.broadcasted_iota(jnp.int32, first.shape, 1) < WIDTH
    return first + jnp.where(low, -turned, turned)


def choose(out_ref, pick, refs):
    for index, ref in enumerate(refs):

        @pl.when(pick == index)
        def _():
            out_ref[...] = ref[...]


def product_kernel(counts, pick_ref, recv_ref, *refs):
    tiles, refs = refs[:4], refs[4:]
    total, places = sum(counts), len(counts)
    out_refs, right_refs = refs[total:total + places], refs[total + places:-1]
    sem = refs[-1]

    @pl.when(pl.program_id(0) == 0)
    def _():
        used = 0
        for place, count in enumerate(counts):
            for index, ref in enumerate(refs[used:used + count]):

                @pl.when(pick_ref[place] == index)
                def _():
                    copy = pltpu.make_async_copy(ref, right_refs[place], sem.at[place])
                    copy.start()
                    copy.wait()

            used += count

    recv = recv_ref[0:1, :]
    half = tiles[0].shape[1]
    for side in range(2):
        real_rows, imag_rows = (tiles[2 * part + side][0] * recv for part in range(2))
        for out_ref, right_ref in zip(out_refs, right_refs):
            out_ref[side * half:(side + 1) * half, :] = complex_rows(
                real_rows, imag_rows, right_ref[...]
            )


def products(traces, recv8, groups):
    _, rows, cols = traces.shape
    lanes = groups[0][1][0].shape[1]
    counts = tuple(len(sources) for _, sources in groups)
    flat = [source for _, sources in groups for source in sources]
    picks = jnp.stack([pick for pick, _ in groups]).astype(jnp.int32)
    block = row_block(rows)
    quarter = lambda part, side: pl.BlockSpec(
        (1, block // 2, cols), lambda i: (part, 2 * i + side, 0)
    )
    return pl.pallas_call(
        functools.partial(product_kernel, counts),
        grid=(rows // block,),
        in_specs=[
            SMEM,
            pl.BlockSpec((8, cols), lambda i: (0, 0)),
        ]
        + [quarter(part, side) for part in range(2) for side in range(2)]
        + [pl.BlockSpec(memory_space=pl.ANY)] * len(flat),
        out_specs=[pl.BlockSpec((block, lanes), lambda i: (i, 0))] * len(groups),
        out_shape=[jax.ShapeDtypeStruct((rows, lanes), jnp.float32)] * len(groups),
        scratch_shapes=[pltpu.VMEM((cols, lanes), jnp.bfloat16)] * len(groups)
        + [pltpu.SemaphoreType.DMA((len(groups),))],
        compiler_params=params(),
        cost_estimate=cost(8 * rows * cols * lanes * len(groups), 4 * rows * lanes),
        name="products",
    )(picks, recv8, *[traces] * 4, *flat)


def extra_kernel(counts, pick_ref, real_ref, imag_ref, *refs):
    out_ref, right_ref = refs[-2:]
    used = 0
    for place, count in enumerate(counts):
        choose(right_ref, pick_ref[2 * place], refs[used:used + count])
        used += count
        out_ref[pick_ref[2 * place + 1]] = complex_rows(real_ref[...], imag_ref[...], right_ref[...])


def extra_products(rows, groups):
    misses, cols = rows[0].shape
    lanes = groups[0][2][0].shape[1]
    counts = tuple(len(sources) for _, _, sources in groups)
    flat = [source for _, _, sources in groups for source in sources]
    picks = jnp.stack([x for pick, place, _ in groups for x in (pick, place)]).astype(jnp.int32)
    return pl.pallas_call(
        functools.partial(extra_kernel, counts),
        in_specs=[SMEM] + [VMEM] * (2 + len(flat)),
        out_specs=VMEM,
        out_shape=jax.ShapeDtypeStruct((len(groups), misses, lanes), jnp.float32),
        scratch_shapes=[pltpu.VMEM((cols, lanes), jnp.bfloat16)],
        compiler_params=params(),
        cost_estimate=cost(8 * misses * cols * lanes * len(groups), 4 * cols * lanes),
        name="extra_products",
    )(picks, *rows, *flat)


def finish_kernel(wave_ref, miss_ref, recv_ref, tile_ref, real_ref, imag_ref, *refs):
    out_ref, row_ref = refs[-2:]
    totals = [ref[...] for ref in refs[:-2]]

    def write(target, window, chunks):
        real_part, imag_part = unpack(chunks)
        real_pred = real_part * wave_ref[0] - imag_part * wave_ref[1]
        imag_pred = imag_part * wave_ref[0] + real_part * wave_ref[1]
        target[0] = window[0] - real_pred
        target[1] = window[1] - imag_pred

    recv = recv_ref[0:1, :].astype(jnp.float32)
    write(out_ref, [tile_ref[part].astype(jnp.float32) * recv for part in range(2)], totals[:CHUNKS])
    write(row_ref, [ref[...].astype(jnp.float32) for ref in (real_ref, imag_ref)], totals[CHUNKS:])

    def place(m, carry):
        for part in range(2):
            out_ref[part, pl.ds(miss_ref[m], 1), :] = row_ref[part, pl.ds(m, 1), :]
        return carry

    lax.fori_loop(0, row_ref.shape[1], place, 0, unroll=8)


def finish(wave, miss, recv8, traces, extra, terms):
    _, rows, _ = traces.shape
    misses = extra[0].shape[0]
    flat = [term for group in terms for term in group]
    window = lambda size: pl.BlockSpec((2, size, WIN), lambda i: (0, 0, 0))
    return pl.pallas_call(
        finish_kernel,
        grid=(1,),
        in_specs=[SMEM, SMEM, pl.BlockSpec((8, WIN), lambda i: (0, 0)), window(rows)]
        + [pl.BlockSpec((misses, WIN), lambda i: (0, 0))] * 2
        + [VMEM] * len(flat),
        out_specs=window(rows),
        out_shape=jax.ShapeDtypeStruct((2, rows, WIN), jnp.float32),
        scratch_shapes=[pltpu.VMEM((2, misses, WIN), jnp.float32)],
        compiler_params=params(),
        cost_estimate=cost(20 * rows * WIN, 40 * rows * WIN),
        name="finish",
    )(wave, miss, recv8, traces, *extra, *flat)


def mirror_routes(grid_size):
    cells = [(a, b) for a in range(grid_size) for b in range(grid_size)]
    index = lambda row, col: row * grid_size + col
    whole = [(index(a, b), index(b, a)) for a, b in cells]
    near = [(index(a, b), index(b, a)) for a, b in cells if a // 2 == b // 2]
    far = [(a, b) for a, b in cells if a // 2 != b // 2]
    hop = lambda a, b: index(a, a // 2 * 2 + b % 2)
    first = [(index(a, b), hop(a, b)) for a, b in far]
    second = [(hop(a, b), index(b, a)) for a, b in far]
    if len({target for _, target in first}) < len(first):
        return whole, None
    return whole, (near, first, second)


def sources_of(up, down, offset, grid_size, row_index):
    places, sources = [], []
    for row in range(grid_size):
        other = row ^ offset
        source = up[row - other] if other < row else down[other - row]
        known = [index for index, seen in enumerate(sources) if seen is source]
        places.append(known[0] if known else len(sources))
        if not known:
            sources.append(source)
    pick = jnp.zeros((), jnp.int32)
    for row, place in enumerate(places):
        pick = jnp.where(row_index == row, place, pick)
    return pick, sources


def sum_route(offset, grid_size, stride, skip):
    route = []
    for row in range(grid_size):
        for col in range(grid_size):
            if ((col ^ row ^ offset) & ~skip) % (2 * stride) == stride:
                route.append((row * grid_size + col, row * grid_size + (col ^ stride)))
    return route


def local(traces, recv_live, missing, wavelet):
    tile = traces.shape[1]
    grid_size = lax.axis_size("row")
    misses = missing.shape[1]
    order = recv_live.shape[0]
    row_index = lax.axis_index("row")
    col_index = lax.axis_index("col")
    whole, hops = mirror_routes(grid_size)

    def move(block, route):
        return lax.ppermute(block, ("row", "col"), route)

    def transpose(block):
        return move(block, whole)

    def transpose_round(block):
        if hops is None:
            return [move(block, whole)]
        near, first, second = hops
        return [move(move(block, first), second), move(block, near)]

    direct, round_about = cut_window(traces)
    arrived = [[transpose(direct)], transpose_round(round_about)]
    if CHUNKS == 1:
        arrived = [arrived]
    else:
        arrived = [arrived[:1], arrived[1:]]

    miss_row = lax.dynamic_index_in_dim(missing, row_index, 0, keepdims=False)
    miss_col = lax.dynamic_index_in_dim(missing, col_index, 0, keepdims=False)
    as_lanes = lambda m: jnp.pad(m, (0, LANES - misses), constant_values=-1)[None]
    miss_col_lanes = as_lanes(miss_col)
    positions = jnp.arange(tile, dtype=jnp.int32)
    live_row = jnp.all(positions[:, None] != miss_row[None, :], axis=1)
    live8 = jnp.broadcast_to(live_row.astype(jnp.float32)[None], (8, tile))
    recv_mask = (recv_live == 1).astype(jnp.bfloat16)
    recv_row = lax.dynamic_slice_in_dim(recv_mask, row_index * tile, WIN)
    recv_row8 = jnp.broadcast_to(recv_row[None], (8, WIN))
    recv_col = lax.dynamic_slice_in_dim(recv_mask, col_index * tile, tile)
    recv_col8 = jnp.broadcast_to(recv_col[None], (8, tile))

    picked = pick_columns(traces, miss_col_lanes, recv_col8, live8, misses)
    both = transpose(jnp.concatenate(picked))
    extra = [both[:misses], both[misses:]]
    apart = row_index ^ col_index
    strides = [2**bit for bit in range(grid_size.bit_length() - 1)]
    terms, extra_terms = [], []
    for chunk in range(CHUNKS):
        window = fill_window(chunk, arrived[chunk], picked, miss_col_lanes, recv_row8)
        up, down = [window], [window]
        sums = []

        def hop(distance):
            ends = [(i, i + 1) for i in range(distance - 1, grid_size - 1)]
            back = [(i + 1, i) for i in range(grid_size - distance)]
            up.append(lax.ppermute(up[-1], "row", ends))
            down.append(lax.ppermute(down[-1], "row", back))

        def add_up(total, offset, strides, skip):
            for stride in strides:
                total = total + move(total, sum_route(offset, grid_size, stride, skip))
            return total

        def shrink(total):
            unit = jnp.maximum(jnp.max(jnp.abs(total)), TINY) * (1.0 / HALF_TOP)
            sent = (total * (1.0 / unit)).astype(jnp.float16)
            return sent, jnp.broadcast_to(unit, (1, LANES))

        def last(shrunk, offset, skip):
            route = sum_route(offset, grid_size, strides[-1], skip)
            return [move(part, route) for part in shrunk]

        def options(offset):
            return sources_of(up, down, offset, grid_size, row_index)

        hop(1)
        extra, up[-1], down[-1] = lax.optimization_barrier((extra, up[-1], down[-1]))
        hop(2)
        other_core = [(i, i ^ 1) for i in range(grid_size)]
        odd = apart & 1

        def pair_sum(first, mask):
            pick0, sources0 = options(first)
            pick1, sources1 = options(first + 1)
            pick1 = pick1 + len(sources0)
            both_sources = sources0 + sources1
            keep, sent = products(
                traces,
                mask,
                [
                    (jnp.where(odd == 1, pick1, pick0), both_sources),
                    (jnp.where(odd == 1, pick0, pick1), both_sources),
                ],
            )
            return add_up(keep + lax.ppermute(sent, "col", other_core), first, strides[1:-1], 1)

        sums = [pair_sum(0, recv_col8)]
        shrunk, up[-1], down[-1] = lax.optimization_barrier((shrink(sums[0]), up[-1], down[-1]))
        for distance in range(3, grid_size):
            hop(distance)
        got = [last(shrunk, 0, 1)]
        mask = recv_col8
        for first in range(2, grid_size, 2):
            if first == grid_size - 2:
                group = [(pick, apart ^ offset, sources) for offset in range(grid_size)
                         for pick, sources in [options(offset)]]
                rest = extra_products(extra, group)
                mask, rest = lax.optimization_barrier((mask, rest))
            sums.append(pair_sum(first, mask))
            got.append(last(shrink(sums[-1]), first, 1))
        whole_sum = None
        for index, (part, (sent, units)) in enumerate(zip(sums, got)):
            mine = apart // 2 == index
            term = jnp.where(mine, part, 0.0) + sent.astype(jnp.float32) * units[0, 0]
            whole_sum = term if whole_sum is None else whole_sum + term
        terms.append((whole_sum,))
        for stride in strides:
            pairs = [(i, i ^ stride) for i in range(grid_size)]
            arrive = lax.ppermute(rest[1::2], "col", pairs)
            rest = rest[0::2] + arrive
        extra_terms.append((rest[0],))
    wave = wavelet * (1.0 / math.sqrt(order))
    return finish(wave, miss_row, recv_col8, traces, extra, terms + extra_terms)


def solution(mesh):
    in_specs = (P("freq", "row", "col"), P("freq"), P("freq", None), P("freq"))
    out_specs = P("freq", "row", "col")
    return jax.shard_map(local, mesh=mesh, in_specs=in_specs, out_specs=out_specs, check_vma=False)
```

```python
import functools
import math

import jax
import jax.numpy as jnp
from jax import lax
from jax.experimental import pallas as pl
from jax.experimental.pallas import tpu as pltpu
from jax.sharding import PartitionSpec as P

WIN = 128
LANES = 128
CHUNKS = 1
WIDTH = WIN // CHUNKS
TINY = 1e-30
HALF_TOP = 32768.0
VMEM_LIMIT = 48 * 2**20
VMEM = pl.BlockSpec(memory_space=pltpu.VMEM)
SMEM = pl.BlockSpec(memory_space=pltpu.SMEM)


def params():
    return pltpu.CompilerParams(vmem_limit_bytes=VMEM_LIMIT)


def cost(flops, accessed):
    return pl.CostEstimate(
        flops=int(flops) // 64, bytes_accessed=int(accessed) // 64, transcendentals=0
    )


def row_block(rows):
    for size in (512, 384, 256, 128):
        if rows % size == 0:
            return size
    return rows


def one_hot(positions_row, rows, dtype):
    lanes = positions_row.shape[1]
    row_ids = lax.broadcasted_iota(jnp.int32, (rows, lanes), 0)
    return jnp.where(row_ids == positions_row, 1.0, 0.0).astype(dtype)


def pack(real_part, imag_part):
    if CHUNKS == 1:
        return [jnp.concatenate([real_part, imag_part], axis=1)]
    first = lax.broadcasted_iota(jnp.int32, real_part.shape, 1) < WIDTH
    low = jnp.where(first, real_part, pltpu.roll(imag_part, WIDTH, 1))
    high = jnp.where(first, pltpu.roll(real_part, WIDTH, 1), imag_part)
    return [low, high]


def unpack(chunks):
    if CHUNKS == 1:
        return chunks[0][:, :WIN], chunks[0][:, WIN:]
    low, high = chunks
    first = lax.broadcasted_iota(jnp.int32, low.shape, 1) < WIDTH
    real_part = jnp.where(first, low, pltpu.roll(high, WIDTH, 1))
    imag_part = jnp.where(first, pltpu.roll(low, WIDTH, 1), high)
    return real_part, imag_part


def halves(real_part, imag_part):
    return [real_part, imag_part] if CHUNKS == 1 else pack(real_part, imag_part)


def cut_kernel(traces_ref, *out_refs):
    parts = halves(traces_ref[0].astype(jnp.float32), traces_ref[1].astype(jnp.float32))
    for out_ref, part in zip(out_refs, parts):
        out_ref[...] = part.astype(jnp.bfloat16)


def cut_window(traces):
    rows = traces.shape[1]
    return pl.pallas_call(
        cut_kernel,
        grid=(1,),
        in_specs=[pl.BlockSpec((2, rows, WIN), lambda i: (0, 0, 0))],
        out_specs=[pl.BlockSpec((rows, WIN), lambda i: (0, 0))] * 2,
        out_shape=[jax.ShapeDtypeStruct((rows, WIN), jnp.bfloat16)] * 2,
        compiler_params=params(),
        cost_estimate=cost(rows * WIN, 8 * rows * WIN),
        name="cut_window",
    )(traces)


def pick_kernel(traces_ref, miss_ref, recv_ref, live_ref, real_ref, imag_ref, hot_ref):
    @pl.when(pl.program_id(0) == 0)
    def _():
        hot = one_hot(miss_ref[...], hot_ref.shape[0], jnp.bfloat16)
        alive = jnp.dot(recv_ref[...], hot, preferred_element_type=jnp.float32)
        hot_ref[...] = hot * alive[0:1].astype(jnp.bfloat16)

    misses = real_ref.shape[0]
    for part, out_ref in enumerate((real_ref, imag_ref)):
        picked = jnp.dot(traces_ref[part], hot_ref[...], preferred_element_type=jnp.float32)
        turned = picked.T * live_ref[0:1, :]
        out_ref[...] = turned[:misses].astype(jnp.bfloat16)


def pick_columns(traces, miss_lanes, recv8, live8, misses):
    _, rows, cols = traces.shape
    block = row_block(rows)
    return pl.pallas_call(
        pick_kernel,
        grid=(rows // block,),
        in_specs=[
            pl.BlockSpec((2, block, cols), lambda i: (0, i, 0)),
            pl.BlockSpec((1, LANES), lambda i: (0, 0)),
            pl.BlockSpec((8, cols), lambda i: (0, 0)),
            pl.BlockSpec((8, block), lambda i: (0, i)),
        ],
        out_specs=[pl.BlockSpec((misses, block), lambda i: (0, i))] * 2,
        out_shape=[jax.ShapeDtypeStruct((misses, rows), jnp.bfloat16)] * 2,
        scratch_shapes=[pltpu.VMEM((cols, LANES), jnp.bfloat16)],
        compiler_params=params(),
        cost_estimate=cost(4 * rows * cols * 2 * LANES, 4 * rows * cols),
        name="pick_columns",
    )(traces, miss_lanes, recv8, live8)


def fill_kernel(counts, first_half, real_ref, imag_ref, miss_ref, recv_ref, *refs):
    out_ref = refs[-1]
    rows = out_ref.shape[0]
    misses = real_ref.shape[0]
    hot = one_hot(miss_ref[...], rows, jnp.float32)
    dead = jnp.max(hot, axis=1, keepdims=True)
    hot = hot[:, :misses].astype(jnp.bfloat16)
    patches = halves(real_ref[...].astype(jnp.float32), imag_ref[...].astype(jnp.float32))
    mask = recv_ref[...].astype(jnp.float32)
    mask = halves(mask, mask)[0][0:1, :]
    used = 0
    for index, count in enumerate(counts):
        arrived = refs[used][...].astype(jnp.float32)
        for more in refs[used + 1:used + count]:
            arrived = arrived + more[...].astype(jnp.float32)
        used += count
        patch = patches[first_half + index].astype(jnp.bfloat16)
        moved = jnp.dot(hot, patch, preferred_element_type=jnp.float32)
        filled = arrived * ((1.0 - dead) * mask) + moved
        out_ref[:, index * WIN:(index + 1) * WIN] = filled.astype(jnp.bfloat16)


def fill_window(first_half, arrived, picked, miss_lanes, recv8):
    rows = arrived[0][0].shape[0]
    misses = picked[0].shape[0]
    counts = tuple(len(group) for group in arrived)
    flat = [part for group in arrived for part in group]
    lanes = len(counts) * WIN
    whole = pl.BlockSpec((rows, WIN), lambda i: (0, 0))
    return pl.pallas_call(
        functools.partial(fill_kernel, counts, first_half),
        grid=(1,),
        in_specs=[
            pl.BlockSpec((misses, WIN), lambda i: (0, 0)),
            pl.BlockSpec((misses, WIN), lambda i: (0, 0)),
            pl.BlockSpec((1, LANES), lambda i: (0, 0)),
            pl.BlockSpec((8, WIN), lambda i: (0, 0)),
        ]
        + [whole] * len(flat),
        out_specs=pl.BlockSpec((rows, lanes), lambda i: (0, 0)),
        out_shape=jax.ShapeDtypeStruct((rows, lanes), jnp.bfloat16),
        compiler_params=params(),
        cost_estimate=cost(4 * rows * LANES * lanes, 8 * rows * lanes),
        name="fill_window",
    )(*picked, miss_lanes, recv8, *flat)


def complex_rows(real_rows, imag_rows, right):
    first = jnp.dot(real_rows, right, preferred_element_type=jnp.float32)
    second = jnp.dot(imag_rows, right, preferred_element_type=jnp.float32)
    if CHUNKS == 1:
        real_part = first[:, :WIN] - second[:, WIN:]
        imag_part = first[:, WIN:] + second[:, :WIN]
        return jnp.concatenate([real_part, imag_part], axis=1)
    turned = pltpu.roll(second, WIDTH, 1)
    low = lax.broadcasted_iota(jnp.int32, first.shape, 1) < WIDTH
    return first + jnp.where(low, -turned, turned)


def choose(out_ref, pick, refs):
    for index, ref in enumerate(refs):

        @pl.when(pick == index)
        def _():
            out_ref[...] = ref[...]


def product_kernel(counts, pick_ref, recv_ref, *refs):
    tiles, refs = refs[:4], refs[4:]
    total, places = sum(counts), len(counts)
    out_refs, right_refs = refs[total:total + places], refs[total + places:-1]
    sem = refs[-1]

    @pl.when(pl.program_id(0) == 0)
    def _():
        used = 0
        for place, count in enumerate(counts):
            for index, ref in enumerate(refs[used:used + count]):

                @pl.when(pick_ref[place] == index)
                def _():
                    copy = pltpu.make_async_copy(ref, right_refs[place], sem.at[place])
                    copy.start()
                    copy.wait()

            used += count

    recv = recv_ref[0:1, :]
    half = tiles[0].shape[1]
    for side in range(2):
        real_rows, imag_rows = (tiles[2 * part + side][0] * recv for part in range(2))
        for out_ref, right_ref in zip(out_refs, right_refs):
            out_ref[side * half:(side + 1) * half, :] = complex_rows(
                real_rows, imag_rows, right_ref[...]
            )


def products(traces, recv8, groups):
    _, rows, cols = traces.shape
    lanes = groups[0][1][0].shape[1]
    counts = tuple(len(sources) for _, sources in groups)
    flat = [source for _, sources in groups for source in sources]
    picks = jnp.stack([pick for pick, _ in groups]).astype(jnp.int32)
    block = row_block(rows)
    quarter = lambda part, side: pl.BlockSpec(
        (1, block // 2, cols), lambda i: (part, 2 * i + side, 0)
    )
    return pl.pallas_call(
        functools.partial(product_kernel, counts),
        grid=(rows // block,),
        in_specs=[
            SMEM,
            pl.BlockSpec((8, cols), lambda i: (0, 0)),
        ]
        + [quarter(part, side) for part in range(2) for side in range(2)]
        + [pl.BlockSpec(memory_space=pl.ANY)] * len(flat),
        out_specs=[pl.BlockSpec((block, lanes), lambda i: (i, 0))] * len(groups),
        out_shape=[jax.ShapeDtypeStruct((rows, lanes), jnp.float32)] * len(groups),
        scratch_shapes=[pltpu.VMEM((cols, lanes), jnp.bfloat16)] * len(groups)
        + [pltpu.SemaphoreType.DMA((len(groups),))],
        compiler_params=params(),
        cost_estimate=cost(8 * rows * cols * lanes * len(groups), 4 * rows * lanes),
        name="products",
    )(picks, recv8, *[traces] * 4, *flat)


def extra_kernel(counts, pick_ref, real_ref, imag_ref, *refs):
    out_ref, right_ref = refs[-2:]
    used = 0
    for place, count in enumerate(counts):
        choose(right_ref, pick_ref[2 * place], refs[used:used + count])
        used += count
        out_ref[pick_ref[2 * place + 1]] = complex_rows(real_ref[...], imag_ref[...], right_ref[...])


def extra_products(rows, groups):
    misses, cols = rows[0].shape
    lanes = groups[0][2][0].shape[1]
    counts = tuple(len(sources) for _, _, sources in groups)
    flat = [source for _, _, sources in groups for source in sources]
    picks = jnp.stack([x for pick, place, _ in groups for x in (pick, place)]).astype(jnp.int32)
    return pl.pallas_call(
        functools.partial(extra_kernel, counts),
        in_specs=[SMEM] + [VMEM] * (2 + len(flat)),
        out_specs=VMEM,
        out_shape=jax.ShapeDtypeStruct((len(groups), misses, lanes), jnp.float32),
        scratch_shapes=[pltpu.VMEM((cols, lanes), jnp.bfloat16)],
        compiler_params=params(),
        cost_estimate=cost(8 * misses * cols * lanes * len(groups), 4 * cols * lanes),
        name="extra_products",
    )(picks, *rows, *flat)


def finish_kernel(wave_ref, miss_ref, recv_ref, tile_ref, real_ref, imag_ref, *refs):
    out_ref, row_ref = refs[-2:]
    totals = [ref[...] for ref in refs[:-2]]

    def write(target, window, chunks):
        real_part, imag_part = unpack(chunks)
        real_pred = real_part * wave_ref[0] - imag_part * wave_ref[1]
        imag_pred = imag_part * wave_ref[0] + real_part * wave_ref[1]
        target[0] = window[0] - real_pred
        target[1] = window[1] - imag_pred

    recv = recv_ref[0:1, :].astype(jnp.float32)
    write(out_ref, [tile_ref[part].astype(jnp.float32) * recv for part in range(2)], totals[:CHUNKS])
    write(row_ref, [ref[...].astype(jnp.float32) for ref in (real_ref, imag_ref)], totals[CHUNKS:])

    def place(m, carry):
        for part in range(2):
            out_ref[part, pl.ds(miss_ref[m], 1), :] = row_ref[part, pl.ds(m, 1), :]
        return carry

    lax.fori_loop(0, row_ref.shape[1], place, 0, unroll=8)


def finish(wave, miss, recv8, traces, extra, terms):
    _, rows, _ = traces.shape
    misses = extra[0].shape[0]
    flat = [term for group in terms for term in group]
    window = lambda size: pl.BlockSpec((2, size, WIN), lambda i: (0, 0, 0))
    return pl.pallas_call(
        finish_kernel,
        grid=(1,),
        in_specs=[SMEM, SMEM, pl.BlockSpec((8, WIN), lambda i: (0, 0)), window(rows)]
        + [pl.BlockSpec((misses, WIN), lambda i: (0, 0))] * 2
        + [VMEM] * len(flat),
        out_specs=window(rows),
        out_shape=jax.ShapeDtypeStruct((2, rows, WIN), jnp.float32),
        scratch_shapes=[pltpu.VMEM((2, misses, WIN), jnp.float32)],
        compiler_params=params(),
        cost_estimate=cost(20 * rows * WIN, 40 * rows * WIN),
        name="finish",
    )(wave, miss, recv8, traces, *extra, *flat)


def mirror_routes(grid_size):
    cells = [(a, b) for a in range(grid_size) for b in range(grid_size)]
    index = lambda row, col: row * grid_size + col
    whole = [(index(a, b), index(b, a)) for a, b in cells]
    near = [(index(a, b), index(b, a)) for a, b in cells if a // 2 == b // 2]
    far = [(a, b) for a, b in cells if a // 2 != b // 2]
    hop = lambda a, b: index(a, a // 2 * 2 + b % 2)
    first = [(index(a, b), hop(a, b)) for a, b in far]
    second = [(hop(a, b), index(b, a)) for a, b in far]
    if len({target for _, target in first}) < len(first):
        return whole, None
    return whole, (near, first, second)


def sources_of(up, down, offset, grid_size, row_index):
    places, sources = [], []
    for row in range(grid_size):
        other = row ^ offset
        source = up[row - other] if other < row else down[other - row]
        known = [index for index, seen in enumerate(sources) if seen is source]
        places.append(known[0] if known else len(sources))
        if not known:
            sources.append(source)
    pick = jnp.zeros((), jnp.int32)
    for row, place in enumerate(places):
        pick = jnp.where(row_index == row, place, pick)
    return pick, sources


def sum_route(offset, grid_size, stride, skip):
    route = []
    for row in range(grid_size):
        for col in range(grid_size):
            if ((col ^ row ^ offset) & ~skip) % (2 * stride) == stride:
                route.append((row * grid_size + col, row * grid_size + (col ^ stride)))
    return route


def local(traces, recv_live, missing, wavelet):
    tile = traces.shape[1]
    grid_size = lax.axis_size("row")
    misses = missing.shape[1]
    order = recv_live.shape[0]
    row_index = lax.axis_index("row")
    col_index = lax.axis_index("col")
    whole, hops = mirror_routes(grid_size)

    def move(block, route):
        return lax.ppermute(block, ("row", "col"), route)

    def transpose(block):
        return move(block, whole)

    def transpose_round(block):
        if hops is None:
            return [move(block, whole)]
        near, first, second = hops
        return [move(move(block, first), second), move(block, near)]

    direct, round_about = cut_window(traces)
    arrived = [[transpose(direct)], transpose_round(round_about)]
    if CHUNKS == 1:
        arrived = [arrived]
    else:
        arrived = [arrived[:1], arrived[1:]]

    miss_row = lax.dynamic_index_in_dim(missing, row_index, 0, keepdims=False)
    miss_col = lax.dynamic_index_in_dim(missing, col_index, 0, keepdims=False)
    as_lanes = lambda m: jnp.pad(m, (0, LANES - misses), constant_values=-1)[None]
    miss_col_lanes = as_lanes(miss_col)
    positions = jnp.arange(tile, dtype=jnp.int32)
    live_row = jnp.all(positions[:, None] != miss_row[None, :], axis=1)
    live8 = jnp.broadcast_to(live_row.astype(jnp.float32)[None], (8, tile))
    recv_mask = (recv_live == 1).astype(jnp.bfloat16)
    recv_row = lax.dynamic_slice_in_dim(recv_mask, row_index * tile, WIN)
    recv_row8 = jnp.broadcast_to(recv_row[None], (8, WIN))
    recv_col = lax.dynamic_slice_in_dim(recv_mask, col_index * tile, tile)
    recv_col8 = jnp.broadcast_to(recv_col[None], (8, tile))

    picked = pick_columns(traces, miss_col_lanes, recv_col8, live8, misses)
    both = jnp.concatenate(picked)
    extra = None
    apart = row_index ^ col_index
    strides = [2**bit for bit in range(grid_size.bit_length() - 1)]
    terms, extra_terms = [], []
    for chunk in range(CHUNKS):
        window = fill_window(chunk, arrived[chunk], picked, miss_col_lanes, recv_row8)
        if extra is None:
            both, window = lax.optimization_barrier((both, window))
            both = transpose(both)
            extra = [both[:misses], both[misses:]]
        up, down = [window], [window]
        sums = []

        def hop(distance):
            ends = [(i, i + 1) for i in range(distance - 1, grid_size - 1)]
            back = [(i + 1, i) for i in range(grid_size - distance)]
            up.append(lax.ppermute(up[-1], "row", ends))
            down.append(lax.ppermute(down[-1], "row", back))

        def add_up(total, offset, strides, skip):
            for stride in strides:
                total = total + move(total, sum_route(offset, grid_size, stride, skip))
            return total

        def shrink(total):
            unit = jnp.maximum(jnp.max(jnp.abs(total)), TINY) * (1.0 / HALF_TOP)
            sent = (total * (1.0 / unit)).astype(jnp.float16)
            return sent, jnp.broadcast_to(unit, (1, LANES))

        def last(shrunk, offset, skip):
            route = sum_route(offset, grid_size, strides[-1], skip)
            return [move(part, route) for part in shrunk]

        def options(offset):
            return sources_of(up, down, offset, grid_size, row_index)

        hop(1)
        extra, up[-1], down[-1] = lax.optimization_barrier((extra, up[-1], down[-1]))
        hop(2)
        other_core = [(i, i ^ 1) for i in range(grid_size)]
        odd = apart & 1

        def pair_sum(first, mask):
            pick0, sources0 = options(first)
            pick1, sources1 = options(first + 1)
            pick1 = pick1 + len(sources0)
            both_sources = sources0 + sources1
            keep, sent = products(
                traces,
                mask,
                [
                    (jnp.where(odd == 1, pick1, pick0), both_sources),
                    (jnp.where(odd == 1, pick0, pick1), both_sources),
                ],
            )
            return add_up(keep + lax.ppermute(sent, "col", other_core), first, strides[1:-1], 1)

        sums = [pair_sum(0, recv_col8)]
        shrunk, up[-1], down[-1] = lax.optimization_barrier((shrink(sums[0]), up[-1], down[-1]))
        for distance in range(3, grid_size):
            hop(distance)
        got = [last(shrunk, 0, 1)]
        mask = recv_col8
        for first in range(2, grid_size, 2):
            if first == grid_size - 2:
                group = [(pick, apart ^ offset, sources) for offset in range(grid_size)
                         for pick, sources in [options(offset)]]
                rest = extra_products(extra, group)
                mask, rest = lax.optimization_barrier((mask, rest))
            sums.append(pair_sum(first, mask))
            got.append(last(shrink(sums[-1]), first, 1))
        whole_sum = None
        for index, (part, (sent, units)) in enumerate(zip(sums, got)):
            mine = apart // 2 == index
            term = jnp.where(mine, part, 0.0) + sent.astype(jnp.float32) * units[0, 0]
            whole_sum = term if whole_sum is None else whole_sum + term
        terms.append((whole_sum,))
        for stride in strides:
            pairs = [(i, i ^ stride) for i in range(grid_size)]
            arrive = lax.ppermute(rest[1::2], "col", pairs)
            rest = rest[0::2] + arrive
        extra_terms.append((rest[0],))
    wave = wavelet * (1.0 / math.sqrt(order))
    return finish(wave, miss_row, recv_col8, traces, extra, terms + extra_terms)


def solution(mesh):
    in_specs = (P("freq", "row", "col"), P("freq"), P("freq", None), P("freq"))
    out_specs = P("freq", "row", "col")
    return jax.shard_map(local, mesh=mesh, in_specs=in_specs, out_specs=out_specs, check_vma=False)
```

```python
import functools
import math

import jax
import jax.numpy as jnp
from jax import lax
from jax.experimental import pallas as pl
from jax.experimental.pallas import tpu as pltpu
from jax.sharding import PartitionSpec as P

WIN = 128
LANES = 128
CHUNKS = 1
WIDTH = WIN // CHUNKS
TINY = 1e-30
HALF_TOP = 32768.0
VMEM_LIMIT = 48 * 2**20
VMEM = pl.BlockSpec(memory_space=pltpu.VMEM)
SMEM = pl.BlockSpec(memory_space=pltpu.SMEM)


def params():
    return pltpu.CompilerParams(vmem_limit_bytes=VMEM_LIMIT)


def cost(flops, accessed):
    return pl.CostEstimate(
        flops=int(flops) // 64, bytes_accessed=int(accessed) // 64, transcendentals=0
    )


def row_block(rows):
    for size in (512, 384, 256, 128):
        if rows % size == 0:
            return size
    return rows


def one_hot(positions_row, rows, dtype):
    lanes = positions_row.shape[1]
    row_ids = lax.broadcasted_iota(jnp.int32, (rows, lanes), 0)
    return jnp.where(row_ids == positions_row, 1.0, 0.0).astype(dtype)


def pack(real_part, imag_part):
    if CHUNKS == 1:
        return [jnp.concatenate([real_part, imag_part], axis=1)]
    first = lax.broadcasted_iota(jnp.int32, real_part.shape, 1) < WIDTH
    low = jnp.where(first, real_part, pltpu.roll(imag_part, WIDTH, 1))
    high = jnp.where(first, pltpu.roll(real_part, WIDTH, 1), imag_part)
    return [low, high]


def unpack(chunks):
    if CHUNKS == 1:
        return chunks[0][:, :WIN], chunks[0][:, WIN:]
    low, high = chunks
    first = lax.broadcasted_iota(jnp.int32, low.shape, 1) < WIDTH
    real_part = jnp.where(first, low, pltpu.roll(high, WIDTH, 1))
    imag_part = jnp.where(first, pltpu.roll(low, WIDTH, 1), high)
    return real_part, imag_part


def halves(real_part, imag_part):
    return [real_part, imag_part] if CHUNKS == 1 else pack(real_part, imag_part)


def cut_kernel(traces_ref, *out_refs):
    parts = halves(traces_ref[0].astype(jnp.float32), traces_ref[1].astype(jnp.float32))
    for out_ref, part in zip(out_refs, parts):
        out_ref[...] = part.astype(jnp.bfloat16)


def cut_window(traces):
    rows = traces.shape[1]
    return pl.pallas_call(
        cut_kernel,
        grid=(1,),
        in_specs=[pl.BlockSpec((2, rows, WIN), lambda i: (0, 0, 0))],
        out_specs=[pl.BlockSpec((rows, WIN), lambda i: (0, 0))] * 2,
        out_shape=[jax.ShapeDtypeStruct((rows, WIN), jnp.bfloat16)] * 2,
        compiler_params=params(),
        cost_estimate=cost(rows * WIN, 8 * rows * WIN),
        name="cut_window",
    )(traces)


def pick_kernel(traces_ref, miss_ref, recv_ref, live_ref, real_ref, imag_ref, hot_ref):
    @pl.when(pl.program_id(0) == 0)
    def _():
        hot = one_hot(miss_ref[...], hot_ref.shape[0], jnp.bfloat16)
        alive = jnp.dot(recv_ref[...], hot, preferred_element_type=jnp.float32)
        hot_ref[...] = hot * alive[0:1].astype(jnp.bfloat16)

    misses = real_ref.shape[0]
    for part, out_ref in enumerate((real_ref, imag_ref)):
        picked = jnp.dot(traces_ref[part], hot_ref[...], preferred_element_type=jnp.float32)
        turned = picked.T * live_ref[0:1, :]
        out_ref[...] = turned[:misses].astype(jnp.bfloat16)


def pick_columns(traces, miss_lanes, recv8, live8, misses):
    _, rows, cols = traces.shape
    block = row_block(rows)
    return pl.pallas_call(
        pick_kernel,
        grid=(rows // block,),
        in_specs=[
            pl.BlockSpec((2, block, cols), lambda i: (0, i, 0)),
            pl.BlockSpec((1, LANES), lambda i: (0, 0)),
            pl.BlockSpec((8, cols), lambda i: (0, 0)),
            pl.BlockSpec((8, block), lambda i: (0, i)),
        ],
        out_specs=[pl.BlockSpec((misses, block), lambda i: (0, i))] * 2,
        out_shape=[jax.ShapeDtypeStruct((misses, rows), jnp.bfloat16)] * 2,
        scratch_shapes=[pltpu.VMEM((cols, LANES), jnp.bfloat16)],
        compiler_params=params(),
        cost_estimate=cost(4 * rows * cols * 2 * LANES, 4 * rows * cols),
        name="pick_columns",
    )(traces, miss_lanes, recv8, live8)


def fill_kernel(counts, first_half, real_ref, imag_ref, miss_ref, recv_ref, *refs):
    out_ref = refs[-1]
    rows = out_ref.shape[0]
    misses = real_ref.shape[0]
    hot = one_hot(miss_ref[...], rows, jnp.float32)
    dead = jnp.max(hot, axis=1, keepdims=True)
    hot = hot[:, :misses].astype(jnp.bfloat16)
    patches = halves(real_ref[...].astype(jnp.float32), imag_ref[...].astype(jnp.float32))
    mask = recv_ref[...].astype(jnp.float32)
    mask = halves(mask, mask)[0][0:1, :]
    used = 0
    for index, count in enumerate(counts):
        arrived = refs[used][...].astype(jnp.float32)
        for more in refs[used + 1:used + count]:
            arrived = arrived + more[...].astype(jnp.float32)
        used += count
        patch = patches[first_half + index].astype(jnp.bfloat16)
        moved = jnp.dot(hot, patch, preferred_element_type=jnp.float32)
        filled = arrived * ((1.0 - dead) * mask) + moved
        out_ref[:, index * WIN:(index + 1) * WIN] = filled.astype(jnp.bfloat16)


def fill_window(first_half, arrived, picked, miss_lanes, recv8):
    rows = arrived[0][0].shape[0]
    misses = picked[0].shape[0]
    counts = tuple(len(group) for group in arrived)
    flat = [part for group in arrived for part in group]
    lanes = len(counts) * WIN
    whole = pl.BlockSpec((rows, WIN), lambda i: (0, 0))
    return pl.pallas_call(
        functools.partial(fill_kernel, counts, first_half),
        grid=(1,),
        in_specs=[
            pl.BlockSpec((misses, WIN), lambda i: (0, 0)),
            pl.BlockSpec((misses, WIN), lambda i: (0, 0)),
            pl.BlockSpec((1, LANES), lambda i: (0, 0)),
            pl.BlockSpec((8, WIN), lambda i: (0, 0)),
        ]
        + [whole] * len(flat),
        out_specs=pl.BlockSpec((rows, lanes), lambda i: (0, 0)),
        out_shape=jax.ShapeDtypeStruct((rows, lanes), jnp.bfloat16),
        compiler_params=params(),
        cost_estimate=cost(4 * rows * LANES * lanes, 8 * rows * lanes),
        name="fill_window",
    )(*picked, miss_lanes, recv8, *flat)


def complex_rows(real_rows, imag_rows, right):
    first = jnp.dot(real_rows, right, preferred_element_type=jnp.float32)
    second = jnp.dot(imag_rows, right, preferred_element_type=jnp.float32)
    if CHUNKS == 1:
        real_part = first[:, :WIN] - second[:, WIN:]
        imag_part = first[:, WIN:] + second[:, :WIN]
        return jnp.concatenate([real_part, imag_part], axis=1)
    turned = pltpu.roll(second, WIDTH, 1)
    low = lax.broadcasted_iota(jnp.int32, first.shape, 1) < WIDTH
    return first + jnp.where(low, -turned, turned)


def choose(out_ref, pick, refs):
    for index, ref in enumerate(refs):

        @pl.when(pick == index)
        def _():
            out_ref[...] = ref[...]


def product_kernel(counts, pick_ref, recv_ref, *refs):
    tiles, refs = refs[:4], refs[4:]
    total, places = sum(counts), len(counts)
    out_refs, right_refs = refs[total:total + places], refs[total + places:-1]
    sem = refs[-1]

    @pl.when(pl.program_id(0) == 0)
    def _():
        used = 0
        for place, count in enumerate(counts):
            for index, ref in enumerate(refs[used:used + count]):

                @pl.when(pick_ref[place] == index)
                def _():
                    copy = pltpu.make_async_copy(ref, right_refs[place], sem.at[place])
                    copy.start()
                    copy.wait()

            used += count

    recv = recv_ref[0:1, :]
    half = tiles[0].shape[1]
    for side in range(2):
        real_rows, imag_rows = (tiles[2 * part + side][0] * recv for part in range(2))
        for out_ref, right_ref in zip(out_refs, right_refs):
            out_ref[side * half:(side + 1) * half, :] = complex_rows(
                real_rows, imag_rows, right_ref[...]
            )


def products(traces, recv8, groups):
    _, rows, cols = traces.shape
    lanes = groups[0][1][0].shape[1]
    counts = tuple(len(sources) for _, sources in groups)
    flat = [source for _, sources in groups for source in sources]
    picks = jnp.stack([pick for pick, _ in groups]).astype(jnp.int32)
    block = rows // 4 if rows % 128 == 0 else rows
    quarter = lambda part, side: pl.BlockSpec(
        (1, block // 2, cols), lambda i: (part, 2 * i + side, 0)
    )
    return pl.pallas_call(
        functools.partial(product_kernel, counts),
        grid=(rows // block,),
        in_specs=[
            SMEM,
            pl.BlockSpec((8, cols), lambda i: (0, 0)),
        ]
        + [quarter(part, side) for part in range(2) for side in range(2)]
        + [pl.BlockSpec(memory_space=pl.ANY)] * len(flat),
        out_specs=[pl.BlockSpec((block, lanes), lambda i: (i, 0))] * len(groups),
        out_shape=[jax.ShapeDtypeStruct((rows, lanes), jnp.float32)] * len(groups),
        scratch_shapes=[pltpu.VMEM((cols, lanes), jnp.bfloat16)] * len(groups)
        + [pltpu.SemaphoreType.DMA((len(groups),))],
        compiler_params=params(),
        cost_estimate=cost(8 * rows * cols * lanes * len(groups), 4 * rows * lanes),
        name="products",
    )(picks, recv8, *[traces] * 4, *flat)


def extra_kernel(counts, pick_ref, real_ref, imag_ref, *refs):
    out_ref, right_ref = refs[-2:]
    used = 0
    for place, count in enumerate(counts):
        choose(right_ref, pick_ref[2 * place], refs[used:used + count])
        used += count
        out_ref[pick_ref[2 * place + 1]] = complex_rows(real_ref[...], imag_ref[...], right_ref[...])


def extra_products(rows, groups):
    misses, cols = rows[0].shape
    lanes = groups[0][2][0].shape[1]
    counts = tuple(len(sources) for _, _, sources in groups)
    flat = [source for _, _, sources in groups for source in sources]
    picks = jnp.stack([x for pick, place, _ in groups for x in (pick, place)]).astype(jnp.int32)
    return pl.pallas_call(
        functools.partial(extra_kernel, counts),
        in_specs=[SMEM] + [VMEM] * (2 + len(flat)),
        out_specs=VMEM,
        out_shape=jax.ShapeDtypeStruct((len(groups), misses, lanes), jnp.float32),
        scratch_shapes=[pltpu.VMEM((cols, lanes), jnp.bfloat16)],
        compiler_params=params(),
        cost_estimate=cost(8 * misses * cols * lanes * len(groups), 4 * cols * lanes),
        name="extra_products",
    )(picks, *rows, *flat)


def finish_kernel(wave_ref, miss_ref, recv_ref, tile_ref, real_ref, imag_ref, *refs):
    out_ref, row_ref = refs[-2:]
    totals = [ref[...] for ref in refs[:-2]]

    def write(target, window, chunks):
        real_part, imag_part = unpack(chunks)
        real_pred = real_part * wave_ref[0] - imag_part * wave_ref[1]
        imag_pred = imag_part * wave_ref[0] + real_part * wave_ref[1]
        target[0] = window[0] - real_pred
        target[1] = window[1] - imag_pred

    recv = recv_ref[0:1, :].astype(jnp.float32)
    write(out_ref, [tile_ref[part].astype(jnp.float32) * recv for part in range(2)], totals[:CHUNKS])
    write(row_ref, [ref[...].astype(jnp.float32) for ref in (real_ref, imag_ref)], totals[CHUNKS:])

    def place(m, carry):
        for part in range(2):
            out_ref[part, pl.ds(miss_ref[m], 1), :] = row_ref[part, pl.ds(m, 1), :]
        return carry

    lax.fori_loop(0, row_ref.shape[1], place, 0, unroll=8)


def finish(wave, miss, recv8, traces, extra, terms):
    _, rows, _ = traces.shape
    misses = extra[0].shape[0]
    flat = [term for group in terms for term in group]
    window = lambda size: pl.BlockSpec((2, size, WIN), lambda i: (0, 0, 0))
    return pl.pallas_call(
        finish_kernel,
        grid=(1,),
        in_specs=[SMEM, SMEM, pl.BlockSpec((8, WIN), lambda i: (0, 0)), window(rows)]
        + [pl.BlockSpec((misses, WIN), lambda i: (0, 0))] * 2
        + [VMEM] * len(flat),
        out_specs=window(rows),
        out_shape=jax.ShapeDtypeStruct((2, rows, WIN), jnp.float32),
        scratch_shapes=[pltpu.VMEM((2, misses, WIN), jnp.float32)],
        compiler_params=params(),
        cost_estimate=cost(20 * rows * WIN, 40 * rows * WIN),
        name="finish",
    )(wave, miss, recv8, traces, *extra, *flat)


def mirror_routes(grid_size):
    cells = [(a, b) for a in range(grid_size) for b in range(grid_size)]
    index = lambda row, col: row * grid_size + col
    whole = [(index(a, b), index(b, a)) for a, b in cells]
    near = [(index(a, b), index(b, a)) for a, b in cells if a // 2 == b // 2]
    far = [(a, b) for a, b in cells if a // 2 != b // 2]
    hop = lambda a, b: index(a, a // 2 * 2 + b % 2)
    first = [(index(a, b), hop(a, b)) for a, b in far]
    second = [(hop(a, b), index(b, a)) for a, b in far]
    if len({target for _, target in first}) < len(first):
        return whole, None
    return whole, (near, first, second)


def sources_of(up, down, offset, grid_size, row_index):
    places, sources = [], []
    for row in range(grid_size):
        other = row ^ offset
        source = up[row - other] if other < row else down[other - row]
        known = [index for index, seen in enumerate(sources) if seen is source]
        places.append(known[0] if known else len(sources))
        if not known:
            sources.append(source)
    pick = jnp.zeros((), jnp.int32)
    for row, place in enumerate(places):
        pick = jnp.where(row_index == row, place, pick)
    return pick, sources


def sum_route(offset, grid_size, stride, skip):
    route = []
    for row in range(grid_size):
        for col in range(grid_size):
            if ((col ^ row ^ offset) & ~skip) % (2 * stride) == stride:
                route.append((row * grid_size + col, row * grid_size + (col ^ stride)))
    return route


def local(traces, recv_live, missing, wavelet):
    tile = traces.shape[1]
    grid_size = lax.axis_size("row")
    misses = missing.shape[1]
    order = recv_live.shape[0]
    row_index = lax.axis_index("row")
    col_index = lax.axis_index("col")
    whole, hops = mirror_routes(grid_size)

    def move(block, route):
        return lax.ppermute(block, ("row", "col"), route)

    def transpose(block):
        return move(block, whole)

    def transpose_round(block):
        if hops is None:
            return [move(block, whole)]
        near, first, second = hops
        return [move(move(block, first), second), move(block, near)]

    direct, round_about = cut_window(traces)
    arrived = [[transpose(direct)], transpose_round(round_about)]
    if CHUNKS == 1:
        arrived = [arrived]
    else:
        arrived = [arrived[:1], arrived[1:]]

    miss_row = lax.dynamic_index_in_dim(missing, row_index, 0, keepdims=False)
    miss_col = lax.dynamic_index_in_dim(missing, col_index, 0, keepdims=False)
    as_lanes = lambda m: jnp.pad(m, (0, LANES - misses), constant_values=-1)[None]
    miss_col_lanes = as_lanes(miss_col)
    positions = jnp.arange(tile, dtype=jnp.int32)
    live_row = jnp.all(positions[:, None] != miss_row[None, :], axis=1)
    live8 = jnp.broadcast_to(live_row.astype(jnp.float32)[None], (8, tile))
    recv_mask = (recv_live == 1).astype(jnp.bfloat16)
    recv_row = lax.dynamic_slice_in_dim(recv_mask, row_index * tile, WIN)
    recv_row8 = jnp.broadcast_to(recv_row[None], (8, WIN))
    recv_col = lax.dynamic_slice_in_dim(recv_mask, col_index * tile, tile)
    recv_col8 = jnp.broadcast_to(recv_col[None], (8, tile))

    picked = pick_columns(traces, miss_col_lanes, recv_col8, live8, misses)
    both = transpose(jnp.concatenate(picked))
    extra = [both[:misses], both[misses:]]
    apart = row_index ^ col_index
    strides = [2**bit for bit in range(grid_size.bit_length() - 1)]
    terms, extra_terms = [], []
    for chunk in range(CHUNKS):
        window = fill_window(chunk, arrived[chunk], picked, miss_col_lanes, recv_row8)
        up, down = [window], [window]
        sums = []

        def hop(distance):
            ends = [(i, i + 1) for i in range(distance - 1, grid_size - 1)]
            back = [(i + 1, i) for i in range(grid_size - distance)]
            up.append(lax.ppermute(up[-1], "row", ends))
            down.append(lax.ppermute(down[-1], "row", back))

        def add_up(total, offset, strides, skip):
            for stride in strides:
                total = total + move(total, sum_route(offset, grid_size, stride, skip))
            return total

        def shrink(total):
            unit = jnp.maximum(jnp.max(jnp.abs(total)), TINY) * (1.0 / HALF_TOP)
            sent = (total * (1.0 / unit)).astype(jnp.float16)
            return sent, jnp.broadcast_to(unit, (1, LANES))

        def last(shrunk, offset, skip):
            route = sum_route(offset, grid_size, strides[-1], skip)
            return [move(part, route) for part in shrunk]

        def options(offset):
            return sources_of(up, down, offset, grid_size, row_index)

        hop(1)
        extra, up[-1], down[-1] = lax.optimization_barrier((extra, up[-1], down[-1]))
        hop(2)
        other_core = [(i, i ^ 1) for i in range(grid_size)]
        odd = apart & 1

        def pair_sum(first, mask):
            pick0, sources0 = options(first)
            pick1, sources1 = options(first + 1)
            pick1 = pick1 + len(sources0)
            both_sources = sources0 + sources1
            keep, sent = products(
                traces,
                mask,
                [
                    (jnp.where(odd == 1, pick1, pick0), both_sources),
                    (jnp.where(odd == 1, pick0, pick1), both_sources),
                ],
            )
            return add_up(keep + lax.ppermute(sent, "col", other_core), first, strides[1:-1], 1)

        sums = [pair_sum(0, recv_col8)]
        shrunk, up[-1], down[-1] = lax.optimization_barrier((shrink(sums[0]), up[-1], down[-1]))
        for distance in range(3, grid_size):
            hop(distance)
        got = [last(shrunk, 0, 1)]
        mask = recv_col8
        for first in range(2, grid_size, 2):
            if first == grid_size - 2:
                group = [(pick, apart ^ offset, sources) for offset in range(grid_size)
                         for pick, sources in [options(offset)]]
                rest = extra_products(extra, group)
                mask, rest = lax.optimization_barrier((mask, rest))
            sums.append(pair_sum(first, mask))
            got.append(last(shrink(sums[-1]), first, 1))
        whole_sum = None
        for index, (part, (sent, units)) in enumerate(zip(sums, got)):
            mine = apart // 2 == index
            term = jnp.where(mine, part, 0.0) + sent.astype(jnp.float32) * units[0, 0]
            whole_sum = term if whole_sum is None else whole_sum + term
        terms.append((whole_sum,))
        for stride in strides:
            pairs = [(i, i ^ stride) for i in range(grid_size)]
            arrive = lax.ppermute(rest[1::2], "col", pairs)
            rest = rest[0::2] + arrive
        extra_terms.append((rest[0],))
    wave = wavelet * (1.0 / math.sqrt(order))
    return finish(wave, miss_row, recv_col8, traces, extra, terms + extra_terms)


def solution(mesh):
    in_specs = (P("freq", "row", "col"), P("freq"), P("freq", None), P("freq"))
    out_specs = P("freq", "row", "col")
    return jax.shard_map(local, mesh=mesh, in_specs=in_specs, out_specs=out_specs, check_vma=False)
```
